32 devices in a mesh: fsdp: 8 (over y, x, core), seq: 4 (over z).
Axes of the slice: x: 2, y: 2, z: 4, core: 2. Of those that a mesh axis runs over, the one named last changes fastest.
Arguments:
- source_copy: bfloat16 [8, 1024, 512], P('fsdp', 'seq'), may hold values from -6 to 6
- target_embed: bfloat16 [8, 1024, 512], P('fsdp', 'seq'), may hold values from -6 to 6
- glance_mask: int32 [8, 1024], P('fsdp', 'seq'), may hold values 0 or 1
- segment_ids: int32 [8, 1024], P('fsdp', 'seq'), may hold values from 0 to 6, as said below
- pad_mask: int32 [8, 1024], P('fsdp', 'seq'), may hold values from 0 to 1, as said below
- encoder_out: bfloat16 [8, 1024, 512], P('fsdp', 'seq'), may hold values from -6 to 6
- out_grad: bfloat16 [8, 1024, 512], P('fsdp', 'seq'), may hold values from -6 to 6
- self_query: bfloat16 [512, 512], P(('fsdp', 'seq')), may hold values from -0.25 to 0.25
- self_key: bfloat16 [512, 512], P(('fsdp', 'seq')), may hold values from -0.25 to 0.25
- self_value: bfloat16 [512, 512], P(('fsdp', 'seq')), may hold values from -0.25 to 0.25
- self_output: bfloat16 [512, 512], P(('fsdp', 'seq')), may hold values from -1 to 1
- norm1_gain: bfloat16 [512], P(('fsdp', 'seq')), may hold values from 0.5 to 1.5
- norm1_shift: bfloat16 [512], P(('fsdp', 'seq')), may hold values from -3 to 3
- cross_query: bfloat16 [512, 512], P(('fsdp', 'seq')), may hold values from -0.25 to 0.25
- cross_key: bfloat16 [512, 512], P(('fsdp', 'seq')), may hold values from -0.25 to 0.25
- cross_value: bfloat16 [512, 512], P(('fsdp', 'seq')), may hold values from -0.25 to 0.25
- cross_output: bfloat16 [512, 512], P(('fsdp', 'seq')), may hold values from -1 to 1
- norm2_gain: bfloat16 [512], P(('fsdp', 'seq')), may hold values from 0.5 to 1.5
- norm2_shift: bfloat16 [512], P(('fsdp', 'seq')), may hold values from -3 to 3
- inner_weight: bfloat16 [512, 2048], P(('fsdp', 'seq')), may hold values from -0.25 to 0.25
- outer_weight: bfloat16 [2048, 512], P(('fsdp', 'seq')), may hold values from -0.125 to 0.125
- norm3_gain: bfloat16 [512], P(('fsdp', 'seq')), may hold values from 0.5 to 1.5
- norm3_shift: bfloat16 [512], P(('fsdp', 'seq')), may hold values from -3 to 3
Outputs:
- layer_out: bfloat16 [8, 1024, 512], P('fsdp', 'seq')
- input_grad: float32 [8, 1024, 512], P('fsdp', 'seq')
- encoder_grad: float32 [8, 1024, 512], P('fsdp', 'seq')
- grad_self_query: float32 [512, 512], P(('fsdp', 'seq'))
- grad_self_key: float32 [512, 512], P(('fsdp', 'seq'))
- grad_self_value: float32 [512, 512], P(('fsdp', 'seq'))
- grad_self_output: float32 [512, 512], P(('fsdp', 'seq'))
- grad_norm1_gain: float32 [512], P(('fsdp', 'seq'))
- grad_norm1_shift: float32 [512], P(('fsdp', 'seq'))
- grad_cross_query: float32 [512, 512], P(('fsdp', 'seq'))
- grad_cross_key: float32 [512, 512], P(('fsdp', 'seq'))
- grad_cross_value: float32 [512, 512], P(('fsdp', 'seq'))
- grad_cross_output: float32 [512, 512], P(('fsdp', 'seq'))
- grad_norm2_gain: float32 [512], P(('fsdp', 'seq'))
- grad_norm2_shift: float32 [512], P(('fsdp', 'seq'))
- grad_inner_weight: float32 [512, 2048], P(('fsdp', 'seq'))
- grad_outer_weight: float32 [2048, 512], P(('fsdp', 'seq'))
- grad_norm3_gain: float32 [512], P(('fsdp', 'seq'))
- grad_norm3_shift: float32 [512], P(('fsdp', 'seq'))
The draws below stay inside these ranges and needn't reach their ends.
Inputs may be any that keep to these rules, and one draw needn't show every extreme that they name: `segment_ids`: within a row the numbers start at 0, rise by at most one from a position to the next and reach 6; in every row one document starts at or before position 128 and ends at or after position 896. `pad_mask`: in each row the zeros form a tail of the row, inside the row's last document, which holds a real position.
All inputs are finite; a program needn't handle non-finite values. No bound on the sum of `glance_mask` on one device may be relied on, other than what follows from the above.
Results may differ from the reference program's by a relative error of at most 0.025.
Values may be sent and summed in bfloat16 or wider, within the bound.
No kernel may reach another device: no remote copies, remote signals or barrier semaphores. Data moves between devices by JAX's collectives and lax.ppermute only.
A program may use at most 128 MiB of HBM per device.

```python
import jax
import jax.numpy as jnp
from jax import lax

D = 512
HEADS = 8
HEAD = 64
FF = 2048
ROW_LEN = 1024
ROWS = 8


extra_cuts = 4


def row_layout(key):
    first_key, last_key, tail_key, cut_key = jax.random.split(key, 4)
    place = jnp.arange(ROW_LEN, dtype=jnp.int32)[None, :]
    first = jax.random.randint(first_key, (ROWS, 1), extra_cuts + 1, ROW_LEN // 8 + 1)
    last = jax.random.randint(last_key, (ROWS, 1), 7 * ROW_LEN // 8 + 1, ROW_LEN - ROW_LEN // 32)
    tail = jax.random.randint(tail_key, (ROWS, 1), last + 1, ROW_LEN + 1)
    marks = ((place == first) | (place == last)).astype(jnp.int32)
    for stratum in range(extra_cuts):
        lower = 1 + stratum * (first - 1) // extra_cuts
        upper = 1 + (stratum + 1) * (first - 1) // extra_cuts
        cut_at = jax.random.randint(jax.random.fold_in(cut_key, stratum), (ROWS, 1), lower, upper)
        marks = marks + (place == cut_at).astype(jnp.int32)
    segments = jnp.cumsum(marks, axis=1).astype(jnp.int32)
    return (segments, tail)


def draw_segment_ids(key, part):
    segments, tail = row_layout(key)
    return segments


def draw_pad_mask(key, part):
    segments, tail = row_layout(key)
    place = jnp.arange(ROW_LEN, dtype=jnp.int32)[None, :]
    return (place < tail).astype(jnp.int32)


def place_ends(drawn, rng, least, largest):
    longest = drawn.shape.index(max(drawn.shape))
    spots = []
    for shift in (0, 1):
        where = [jax.random.randint(jax.random.fold_in(rng, axis), (), 0, length) for axis, length in enumerate(drawn.shape)]
        where[longest] = (where[longest] + shift) % drawn.shape[longest]
        spots.append(tuple(where))
    return drawn.at[spots[0]].set(least).at[spots[1]].set(largest)


def levels(stream_key, dims, cuts, least, high):
    loudness, own = 1.0, jax.random.fold_in(stream_key, 6)
    for position, blocks in cuts:
        draws = jnp.exp(jax.random.uniform(jax.random.fold_in(own, position), (blocks,), jnp.float32, least / len(cuts), high / len(cuts)))
        loudness = loudness * jnp.repeat(draws, dims[position] // blocks).reshape([-1 if axis == position else 1 for axis in range(len(dims))])
    return loudness


def scatter_about(own_key, extent, width, bound, pieces=(), kind=jnp.bfloat16):
    level = levels(own_key, extent, pieces, -0.22, 0.18) if pieces else 1.0
    drawn = jax.random.normal(own_key, extent, jnp.float32) * width * level
    return jnp.minimum(jnp.maximum(drawn, -bound), bound).astype(kind)


def setup_inputs(seed: int = 0) -> dict:
    key_of = jax.random.split(jax.random.key(seed), 24)
    source_copy = scatter_about(key_of[0], (ROWS, ROW_LEN, D), 1.0, 6.0, ((0, 8), (1, 4)))
    target_embed = scatter_about(key_of[1], (ROWS, ROW_LEN, D), 1.0, 6.0, ((0, 8), (1, 4)))
    glance_mask = place_ends((jax.random.randint(key_of[2], (ROWS, ROW_LEN), 0, 2) < 1).astype(jnp.int32), jax.random.fold_in(key_of[2], 1), 0, 1)
    segment_ids = draw_segment_ids(jax.random.fold_in(key_of[23], 71), 0)
    pad_mask = draw_pad_mask(jax.random.fold_in(key_of[23], 71), 0)
    encoder_out = scatter_about(key_of[5], (ROWS, ROW_LEN, D), 1.0, 6.0, ((0, 8), (1, 4)))
    out_grad = scatter_about(key_of[6], (ROWS, ROW_LEN, D), 1.0, 6.0, ((0, 8), (1, 4)))
    self_query = scatter_about(key_of[7], (D, D), D ** -0.5, 0.25, ((0, 32),))
    self_key = scatter_about(key_of[8], (D, D), D ** -0.5, 0.25, ((0, 32),))
    self_value = scatter_about(key_of[9], (D, D), D ** -0.5, 0.25, ((0, 32),))
    self_output = scatter_about(key_of[10], (D, D), (D // 16) ** -0.5, 1.0, ((0, 32),))
    norm1_gain = jnp.clip(1.0 + 0.1 * jax.random.normal(key_of[11], (D,), jnp.float32), 0.5, 1.5).astype(jnp.bfloat16)
    norm1_shift = scatter_about(key_of[12], (D,), 0.5, 3.0, ((0, 32),))
    cross_query = scatter_about(key_of[13], (D, D), D ** -0.5, 0.25, ((0, 32),))
    cross_key = scatter_about(key_of[14], (D, D), D ** -0.5, 0.25, ((0, 32),))
    cross_value = scatter_about(key_of[15], (D, D), D ** -0.5, 0.25, ((0, 32),))
    cross_output = scatter_about(key_of[16], (D, D), (D // 16) ** -0.5, 1.0, ((0, 32),))
    norm2_gain = jnp.clip(1.0 + 0.1 * jax.random.normal(key_of[17], (D,), jnp.float32), 0.5, 1.5).astype(jnp.bfloat16)
    norm2_shift = scatter_about(key_of[18], (D,), 0.5, 3.0, ((0, 32),))
    inner_weight = scatter_about(key_of[19], (D, FF), D ** -0.5, 0.25, ((0, 32),))
    outer_weight = scatter_about(key_of[20], (FF, D), FF ** -0.5, 0.125, ((0, 32),))
    norm3_gain = jnp.clip(1.0 + 0.1 * jax.random.normal(key_of[21], (D,), jnp.float32), 0.5, 1.5).astype(jnp.bfloat16)
    norm3_shift = scatter_about(key_of[22], (D,), 0.5, 3.0, ((0, 32),))
    return {"source_copy": source_copy, "target_embed": target_embed, "glance_mask": glance_mask, "segment_ids": segment_ids, "pad_mask": pad_mask, "encoder_out": encoder_out, "out_grad": out_grad, "self_query": self_query, "self_key": self_key, "self_value": self_value, "self_output": self_output, "norm1_gain": norm1_gain, "norm1_shift": norm1_shift, "cross_query": cross_query, "cross_key": cross_key, "cross_value": cross_value, "cross_output": cross_output, "norm2_gain": norm2_gain, "norm2_shift": norm2_shift, "inner_weight": inner_weight, "outer_weight": outer_weight, "norm3_gain": norm3_gain, "norm3_shift": norm3_shift}


@jax.custom_vjp
def low(v):
    return lax.optimization_barrier(v.astype(jnp.bfloat16)).astype(jnp.float32)

@jax.custom_vjp
def low_back(v):
    return v

def low_keep(v):
    return (low(v), None)

def low_pass(kept, grad):
    return (grad,)

def back_keep(v):
    return (v, None)

def back_low(kept, grad):
    return (low(grad),)
low.defvjp(low_keep, low_pass)
low_back.defvjp(back_keep, back_low)
norm_eps = 1e-05
mask_fill = -1e+30

def product(left, right):
    return jnp.dot(left, right, precision=lax.Precision.HIGHEST)

def gelu_tanh(values):
    return jax.nn.gelu(values, approximate=True)

def norm_apply(hidden, gain, shift):
    centre = lax.optimization_barrier(jnp.mean(hidden, axis=-1, keepdims=True))
    centered = hidden - centre
    spread = lax.optimization_barrier(jnp.mean(centered * centered, axis=-1, keepdims=True))
    return centered * lax.rsqrt(spread + norm_eps) * gain + shift

def attention(query_rows, key_rows, value_rows, allowed):
    length = query_rows.shape[0]
    heads_query = query_rows.reshape(length, HEADS, HEAD)
    heads_key = key_rows.reshape(key_rows.shape[0], HEADS, HEAD)
    heads_value = value_rows.reshape(value_rows.shape[0], HEADS, HEAD)
    scores = jnp.einsum('qhd,khd->hqk', heads_query, heads_key, precision=lax.Precision.HIGHEST) * HEAD ** (-0.5)
    scores = jnp.where(allowed[None], low_back(scores), mask_fill)
    score_max = lax.optimization_barrier(jnp.max(scores, axis=2, keepdims=True))
    exp_scores = jnp.exp(scores - score_max)
    probability = exp_scores / lax.optimization_barrier(jnp.sum(exp_scores, axis=2, keepdims=True))
    mixed_heads = jnp.einsum('hqk,khd->qhd', low(probability), heads_value, precision=lax.Precision.HIGHEST)
    return low_back(low(mixed_heads.reshape(length, HEADS * HEAD)))

def row_layer(params, mixed_row, encoder_row, segment_row, pad_row):
    self_query, self_key, self_value, self_output, norm1_gain, norm1_shift, cross_query, cross_key, cross_value, cross_output, norm2_gain, norm2_shift, inner_weight, outer_weight, norm3_gain, norm3_shift = params
    key_ids = jnp.where(pad_row == 1, segment_row, -1)
    allowed = segment_row[:, None] == key_ids[None, :]
    query_self = low_back(low(product(mixed_row, self_query)))
    key_self = low_back(low(product(mixed_row, self_key)))
    value_self = low_back(low(product(mixed_row, self_value)))
    attn_self = attention(query_self, key_self, value_self, allowed)
    normed_one = norm_apply(mixed_row + low_back(product(attn_self, self_output)), norm1_gain, norm1_shift)
    query_cross = low_back(low(product(low(normed_one), cross_query)))
    key_cross = low_back(low(product(encoder_row, cross_key)))
    value_cross = low_back(low(product(encoder_row, cross_value)))
    attn_cross = attention(query_cross, key_cross, value_cross, allowed)
    normed_two = norm_apply(normed_one + low_back(product(attn_cross, cross_output)), norm2_gain, norm2_shift)
    inner_act = low_back(product(low(normed_two), inner_weight))
    active = low(gelu_tanh(inner_act))
    normed_three = norm_apply(normed_two + low_back(product(active, outer_weight)), norm3_gain, norm3_shift)
    return normed_three * pad_row[:, None].astype(jnp.float32)

def reference(source_copy, target_embed, glance_mask, segment_ids, pad_mask, encoder_out, out_grad, self_query, self_key, self_value, self_output, norm1_gain, norm1_shift, cross_query, cross_key, cross_value, cross_output, norm2_gain, norm2_shift, inner_weight, outer_weight, norm3_gain, norm3_shift):
    mixed_input = jnp.where(glance_mask[..., None] == 1, target_embed, source_copy).astype(jnp.float32)
    encoder = encoder_out.astype(jnp.float32)
    params = tuple((weight.astype(jnp.float32) for weight in (self_query, self_key, self_value, self_output, norm1_gain, norm1_shift, cross_query, cross_key, cross_value, cross_output, norm2_gain, norm2_shift, inner_weight, outer_weight, norm3_gain, norm3_shift)))
    checked_row = jax.checkpoint(row_layer)

    def whole(params, mixed_input, encoder):

        def step(carry, row_parts):
            return (carry, checked_row(params, row_parts[0], row_parts[1], row_parts[2], row_parts[3]))
        _, outputs = lax.scan(step, jnp.zeros((), jnp.int32), (mixed_input, encoder, segment_ids, pad_mask))
        return outputs
    layer_out, pullback = jax.vjp(whole, params, mixed_input, encoder)
    grad_params, input_grad, encoder_grad = pullback(out_grad.astype(jnp.float32))
    grad_self_query, grad_self_key, grad_self_value, grad_self_output, grad_norm1_gain, grad_norm1_shift, grad_cross_query, grad_cross_key, grad_cross_value, grad_cross_output, grad_norm2_gain, grad_norm2_shift, grad_inner_weight, grad_outer_weight, grad_norm3_gain, grad_norm3_shift = grad_params
    return (layer_out.astype(jnp.bfloat16), input_grad, encoder_grad, grad_self_query, grad_self_key, grad_self_value, grad_self_output, grad_norm1_gain, grad_norm1_shift, grad_cross_query, grad_cross_key, grad_cross_value, grad_cross_output, grad_norm2_gain, grad_norm2_shift, grad_inner_weight, grad_outer_weight, grad_norm3_gain, grad_norm3_shift)
```

```python
import jax
import jax.numpy as jnp
from jax import lax
from jax.sharding import PartitionSpec as P

HEADS = 8
HEAD = 64


norm_eps = 1e-05
mask_fill = -1e30


def matmul(left, right):
    return jnp.dot(left, right, preferred_element_type=jnp.float32)


def left_contract(left, right):
    return lax.dot_general(
        left, right, (((0,), (0,)), ((), ())), preferred_element_type=jnp.float32
    )


def right_contract(left, right):
    return lax.dot_general(
        left, right, (((1,), (1,)), ((), ())), preferred_element_type=jnp.float32
    )


def gelu_tanh(values):
    return jax.nn.gelu(values, approximate=True)


def norm_apply(hidden, gain, shift):
    centre = jnp.mean(hidden, axis=-1, keepdims=True)
    centered = hidden - centre
    spread = jnp.mean(centered * centered, axis=-1, keepdims=True)
    return centered * lax.rsqrt(spread + norm_eps) * gain + shift


def masked_scores(query_rows, key_rows, allowed, head_cols):
    scores = right_contract(query_rows[:, head_cols], key_rows[:, head_cols]) * HEAD ** (-0.5)
    return jnp.where(allowed, scores, mask_fill)


def attend_row(query_rows, key_rows, value_rows, query_ids, key_ids):
    allowed = query_ids[:, None] == key_ids[None, :]
    outputs = []
    log_sums = []
    for head_index in range(HEADS):
        head_cols = slice(head_index * HEAD, (head_index + 1) * HEAD)
        scores = masked_scores(query_rows, key_rows, allowed, head_cols)
        score_max = jnp.max(scores, axis=1, keepdims=True)
        exp_scores = jnp.exp(scores - score_max)
        score_total = jnp.sum(exp_scores, axis=1, keepdims=True)
        probability = (exp_scores / score_total).astype(jnp.bfloat16)
        outputs.append(matmul(probability, value_rows[:, head_cols]))
        log_sums.append(score_max[:, 0] + jnp.log(score_total[:, 0]))
    return (jnp.concatenate(outputs, axis=1).astype(jnp.bfloat16), jnp.stack(log_sums))


def attend_row_back(query_rows, key_rows, value_rows, query_ids, key_ids, log_sums, grad_rows):
    allowed = query_ids[:, None] == key_ids[None, :]
    grad_query = []
    grad_key = []
    grad_value = []
    for head_index in range(HEADS):
        head_cols = slice(head_index * HEAD, (head_index + 1) * HEAD)
        scores = masked_scores(query_rows, key_rows, allowed, head_cols)
        probability = jnp.exp(scores - log_sums[head_index][:, None])
        grad_prob = right_contract(grad_rows[:, head_cols], value_rows[:, head_cols])
        row_dot = jnp.sum(probability * grad_prob, axis=1, keepdims=True)
        grad_scores = (probability * (grad_prob - row_dot)).astype(jnp.bfloat16)
        grad_query.append(matmul(grad_scores, key_rows[:, head_cols]) * HEAD ** (-0.5))
        grad_key.append(left_contract(grad_scores, query_rows[:, head_cols]) * HEAD ** (-0.5))
        grad_value.append(left_contract(probability.astype(jnp.bfloat16), grad_rows[:, head_cols]))
    return (
        jnp.concatenate(grad_query, axis=1).astype(jnp.bfloat16),
        jnp.concatenate(grad_key, axis=1).astype(jnp.bfloat16),
        jnp.concatenate(grad_value, axis=1).astype(jnp.bfloat16),
    )


def swap(block, axis_name, size, bit):
    return lax.ppermute(block, axis_name, [(i, i ^ bit) for i in range(size)])


def bit_of(axis_name, bit):
    return (lax.axis_index(axis_name) & bit) != 0


def join(block, axis_name, size, bit, place):
    other = swap(block, axis_name, size, bit)
    high = bit_of(axis_name, bit)
    return jnp.where(
        high, jnp.stack([other, block], axis=place), jnp.stack([block, other], axis=place)
    )


def bits_below(size):
    return [1 << k for k in range(size.bit_length() - 1)]


def gather_blocks(shard, fsdp, seq, turned):
    block = shard
    for bit in bits_below(seq):
        block = join(block, "seq", seq, bit, 1)
    upper = bits_below(fsdp)[1:]
    done = []
    for bit in upper[::-1] if turned else upper:
        place = 1 + sum(b > bit for b in done)
        block = join(block, "fsdp", fsdp, bit, place)
        done.append(bit)
    if fsdp > 1:
        block = join(block, "fsdp", fsdp, 1, 1 + len(upper))
    return block.reshape(shard.shape[0], fsdp * seq * shard.shape[1], shard.shape[2])


def halve(block, axis_name, size, bit, place):
    high = bit_of(axis_name, bit).astype(jnp.int32)
    away = lax.dynamic_index_in_dim(block, 1 - high, place, keepdims=False)
    kept = lax.dynamic_index_in_dim(block, high, place, keepdims=False)
    other = swap(away, axis_name, size, bit)
    return (kept.astype(jnp.float32) + other.astype(jnp.float32)).astype(jnp.bfloat16)


def scatter_blocks(whole, fsdp, seq, turned):
    w, depth, cols = whole.shape
    n_up = len(bits_below(fsdp)) - 1
    n_seq = len(bits_below(seq))
    rows = depth // (fsdp * seq)
    block = whole.reshape((w,) + (2,) * (n_up + 1 + n_seq) + (rows, cols))
    block = halve(block, "fsdp", fsdp, 1, 1 + n_up)
    upper = bits_below(fsdp)[1:]
    left = list(upper)
    for bit in upper[::-1] if turned else upper:
        place = 1 + sum(b > bit for b in left)
        block = halve(block, "fsdp", fsdp, bit, place)
        left.remove(bit)
    for bit in bits_below(seq)[::-1]:
        block = halve(block, "seq", seq, bit, 1)
    return block.astype(jnp.float32)


def make(fsdp, seq):
    def on_device(
        source_copy,
        target_embed,
        glance_mask,
        segment_ids,
        pad_mask,
        encoder_out,
        out_grad,
        self_query,
        self_key,
        self_value,
        self_output,
        norm1_gain,
        norm1_shift,
        cross_query,
        cross_key,
        cross_value,
        cross_output,
        norm2_gain,
        norm2_shift,
        inner_weight,
        outer_weight,
        norm3_gain,
        norm3_shift,
    ):
        row_count, loc_count, feat_count = source_copy.shape
        token_count = row_count * loc_count
        ff_rows = outer_weight.shape[0]
        chunk = self_query.shape[0]
        mixed_input = jnp.where(glance_mask[..., None] == 1, target_embed, source_copy).reshape(
            token_count, feat_count
        )
        encoder = encoder_out.reshape(token_count, feat_count)
        key_local = jnp.where(pad_mask == 1, segment_ids, -1)
        real_rows = pad_mask.reshape(token_count, 1).astype(jnp.float32)
        mixed_all = lax.all_gather(mixed_input, "seq", axis=0, tiled=True)
        key_ids = lax.all_gather(key_local[0], "seq", axis=0, tiled=True)
        query_ids = segment_ids[0]

        self_a = gather_blocks(jnp.stack([self_query, self_key]), fsdp, seq, False)
        self_b = gather_blocks(jnp.stack([self_value, self_output]), fsdp, seq, True)
        encoder_all = lax.all_gather(encoder, "seq", axis=0, tiled=True)
        vectors = jnp.stack(
            [norm1_gain, norm1_shift, norm2_gain, norm2_shift, norm3_gain, norm3_shift], axis=1
        )
        vectors = jnp.pad(vectors, ((0, 0), (0, 128 - 6)))
        cross_a = gather_blocks(
            jnp.concatenate(
                [
                    jnp.stack([cross_query, cross_key]),
                    jnp.stack([vectors, jnp.zeros_like(vectors)]),
                ],
                axis=2,
            ),
            fsdp,
            seq,
            False,
        )
        cross_b = gather_blocks(jnp.stack([cross_value, cross_output]), fsdp, seq, True)
        ff_in = gather_blocks(inner_weight[None], fsdp, seq, False)[0]
        ff_out = gather_blocks(outer_weight[None], fsdp, seq, True)[0]
        w_q1, w_k1 = self_a[0], self_a[1]
        w_v1, w_o1 = self_b[0], self_b[1]
        w_q2, w_k2 = cross_a[0, :, :feat_count], cross_a[1, :, :feat_count]
        w_v2, w_o2 = cross_b[0], cross_b[1]
        flat_vectors = cross_a[0, :, feat_count : feat_count + 6].astype(jnp.float32).T
        gain_one, shift_one, gain_two, shift_two, gain_three, shift_three = [
            flat_vectors[i] for i in range(6)
        ]

        query_self = matmul(mixed_input, w_q1).astype(jnp.bfloat16)
        key_self = matmul(mixed_all, w_k1).astype(jnp.bfloat16)
        value_self = matmul(mixed_all, w_v1).astype(jnp.bfloat16)
        attn_self, sums_self = attend_row(query_self, key_self, value_self, query_ids, key_ids)
        flow_one = mixed_input.astype(jnp.float32) + matmul(attn_self, w_o1)
        normed_one = norm_apply(flow_one, gain_one, shift_one)
        normed_one_low = normed_one.astype(jnp.bfloat16)
        query_cross = matmul(normed_one_low, w_q2).astype(jnp.bfloat16)
        key_cross = matmul(encoder_all, w_k2).astype(jnp.bfloat16)
        value_cross = matmul(encoder_all, w_v2).astype(jnp.bfloat16)
        attn_cross, sums_cross = attend_row(query_cross, key_cross, value_cross, query_ids, key_ids)
        flow_two = normed_one + matmul(attn_cross, w_o2)
        normed_two = norm_apply(flow_two, gain_two, shift_two)
        normed_two_low = normed_two.astype(jnp.bfloat16)
        inner_act = matmul(normed_two_low, ff_in)
        active = gelu_tanh(inner_act).astype(jnp.bfloat16)
        flow_three = normed_two + matmul(active, ff_out)
        normed_three = norm_apply(flow_three, gain_three, shift_three)
        layer_out = (normed_three * real_rows).astype(jnp.bfloat16)

        grad_top = out_grad.reshape(token_count, feat_count).astype(jnp.float32) * real_rows
        _, norm_three_back = jax.vjp(norm_apply, flow_three, gain_three, shift_three)
        grad_flow_three, grad_gain_three, grad_shift_three = norm_three_back(grad_top)
        grad_y_three = grad_flow_three.astype(jnp.bfloat16)
        grad_outer = left_contract(active, grad_y_three).astype(jnp.bfloat16)
        grad_active = right_contract(grad_y_three, ff_out)
        _, gelu_back = jax.vjp(gelu_tanh, inner_act)
        grad_inner_act = gelu_back(grad_active)[0].astype(jnp.bfloat16)
        grad_inner = left_contract(normed_two_low, grad_inner_act).astype(jnp.bfloat16)
        out_inner = scatter_blocks(grad_inner[None], fsdp, seq, False)[0]
        out_outer = scatter_blocks(grad_outer[None], fsdp, seq, True)[0]
        grad_normed_two = grad_flow_three + right_contract(grad_inner_act, ff_in)
        _, norm_two_back = jax.vjp(norm_apply, flow_two, gain_two, shift_two)
        grad_flow_two, grad_gain_two, grad_shift_two = norm_two_back(grad_normed_two)
        grad_y_two = grad_flow_two.astype(jnp.bfloat16)
        grad_cross_out = left_contract(attn_cross, grad_y_two).astype(jnp.bfloat16)
        grad_attn_cross = right_contract(grad_y_two, w_o2).astype(jnp.bfloat16)
        grad_query_cross, grad_key_cross, grad_value_cross = attend_row_back(
            query_cross, key_cross, value_cross, query_ids, key_ids, sums_cross, grad_attn_cross
        )
        grad_cross_q = left_contract(normed_one_low, grad_query_cross).astype(jnp.bfloat16)
        grad_cross_k = left_contract(encoder_all, grad_key_cross).astype(jnp.bfloat16)
        grad_cross_v = left_contract(encoder_all, grad_value_cross).astype(jnp.bfloat16)
        encoder_part = right_contract(grad_key_cross, w_k2) + right_contract(
            grad_value_cross, w_v2
        )
        encoder_grad = lax.psum_scatter(
            encoder_part.astype(jnp.bfloat16), "seq", scatter_dimension=0, tiled=True
        ).astype(jnp.float32)
        out_cross_a = scatter_blocks(jnp.stack([grad_cross_q, grad_cross_k]), fsdp, seq, False)
        out_cross_b = scatter_blocks(jnp.stack([grad_cross_v, grad_cross_out]), fsdp, seq, True)
        grad_normed_one = grad_flow_two + right_contract(grad_query_cross, w_q2)
        _, norm_one_back = jax.vjp(norm_apply, flow_one, gain_one, shift_one)
        grad_flow_one, grad_gain_one, grad_shift_one = norm_one_back(grad_normed_one)
        grad_y_one = grad_flow_one.astype(jnp.bfloat16)
        grad_self_out = left_contract(attn_self, grad_y_one).astype(jnp.bfloat16)
        grad_attn_self = right_contract(grad_y_one, w_o1).astype(jnp.bfloat16)
        grad_query_self, grad_key_self, grad_value_self = attend_row_back(
            query_self, key_self, value_self, query_ids, key_ids, sums_self, grad_attn_self
        )
        grad_self_q = left_contract(mixed_input, grad_query_self).astype(jnp.bfloat16)
        grad_self_k = left_contract(mixed_all, grad_key_self).astype(jnp.bfloat16)
        grad_self_v = left_contract(mixed_all, grad_value_self).astype(jnp.bfloat16)
        input_part = right_contract(grad_key_self, w_k1) + right_contract(grad_value_self, w_v1)
        input_grad = (
            lax.psum_scatter(
                input_part.astype(jnp.bfloat16), "seq", scatter_dimension=0, tiled=True
            ).astype(jnp.float32)
            + grad_flow_one
            + right_contract(grad_query_self, w_q1)
        )
        grad_vectors = jnp.stack(
            [
                grad_gain_one,
                grad_shift_one,
                grad_gain_two,
                grad_shift_two,
                grad_gain_three,
                grad_shift_three,
            ]
        ).astype(jnp.bfloat16)
        grad_vectors = jnp.pad(grad_vectors, ((0, 128 - 6), (0, 0))).T
        out_self_a = scatter_blocks(
            jnp.concatenate(
                [
                    jnp.stack([grad_self_q, grad_self_k]),
                    jnp.stack([grad_vectors, jnp.zeros_like(grad_vectors)]),
                ],
                axis=2,
            ),
            fsdp,
            seq,
            False,
        )
        out_self_b = scatter_blocks(jnp.stack([grad_self_v, grad_self_out]), fsdp, seq, True)
        out_vectors = out_self_a[0, :, feat_count : feat_count + 6].T

        def stacked(flat_rows):
            return flat_rows.reshape(row_count, loc_count, feat_count)

        return (
            stacked(layer_out),
            stacked(input_grad),
            stacked(encoder_grad),
            out_self_a[0, :, :feat_count],
            out_self_a[1, :, :feat_count],
            out_self_b[0],
            out_self_b[1],
            out_vectors[0],
            out_vectors[1],
            out_cross_a[0],
            out_cross_a[1],
            out_cross_b[0],
            out_cross_b[1],
            out_vectors[2],
            out_vectors[3],
            out_inner,
            out_outer,
            out_vectors[4],
            out_vectors[5],
        )

    return on_device


def solution(mesh):
    rows = P("fsdp", "seq", None)
    marks = P("fsdp", "seq")
    weight = P(("fsdp", "seq"), None)
    vector = P(("fsdp", "seq"))
    layer = (weight,) * 4 + (vector,) * 2
    return jax.shard_map(
        make(mesh.shape["fsdp"], mesh.shape["seq"]),
        mesh=mesh,
        in_specs=(rows, rows, marks, marks, marks, rows, rows)
        + layer
        + layer
        + (weight,) * 2
        + (vector,) * 2,
        out_specs=(rows,) * 3 + layer + layer + (weight,) * 2 + (vector,) * 2,
        check_vma=False,
    )
```

```python
import functools

import jax
import jax.numpy as jnp
from jax import lax
from jax.experimental import pallas as pl
from jax.experimental.pallas import tpu as pltpu
from jax.sharding import PartitionSpec as P

HEADS = 8
HEAD = 64
PAIR = 2 * HEAD
SLOT = HEAD + 16


norm_eps = 1e-05
mask_fill = -1e30

BF = jnp.bfloat16
F32 = jnp.float32
VM = pltpu.VMEM
WHOLE = pl.BlockSpec(memory_space=pltpu.VMEM)
SCALARS = pl.BlockSpec(memory_space=pltpu.SMEM)
APART = pl.BlockSpec(memory_space=pl.ANY)


def shape(*dims, dtype=BF):
    return jax.ShapeDtypeStruct(dims, dtype)


def low(values):
    return values.astype(BF)


def dot(left, right):
    return jnp.dot(left, right, preferred_element_type=F32)


def dot_t(left, right):
    return lax.dot_general(left, right, (((1,), (1,)), ((), ())), preferred_element_type=F32)


def head_cols(block, head):
    pair = block[:, head // 2 * PAIR : (head // 2 + 1) * PAIR]
    lane = lax.broadcasted_iota(jnp.int32, pair.shape, 1)
    return jnp.where((lane >= HEAD) == (head % 2 == 1), pair, jnp.zeros_like(pair))


def head_rows(block, head):
    mine = block[head * HEAD : (head + 1) * HEAD, :]
    rest = jnp.zeros_like(mine)
    return jnp.concatenate([mine, rest] if head % 2 == 0 else [rest, mine], axis=0)


def chunk_of(pos, seq, c, e, d):
    return (pos[0] ^ (2 * e + c)) * seq + (pos[1] ^ d)


def in_order(pos, parts, target, col, sub=1):
    width = target.shape[1]
    for c, sides in enumerate(parts):
        if len(sides) == 1:
            sides = [sides[0].at[e] for e in range(sides[0].shape[0])]
        for e, part in enumerate(sides):
            for d in range(part.shape[0]):
                rows = part.shape[1]
                first = chunk_of(pos, part.shape[0], c, e, d) * (rows * sub)
                for r in range(sub):
                    start = pl.multiple_of(first + r * rows, rows)
                    target[pl.ds(start, rows), :] = part[
                        d, :, col + r * width : col + (r + 1) * width
                    ]


def by_distance(pos, source, parts, col, sub=1):
    width = source.shape[1]
    for c, part in enumerate(parts):
        for e in range(part.shape[0]):
            for d in range(part.shape[1]):
                rows = part.shape[2]
                first = chunk_of(pos, part.shape[1], c, e, d) * (rows * sub)
                for r in range(sub):
                    start = pl.multiple_of(first + r * rows, rows)
                    part[e, d, :, col + r * width : col + (r + 1) * width] = source[
                        pl.ds(start, rows), :
                    ]


def normalise(flow):
    centre = jnp.mean(flow, axis=1, keepdims=True)
    centered = flow - centre
    spread = jnp.mean(centered * centered, axis=1, keepdims=True)
    inverse = lax.rsqrt(spread + norm_eps)
    return centered * inverse, inverse


def normalise_back(grad, unit, inverse, gain):
    scaled = grad * gain
    mean_one = jnp.mean(scaled, axis=1, keepdims=True)
    mean_two = jnp.mean(scaled * unit, axis=1, keepdims=True)
    grad_flow = inverse * (scaled - mean_one - unit * mean_two)
    return (
        grad_flow,
        jnp.sum(grad * unit, axis=0, keepdims=True),
        jnp.sum(grad, axis=0, keepdims=True),
    )


def set_bias(key_rows, query_row, bias):
    count = query_row.shape[1]
    for d in range(len(key_rows)):
        column = jnp.broadcast_to(key_rows[d], (128, count)).T
        column = jnp.concatenate([column] * (count // 128), axis=1)
        bias[d * count : (d + 1) * count, :] = jnp.where(column == query_row, 0.0, mask_fill)


def set_values(values, slots, first):
    turned = values.T
    count = values.shape[0]
    cols = slice(first, first + count)
    for head in range(HEADS):
        slots[head * SLOT : head * SLOT + HEAD, cols] = turned[head * HEAD : (head + 1) * HEAD, :]
        slots[head * SLOT + HEAD : (head + 1) * SLOT, cols] = jnp.ones((SLOT - HEAD, count), BF)


def attend(query, keys, slots, bias, exps, exps_out, sem, mixed_out, inverse_out):
    count = query.shape[0]
    for head in range(HEADS):
        pair_keys = keys[:, head // 2 * PAIR : (head // 2 + 1) * PAIR]
        scores = dot_t(pair_keys, head_cols(query, head)) + bias[...]
        top = jnp.max(scores, axis=0, keepdims=True)
        exp_scores = low(jnp.exp(scores - top))
        place = slice(head % 2 * count, (head % 2 + 1) * count)
        exps[head // 2, :, place] = exp_scores
        if head % 2 == 1:
            pltpu.make_async_copy(
                exps.at[head // 2], exps_out.at[head // 2], sem.at[head // 2]
            ).start()
        summed = dot(slots[head * SLOT : (head + 1) * SLOT, :], exp_scores)
        inverse = 1.0 / summed[HEAD : HEAD + 1, :]
        mixed_out[head * HEAD : (head + 1) * HEAD, :] = low(summed[:HEAD, :] * inverse)
        inverse_out[head : head + 1, :] = inverse
    for pair in range(HEADS // 2):
        pltpu.make_async_copy(exps.at[pair], exps_out.at[pair], sem.at[pair]).wait()


def fetch(exps_in, exps, sem, pair):
    return pltpu.make_async_copy(exps_in.at[pair], exps.at[pair], sem.at[pair])


def attend_back(
    query, keys_t, values, mixed_t, grad_t, grad, exps_in, exps, sem, grad_exps, query_t_out, kv_out
):
    count = query.shape[0]
    feat = query.shape[1]
    for pair in range(HEADS // 2):
        fetch(exps_in, exps, sem, pair).wait()
        cols = slice(pair * PAIR, (pair + 1) * PAIR)
        for head in (2 * pair, 2 * pair + 1):
            rows = slice(head * HEAD, (head + 1) * HEAD)
            place = slice(head % 2 * count, (head % 2 + 1) * count)
            row_dot = jnp.sum(
                grad_t[rows, :].astype(F32) * mixed_t[rows, :].astype(F32), axis=0, keepdims=True
            )
            grad_prob = dot(values[:, cols], head_rows(grad_t, head))
            grad_scores = low(exps[pair, :, place].astype(F32) * (grad_prob - row_dot))
            grad_exps[:, place] = grad_scores
            query_t_out[rows, :] = low(dot(keys_t[rows, :], grad_scores) * HEAD ** (-0.5))
        both = jnp.concatenate([head_cols(query, 2 * pair), head_cols(query, 2 * pair + 1)], axis=0)
        kv_out[:, cols] = low(dot(grad_exps[...], both))
        both = jnp.concatenate([head_cols(grad, 2 * pair), head_cols(grad, 2 * pair + 1)], axis=0)
        kv_out[:, feat + pair * PAIR : feat + (pair + 1) * PAIR] = low(dot(exps[pair], both))


def over_sums(grad_t, inverse):
    return low(
        jnp.concatenate(
            [
                grad_t[head * HEAD : (head + 1) * HEAD, :] * inverse[head : head + 1, :]
                for head in range(HEADS)
            ],
            axis=0,
        )
    )


def self_attend_body(n_blocks, n_parts, pos, *refs):
    blocks, refs = refs[:n_blocks], refs[n_blocks:]
    near, far, refs = refs[:n_parts], refs[n_parts : 2 * n_parts], refs[2 * n_parts :]
    (ids, q_out, v_out, kt_out, mixed_out, inverse_out, kid_out, exps_out) = refs[:8]
    weight, keys, slots, bias, exps, sem = refs[8:]
    count, feat = q_out.shape
    in_order(pos, (near, far), weight, 0)
    query = low(dot(blocks[0][:count, :], weight[:, :feat]))
    query = query * BF(HEAD ** (-0.5))
    q_out[...] = query
    for d, block in enumerate(blocks):
        rows = slice(d * count, (d + 1) * count)
        key = low(dot(block[:count, :], weight[:, feat : 2 * feat]))
        value = low(dot(block[:count, :], weight[:, 2 * feat :]))
        keys[rows, :] = key
        kt_out[:, rows] = key.T
        v_out[rows, :] = value
        set_values(value, slots, d * count)
        kid_out[d : d + 1, :] = block[count : count + 1, :count].astype(F32)
    set_bias([kid_out[d : d + 1, :] for d in range(n_blocks)], ids[...].astype(F32), bias)
    attend(query, keys, slots, bias, exps, exps_out, sem, mixed_out, inverse_out)


def attend_scratch(keys, feat, count):
    return [
        VM((keys, feat), BF),
        VM((HEADS * SLOT, keys), BF),
        VM((keys, count), F32),
        VM((HEADS // 2, keys, 2 * count), BF),
        pltpu.SemaphoreType.DMA((HEADS // 2,)),
    ]


SMALL = ("stack", "join", "add_far", "add_mid", "add_near", "add_one", "add_line")
ROOM = {"self_attend": 22, "cross_attend": 24, "feed": 28, "cross_back": 28, "self_back": 22}


def kernel_call(
    body, outs, out_specs, in_specs, scratch, name, flops, size, after=(), held_in=(), held_out=()
):
    n_in = len(in_specs)
    small = name in SMALL

    def space(place, held):
        return pltpu.VMEM if small or place in held else pltpu.HBM

    def run(*refs):
        body(*refs[:n_in], *refs[n_in + len(after) :])

    single = not isinstance(outs, (tuple, list))
    outs = tuple(
        space(place, held_out)(out.shape, out.dtype)
        for place, out in enumerate([outs] if single else outs)
    )
    outs = outs[0] if single else outs
    call = pl.pallas_call(
        run if after else body,
        out_shape=outs,
        in_specs=in_specs + [APART] * len(after),
        out_specs=out_specs,
        scratch_shapes=scratch,
        compiler_params=pltpu.CompilerParams(vmem_limit_bytes=(4 if small else ROOM.get(name, 12)) * 2**20),
        cost_estimate=pl.CostEstimate(flops=flops, bytes_accessed=size, transcendentals=0),
        name=name,
    )

    def go(*operands):
        operands = [
            x
            if spec is SCALARS
            else pltpu.with_memory_space_constraint(x, space(place, held_in))
            for place, (x, spec) in enumerate(zip(operands, in_specs, strict=True))
        ]
        return call(*operands, *after)

    return go


def self_attend(pos, blocks, ids, near, far, count, feat, after):
    keys = count * len(blocks)
    return kernel_call(
        functools.partial(self_attend_body, len(blocks), len(near)),
        (
            shape(count, feat),
            shape(keys, feat),
            shape(feat, keys),
            shape(feat, count),
            shape(HEADS, count, dtype=F32),
            shape(len(blocks), count, dtype=F32),
            shape(HEADS // 2, keys, 2 * count),
        ),
        [WHOLE] * 6 + [APART],
        [SCALARS] + [WHOLE] * (len(blocks) + 2 * len(near) + 1),
        [VM((feat, 3 * feat), BF)] + attend_scratch(keys, feat, count),
        "self_attend",
        12 * 10**9,
        20 * 10**6,
        after,
    )(pos, *blocks, *near, *far, ids)


def cross_attend_body(n_blocks, n_parts, pos, *refs):
    blocks, refs = refs[:n_blocks], refs[n_blocks:]
    near, far, refs = refs[:n_parts], refs[n_parts : 2 * n_parts], refs[2 * n_parts :]
    (ids, kid, mixed, mixed_one) = refs[:4]
    (vec_out, unit_out, inv_out, q_out, v_out, kt_out, mixed_out, inverse_out) = refs[4:12]
    (unit_two_out, inv_two_out, exps_out) = refs[12:15]
    weight, keys, slots, bias, exps, sem = refs[15:]
    count, feat = q_out.shape
    in_order(pos, (near, far), weight, 0)
    vec_out[...] = weight[:, 5 * feat :].astype(F32).T[:8, :]
    flow = mixed[:count, :].astype(F32) + dot(mixed_one[...].T, weight[:, :feat])
    unit, inverse = normalise(flow)
    unit_out[...] = unit
    inv_out[...] = jnp.broadcast_to(inverse, inv_out.shape)
    normed = unit * vec_out[0:1, :] + vec_out[1:2, :]
    query = low(dot(low(normed), weight[:, feat : 2 * feat])) * BF(HEAD ** (-0.5))
    q_out[...] = query
    for d, block in enumerate(blocks):
        rows = slice(d * count, (d + 1) * count)
        key = low(dot(block[...], weight[:, 2 * feat : 3 * feat]))
        value = low(dot(block[...], weight[:, 3 * feat : 4 * feat]))
        keys[rows, :] = key
        kt_out[:, rows] = key.T
        v_out[rows, :] = value
        set_values(value, slots, d * count)
    set_bias([kid[d : d + 1, :] for d in range(n_blocks)], ids[...].astype(F32), bias)
    attend(query, keys, slots, bias, exps, exps_out, sem, mixed_out, inverse_out)
    flow = unit_out[...] * vec_out[0:1, :] + vec_out[1:2, :]
    flow = flow + dot(mixed_out[...].T, weight[:, 4 * feat : 5 * feat])
    unit, inverse = normalise(flow)
    unit_two_out[...] = unit
    inv_two_out[...] = jnp.broadcast_to(inverse, inv_two_out.shape)


def cross_attend(pos, blocks, ids, kid, mixed, mixed_one, near, far, after):
    count, feat = blocks[0].shape
    keys = count * len(blocks)
    return kernel_call(
        functools.partial(cross_attend_body, len(blocks), len(near)),
        (
            shape(8, feat, dtype=F32),
            shape(count, feat, dtype=F32),
            shape(count, 128, dtype=F32),
            shape(count, feat),
            shape(keys, feat),
            shape(feat, keys),
            shape(feat, count),
            shape(HEADS, count, dtype=F32),
            shape(count, feat, dtype=F32),
            shape(count, 128, dtype=F32),
            shape(HEADS // 2, keys, 2 * count),
        ),
        [WHOLE] * 10 + [APART],
        [SCALARS] + [WHOLE] * (len(blocks) + 2 * len(near) + 4),
        [VM((feat, 5 * feat + 128), BF)] + attend_scratch(keys, feat, count),
        "cross_attend",
        14 * 10**9,
        20 * 10**6,
        after,
        held_out=(8, 9),
    )(pos, *blocks, *near, *far, ids, kid, mixed, mixed_one)


def feed_body(pos, unit_in, inv_in, vec, grad_in, pad, three, *refs):
    (layer_out, flow_out, vec_grad_out, keep_out, away_out) = refs[:5]
    w_out, g_in, g_out = refs[5:]
    feat, wide = g_in.shape
    sub = wide // feat
    w_in = three.at[:, :wide]
    rows = keep_out.shape[2]
    for first in range(0, feat, rows):
        for r in range(sub):
            w_out[first * sub + r * rows : first * sub + (r + 1) * rows, :] = three[
                first : first + rows, wide + r * feat : wide + (r + 1) * feat
            ]
    real = jnp.broadcast_to(pad[...].astype(F32), (128, pad.shape[1])).T[:, :1]
    unit_two = unit_in[...]
    normed_two = unit_two * vec[2:3, :] + vec[3:4, :]
    normed_low = low(normed_two)
    inner = dot(normed_low, w_in[...])
    cube = 0.044715 * inner * inner
    bend = jnp.tanh((2.0 / jnp.pi) ** 0.5 * inner * (1.0 + cube))
    active = low(0.5 * inner * (1.0 + bend))
    slope = 0.5 * (1.0 + bend) + 0.5 * inner * (1.0 - bend * bend) * (2.0 / jnp.pi) ** 0.5 * (
        1.0 + 3.0 * cube
    )
    flow = normed_two + dot(active, w_out[...])
    unit, inverse = normalise(flow)
    layer_out[...] = low((unit * vec[4:5, :] + vec[5:6, :]) * real)
    top = grad_in[...].astype(F32) * real
    grad_flow, grad_gain, grad_shift = normalise_back(top, unit, inverse, vec[4:5, :])
    vec_grad_out[...] = jnp.zeros_like(vec_grad_out)
    vec_grad_out[4:5, :] = grad_gain
    vec_grad_out[5:6, :] = grad_shift
    grad_y = low(grad_flow)
    grad_inner = low(slope * dot_t(grad_y, w_out[...]))
    grad_normed = grad_flow + dot_t(grad_inner, w_in[...])
    grad_flow, grad_gain, grad_shift = normalise_back(
        grad_normed, unit_two, inv_in[:, :1], vec[2:3, :]
    )
    vec_grad_out[2:3, :] = grad_gain
    vec_grad_out[3:4, :] = grad_shift
    flow_out[...] = grad_flow
    g_out[...] = low(dot(active.T, grad_y))
    by_distance(pos, g_out, (keep_out, away_out), wide, sub)
    g_in[...] = low(dot(normed_low.T, grad_inner))
    by_distance(pos, g_in, (keep_out, away_out), 0)


def feed(pos, unit, inverse, vec, out_grad, pad, three, whole):
    count, feat = unit.shape
    wide = three.shape[1] // 2
    return kernel_call(
        feed_body,
        (
            shape(count, feat),
            shape(count, feat, dtype=F32),
            shape(8, feat, dtype=F32),
            shape(*whole),
            shape(*whole),
        ),
        [WHOLE] * 5,
        [SCALARS] + [WHOLE] * 6,
        [VM((wide, feat), BF), VM((feat, wide), BF), VM((wide, feat), BF)],
        "feed",
        6 * 10**9,
        20 * 10**6,
        held_in=(1, 2),
        held_out=(1, 2, 3, 4),
    )(pos, unit, inverse, vec, out_grad, pad, three)


def cross_back_body(n_blocks, n_parts, pos, *refs):
    blocks, refs = refs[:n_blocks], refs[n_blocks:]
    near, far, refs = refs[:n_parts], refs[n_parts : 2 * n_parts], refs[2 * n_parts :]
    (flow_in, mixed_two, inverse_two, query, keys_t, values, exps_in) = refs[:7]
    (unit_in, inv_in, vec, vec_grad, mixed_one, inverse_one) = refs[7:13]
    refs = refs[13:]
    flow_out, one_t_out, keep_out, away_out, kv, weight_out = refs[:6]
    weight, grads, query_t, grad_exps, exps, sem = refs[6:]
    count, feat = query.shape
    for pair in range(HEADS // 2):
        fetch(exps_in, exps, sem, pair).start()
    in_order(pos, (near, far), weight, 0)
    grad_y = low(flow_in[...])
    grad_t = over_sums(dot_t(weight[:, 4 * feat : 5 * feat], grad_y), inverse_two)
    grads[:, 4 * feat : 5 * feat] = low(dot(mixed_two[...], grad_y))
    attend_back(
        query, keys_t, values, mixed_two, grad_t, grad_t.T, exps_in, exps, sem, grad_exps, query_t, kv
    )
    grad_query = query_t[...].T
    grad_normed = flow_in[...] + dot_t(grad_query, weight[:, feat : 2 * feat])
    unit = unit_in[...]
    grad_flow, grad_gain, grad_shift = normalise_back(grad_normed, unit, inv_in[:, :1], vec[0:1, :])
    flow_out[...] = grad_flow
    grad_y = low(grad_flow)
    one_t_out[...] = over_sums(dot_t(weight[:, :feat], grad_y), inverse_one)
    grads[:, :feat] = low(dot(mixed_one[...], grad_y))
    normed = low(unit * vec[0:1, :] + vec[1:2, :])
    grads[:, feat : 2 * feat] = low(dot(normed.T, grad_query))
    turned = jnp.concatenate([block[...].T for block in blocks], axis=1)
    grads[:, 2 * feat : 4 * feat] = low(dot(turned, kv[...]))
    rows = jnp.concatenate(
        [grad_gain, grad_shift, vec_grad[2:8, :], jnp.zeros((120, feat), F32)], axis=0
    )
    grads[:, 5 * feat :] = low(rows.T)
    by_distance(pos, grads, (keep_out, away_out), 0)
    weight_out[...] = weight[:, 2 * feat : 4 * feat]


def encoder_part_body(count, pos, kv, weight, parts_out):
    for d in range(kv.shape[0] // count):
        part = dot_t(kv[d * count : (d + 1) * count, :], weight[...])
        place = pl.multiple_of((pos[1] ^ d) * count, count)
        parts_out[pl.ds(place, count), :] = low(part)


def encoder_part(pos, kv, weight, count, after):
    keys, feat = kv.shape[0], weight.shape[0]
    return kernel_call(
        functools.partial(encoder_part_body, count),
        shape(keys, feat),
        WHOLE,
        [SCALARS] + [WHOLE] * 2,
        [],
        "encoder_part",
        4 * 10**9,
        4 * 10**6,
        after,
        held_in=(1, 2),
    )(pos, kv, weight)


def back_scratch(keys, feat, count):
    return [
        VM((keys, 2 * feat), BF),
        VM((feat, count), BF),
        VM((keys, 2 * count), BF),
        VM((HEADS // 2, keys, 2 * count), BF),
        pltpu.SemaphoreType.DMA((HEADS // 2,)),
    ]


def cross_back(pos, blocks, near, far, after, *args):
    count, feat = blocks[0].shape
    keys = count * len(blocks)
    whole = near[0].shape if len(near) == 1 else (len(near),) + near[0].shape
    return kernel_call(
        functools.partial(cross_back_body, len(blocks), len(near)),
        (
            shape(count, feat, dtype=F32),
            shape(feat, count),
            shape(*whole),
            shape(*whole),
        )
        + (shape(keys, 2 * feat), shape(feat, 2 * feat)),
        [WHOLE] * 6,
        [SCALARS] + [WHOLE] * (len(blocks) + 2 * len(near) + 6) + [APART] + [WHOLE] * 6,
        [VM((feat, 5 * feat + 128), BF)] * 2 + back_scratch(keys, feat, count)[1:],
        "cross_back",
        15 * 10**9,
        20 * 10**6,
        after,
        held_in=(1 + len(blocks) + 2 * len(near),),
        held_out=range(6),
    )(pos, *blocks, *near, *far, *args)


def self_back_body(
    n_blocks, n_parts, pos, flow_in, one_t, mixed_one, query, keys_t, values, exps_in, *refs
):
    near, far, refs = refs[:n_parts], refs[n_parts : 2 * n_parts], refs[2 * n_parts :]
    (own_out, query_t_out, kv_out, odd_out, even_out) = refs[:5]
    weight, grad_exps, exps, sem = refs[5:]
    count, feat = query.shape
    for pair in range(HEADS // 2):
        fetch(exps_in, exps, sem, pair).start()
    in_order(pos, (near, far), weight, 0)
    grad_t = one_t[...]
    attend_back(
        query,
        keys_t,
        values,
        mixed_one,
        grad_t,
        grad_t.T,
        exps_in,
        exps,
        sem,
        grad_exps,
        query_t_out,
        kv_out,
    )
    for d in range(1, n_blocks):
        part = dot_t(kv_out[d * count : (d + 1) * count, :], weight[:, feat:])
        if d % 2 == 1:
            odd_out[d // 2] = low(part)
        else:
            even_out[d // 2 - 1] = low(part)
    own = flow_in[...] + dot_t(query_t_out[...].T, weight[:, :feat])
    own_out[...] = own + dot_t(kv_out[:count, :], weight[:, feat:])


def self_back(pos, n_blocks, near, far, after, *args):
    count, feat = args[3].shape
    keys = count * n_blocks
    return kernel_call(
        functools.partial(self_back_body, n_blocks, len(near)),
        (
            shape(count, feat, dtype=F32),
            shape(feat, count),
            shape(keys, 2 * feat),
            shape(n_blocks // 2, count, feat),
            shape((n_blocks - 1) // 2, count, feat),
        ),
        [WHOLE] * 5,
        [SCALARS] + [WHOLE] * 6 + [APART] + [WHOLE] * (2 * len(near)),
        [VM((feat, 3 * feat), BF)] + back_scratch(keys, feat, count)[2:],
        "self_back",
        12 * 10**9,
        20 * 10**6,
        after,
        held_in=(1, 2),
        held_out=range(5),
    )(pos, *args, *near, *far)


def self_grads_body(n_blocks, pos, *refs):
    blocks = refs[:n_blocks]
    query_t, kv, keep_out, away_out, grads = refs[n_blocks:]
    feat, count = query_t.shape
    turned = jnp.concatenate([block[:count, :].T for block in blocks], axis=1)
    grads[:, :feat] = low(dot_t(turned[:, :count], query_t[...]))
    grads[:, feat:] = low(dot(turned, kv[...]))
    by_distance(pos, grads, (keep_out, away_out), 0)


def self_grads(pos, blocks, query_t, kv, part_shape, after):
    feat = query_t.shape[0]
    return kernel_call(
        functools.partial(self_grads_body, len(blocks)),
        (shape(*part_shape), shape(*part_shape)),
        [WHOLE] * 2,
        [SCALARS] + [WHOLE] * (len(blocks) + 2),
        [VM((feat, 3 * feat), BF)],
        "self_grads",
        5 * 10**9,
        8 * 10**6,
        after,
        held_in=(1 + len(blocks), 2 + len(blocks)),
        held_out=(0, 1),
    )(pos, *blocks, query_t, kv)


def pack_body(sub, source, target, glance, ids, pad, *refs):
    weights, (vectors, inner, outer, three, early, mixed) = refs[:8], refs[8:]
    rows, feat = weights[0].shape
    count = glance.shape[1]
    wide = inner.shape[1]
    three[:, :wide] = inner[...]
    for r in range(sub):
        three[:, wide + r * feat : wide + (r + 1) * feat] = outer[r * rows : (r + 1) * rows, :]
    for place, weight in enumerate(weights):
        early[:, place * feat : (place + 1) * feat] = weight[...]
    lines = vectors[...].astype(F32)
    lines = jnp.concatenate([lines, jnp.zeros((128 - lines.shape[0], lines.shape[1]), F32)], axis=0)
    early[:, 8 * feat :] = low(lines.T)[:rows, :]
    taken = jnp.broadcast_to(glance[...].astype(F32), (128, count)).T[:, :1]
    mixed[:count, :] = jnp.where(taken > 0.5, target[0], source[0])
    key_ids = jnp.where(pad[...] == 1, ids[...], -1).astype(F32)
    key_ids = jnp.concatenate([key_ids, jnp.zeros((1, feat - count), F32)], axis=1)
    mixed[count:, :] = low(jnp.broadcast_to(key_ids, (16, feat)))


def join_body(n, *refs):
    for i in range(n):
        refs[n][i] = refs[i][...]


def join(parts, *after):
    return kernel_call(
        functools.partial(join_body, len(parts)),
        shape(len(parts), *parts[0].shape),
        WHOLE,
        [WHOLE] * len(parts),
        [],
        "join",
        10**9,
        2 * 10**6,
        after,
    )(*parts)


def stack_body(n, cuts, *refs):
    parts, outs = refs[:n], refs[n:]
    for out, (first, last) in zip(outs, cuts, strict=True):
        for i in range(n):
            out[i] = parts[i][:, first:last]


def stack(parts, cuts, *after):
    rows = parts[0].shape[0]
    return kernel_call(
        functools.partial(stack_body, len(parts), cuts),
        tuple(shape(len(parts), rows, last - first) for first, last in cuts),
        [WHOLE] * len(cuts),
        [WHOLE] * len(parts),
        [],
        "stack",
        2 * 10**10,
        2 * 10**6,
        after,
    )(*parts)


def hold_body(*refs):
    pass


def hold(block, *after, space=None):
    out = shape(*block.shape, dtype=block.dtype)
    if space is not None:
        block = pltpu.with_memory_space_constraint(block, space)
        out = space(block.shape, block.dtype)
    return pl.pallas_call(
        hold_body,
        out_shape=out,
        in_specs=[APART] * (1 + len(after)),
        out_specs=APART,
        input_output_aliases={0: 0},
        name="hold",
    )(block, *after)


def swap(block, axis_name, size, bits):
    return lax.ppermute(block, axis_name, [(i, i ^ bits) for i in range(size)])


def stages(size):
    bits = size.bit_length() - 1
    return [2] * (bits // 2) + [1] * (bits % 2)


def spread(block, axis_name, size, unit, width):
    return [block] + [swap(block, axis_name, size, unit * far) for far in range(1, 1 << width)]


def spread_line(block, axis_name, size, unit, width):
    if width < 2:
        return spread(block, axis_name, size, unit, width)
    far = swap(block, axis_name, size, 2 * unit)
    return [block, swap(block, axis_name, size, unit), far, swap(far, axis_name, size, unit)]


def over_line(block, seq, way):
    blocks = [block]
    unit = 1
    for width in stages(seq):
        got = [way(b, "seq", seq, unit, width) for b in blocks]
        blocks = [g[far] for far in range(1 << width) for g in got]
        unit <<= width
    return blocks


def add_far_body(cut, keep, away, x_send, y_send, x_rest, y_rest):
    for e in range(4):
        both = low(keep[e].astype(F32) + away[e].astype(F32))
        (x_send if e % 2 == 1 else x_rest)[e // 2] = both[:, :, :cut]
        (y_send if e >= 2 else y_rest)[e % 2] = both[:, :, cut:]


def add_one_body(keep, away, *outs):
    for e in range(4):
        outs[e][...] = low(keep[e].astype(F32) + away[e].astype(F32))


def add_line_body(own, first, second, third, *outs):
    for d in range(4):
        total = own[d].astype(F32) + first[d].astype(F32)
        outs[d][...] = low(total + second[d].astype(F32) + third[d].astype(F32))


def add_mid_body(x_rest, x_got, y_rest, y_got, y_send, x_send, x_own, y_own):
    x_own[...] = x_rest[0].astype(F32) + x_got[0].astype(F32)
    y_send[...] = low(x_rest[1].astype(F32) + x_got[1].astype(F32))
    y_own[...] = y_rest[0].astype(F32) + y_got[0].astype(F32)
    x_send[...] = low(y_rest[1].astype(F32) + y_got[1].astype(F32))


def add_near_body(cut, x_own, x_got, y_own, y_got, own, odd, even):
    for d in range(4):
        left = x_own[d] + x_got[d].astype(F32)
        right = y_own[d] + y_got[d].astype(F32)
        if d == 0:
            own[:, :cut] = left
            own[:, cut:] = right
        elif d == 2:
            even[:, :cut] = low(left)
            even[:, cut:] = low(right)
        else:
            odd[d // 2, :, :cut] = low(left)
            odd[d // 2, :, cut:] = low(right)


def add_call(body, outs, operands, after, name):
    return kernel_call(
        body,
        outs,
        [WHOLE] * len(outs),
        [WHOLE] * len(operands),
        [],
        name,
        10**9,
        4 * 10**6,
        after,
    )(*operands)


def far_step(keep, away, after, fsdp):
    cols = keep.shape[3]
    cut = cols // 256 * 128
    dims = keep.shape[1:3]
    outs = [shape(2, *dims, width) for width in (cut, cols - cut) * 2]
    x_send, y_send, x_rest, y_rest = add_call(
        functools.partial(add_far_body, cut), outs, (keep, away), after, "add_far"
    )
    return (x_send, swap(x_send, "fsdp", fsdp, 2), swap(y_send, "fsdp", fsdp, 4), x_rest, y_rest)


def mid_step(far, after, fsdp):
    _, x_got, y_got, x_rest, y_rest = far
    x_dims, y_dims = x_rest.shape[1:], y_rest.shape[1:]
    outs = [shape(*x_dims), shape(*y_dims), shape(*x_dims, dtype=F32), shape(*y_dims, dtype=F32)]
    y_send, x_send, x_own, y_own = add_call(
        add_mid_body, outs, (x_rest, x_got, y_rest, y_got), after, "add_mid"
    )
    return (y_send, swap(y_send, "fsdp", fsdp, 4), swap(x_send, "fsdp", fsdp, 2), x_own, y_own)


def near_step(mid, after):
    _, x_got, y_got, x_own, y_own = mid
    cut = x_own.shape[2]
    rows, cols = x_own.shape[1], cut + y_own.shape[2]
    outs = [shape(rows, cols, dtype=F32), shape(2, rows, cols), shape(rows, cols)]
    return add_call(
        functools.partial(add_near_body, cut), outs, (x_own, x_got, y_own, y_got), after, "add_near"
    )


def finish_line(near, seq, *after):
    own, odd, even = near
    got = swap(odd, "seq", seq, 1)
    if after:
        got = hold(got, *after, space=pltpu.VMEM)
    even = low(even.astype(F32) + got[1].astype(F32))
    return own.astype(F32) + got[0].astype(F32), swap(even, "seq", seq, 2)


def bit_of(axis_name, bit):
    return (lax.axis_index(axis_name) & bit) != 0


def double(block, axis_name, size, bit, place):
    other = swap(block, axis_name, size, bit)
    high = bit_of(axis_name, bit)
    return jnp.where(
        high, jnp.stack([other, block], axis=place), jnp.stack([block, other], axis=place)
    )


def bits_below(size):
    return [1 << k for k in range(size.bit_length() - 1)]


def gather_blocks(shard, fsdp, seq, turned):
    block = shard
    for bit in bits_below(seq):
        block = double(block, "seq", seq, bit, 1)
    upper = bits_below(fsdp)[1:]
    done = []
    for bit in upper[::-1] if turned else upper:
        place = 1 + sum(b > bit for b in done)
        block = double(block, "fsdp", fsdp, bit, place)
        done.append(bit)
    if fsdp > 1:
        block = double(block, "fsdp", fsdp, 1, 1 + len(upper))
    return block.reshape(shard.shape[0], fsdp * seq * shard.shape[1], shard.shape[2])


def halve(block, axis_name, size, bit, place):
    high = bit_of(axis_name, bit).astype(jnp.int32)
    away = lax.dynamic_index_in_dim(block, 1 - high, place, keepdims=False)
    kept = lax.dynamic_index_in_dim(block, high, place, keepdims=False)
    other = swap(away, axis_name, size, bit)
    return (kept.astype(jnp.float32) + other.astype(jnp.float32)).astype(jnp.bfloat16)


def scatter_blocks(whole, fsdp, seq, turned):
    w, depth, cols = whole.shape
    n_up = len(bits_below(fsdp)) - 1
    n_seq = len(bits_below(seq))
    rows = depth // (fsdp * seq)
    block = whole.reshape((w,) + (2,) * (n_up + 1 + n_seq) + (rows, cols))
    block = halve(block, "fsdp", fsdp, 1, 1 + n_up)
    upper = bits_below(fsdp)[1:]
    left = list(upper)
    for bit in upper[::-1] if turned else upper:
        place = 1 + sum(b > bit for b in left)
        block = halve(block, "fsdp", fsdp, bit, place)
        left.remove(bit)
    for bit in bits_below(seq)[::-1]:
        block = halve(block, "seq", seq, bit, 1)
    return block.astype(jnp.float32)


def whole_parts(shard, fsdp, seq):
    whole = gather_blocks(shard[None], fsdp, seq, False)[0]
    parts = whole.reshape(4, 2, 4, -1, whole.shape[1])
    return parts[:, 0], parts[:, 1]


def whole_sum(keep, away, fsdp, seq):
    whole = jnp.stack([keep, away], axis=1).reshape(-1, keep.shape[3])
    return scatter_blocks(whole[None], fsdp, seq, False)[0]


def regroup(three, rows, to, wide):
    feat = three.shape[0]
    sub = wide // feat
    outer = three[:, wide:].reshape(-1, rows, sub, feat).transpose(0, 2, 1, 3)
    outer = outer.reshape(-1, sub, to, feat).transpose(0, 2, 1, 3)
    return jnp.concatenate([three[:, :wide], outer.reshape(feat, sub * feat)], axis=1)


def make(fsdp, seq):
    def on_device(
        source_copy,
        target_embed,
        glance_mask,
        segment_ids,
        pad_mask,
        encoder_out,
        out_grad,
        self_query,
        self_key,
        self_value,
        self_output,
        norm1_gain,
        norm1_shift,
        cross_query,
        cross_key,
        cross_value,
        cross_output,
        norm2_gain,
        norm2_shift,
        inner_weight,
        outer_weight,
        norm3_gain,
        norm3_shift,
    ):
        row_count, loc_count, feat = source_copy.shape
        count = row_count * loc_count
        chunk = self_query.shape[0]
        sub = outer_weight.shape[0] // chunk
        pos = jnp.stack([lax.axis_index("fsdp"), lax.axis_index("seq")]).astype(jnp.int32)
        ids = segment_ids.reshape(1, count)
        pad = pad_mask.reshape(1, count)
        encoder = encoder_out.reshape(count, feat)
        vectors = jnp.stack(
            [norm1_gain, norm1_shift, norm2_gain, norm2_shift, norm3_gain, norm3_shift]
        )
        vectors = jnp.pad(vectors, ((0, 0), (0, 128 - chunk)))
        wide = sub * feat
        three, early, mixed = kernel_call(
            functools.partial(pack_body, sub),
            (shape(chunk, 2 * wide), shape(chunk, 8 * feat + 128), shape(count + 16, feat)),
            [WHOLE] * 3,
            [WHOLE] * 16,
            [],
            "pack",
            10**9,
            2 * 10**6,
        )(
            source_copy,
            target_embed,
            glance_mask.reshape(1, count),
            ids,
            pad,
            self_query,
            self_key,
            self_value,
            self_output,
            cross_query,
            cross_key,
            cross_value,
            cross_output,
            vectors,
            inner_weight,
            outer_weight,
        )
        all_three = lax.all_gather(three, ("fsdp", "seq"), axis=0, tiled=True)
        home = pos
        near_rows = seq == 4 and fsdp == 8 and chunk % 16 == 0
        if near_rows:
            early_blocks = over_line(early, seq, spread)
            mixed_far = swap(mixed, "seq", seq, 2)
            line_one, line_two = stack(early_blocks, ((0, 3 * feat), (3 * feat, 8 * feat + 128)))
            plane_one = spread(line_one, "fsdp", fsdp, 2, 2)
            mixed_late = hold(mixed, line_one)
            mixed_far = hold(mixed_far, line_one)
            mixed_blocks = [mixed, swap(mixed_late, "seq", seq, 1), mixed_far]
            mixed_blocks.append(swap(mixed_far, "seq", seq, 1))
            near_one = join(plane_one, *mixed_blocks[1:])
            far_one = swap(near_one, "fsdp", fsdp, 1)
            line_two = hold(line_two, near_one)
            encoder_late = hold(encoder, near_one)
            plane_two = spread(line_two, "fsdp", fsdp, 2, 2)
            encoder_far = swap(encoder_late, "seq", seq, 2)
            encoder_near = swap(hold(encoder, far_one), "seq", seq, 1)

        else:
            home = jnp.zeros_like(pos)
            near_one, far_one = whole_parts(early[:, : 3 * feat], fsdp, seq)
            near_two, far_two = whole_parts(early[:, 3 * feat :], fsdp, seq)
            all_three = regroup(all_three, chunk, near_one.shape[2], wide)
            mixed_blocks = over_line(mixed, seq, spread)
            encoder_blocks = over_line(encoder, seq, spread)

        q_one, v_one, kt_one, mixed_one, inverse_one, key_rows, exps_one = self_attend(
            home, mixed_blocks, ids, [near_one], [far_one], count, feat, ()
        )
        if near_rows:
            plane_two = [line_two] + [hold(part, mixed_one) for part in plane_two[1:]]
            encoder_far = hold(encoder_far, mixed_one)
            near_two = plane_two
            far_two = [swap(part, "fsdp", fsdp, 1) for part in near_two]
            encoder_blocks = [encoder, hold(encoder_near, mixed_one), encoder_far]
            encoder_blocks.append(swap(encoder_far, "seq", seq, 1))
        else:
            near_two, far_two = [near_two], [far_two]
        (
            vec,
            unit_one,
            inv_one,
            q_two,
            v_two,
            kt_two,
            mixed_two,
            inverse_two,
            unit_two,
            inv_two,
            exps_two,
        ) = cross_attend(
            home,
            encoder_blocks,
            ids,
            key_rows,
            mixed,
            mixed_one,
            near_two,
            far_two,
            (),
        )
        layer_out, flow_two, vec_grad, keep_three, away_three = feed(
            home,
            unit_two,
            inv_two,
            vec,
            out_grad.reshape(count, feat),
            pad,
            all_three,
            near_one.shape[:3] + (2 * wide,),
        )
        after_feed, after_parts = (), ()
        if near_rows:
            away_three = swap(away_three, "fsdp", fsdp, 1)
            far_three = far_step(keep_three, away_three, (), fsdp)
            after_feed = (far_three[0],)
        flow_one, one_t, keep_two, away_two, kv_two, weight_two = cross_back(
            home,
            encoder_blocks,
            near_two,
            far_two,
            after_feed,
            flow_two,
            mixed_two,
            inverse_two,
            q_two,
            kt_two,
            v_two,
            exps_two,
            unit_one,
            inv_one,
            vec,
            vec_grad,
            mixed_one,
            inverse_one,
        )
        if near_rows:
            mid_three = mid_step(far_three, (flow_one,), fsdp)
            away_two = swap(hold(away_two, mid_three[0], space=pltpu.VMEM), "fsdp", fsdp, 1)
            after_parts = (mid_three[0],)
        encoder_parts = encoder_part(pos, kv_two, weight_two, count, after_parts)
        encoder_grad = lax.psum_scatter(
            encoder_parts, "seq", scatter_dimension=0, tiled=True
        ).astype(F32)
        after_back, after_grads = (), ()
        if near_rows:
            far_two = far_step(keep_two, away_two, (encoder_parts,), fsdp)
            after_back = (far_two[0],)
        input_own, query_t, kv, odd_parts, even_parts = self_back(
            home,
            seq,
            [near_one],
            [far_one],
            after_back,
            flow_one,
            one_t,
            mixed_one,
            q_one,
            kt_one,
            v_one,
            exps_one,
        )
        if near_rows:
            near_three = near_step(mid_three, (query_t,))
            mid_two = mid_step(far_two, (query_t,), fsdp)
            after_grads = (near_three[0], mid_two[0])
        keep_one, away_one = self_grads(
            home, mixed_blocks, query_t, kv, near_one.shape, after_grads
        )
        input_after = ()
        if near_rows:
            got_two = [hold(got, keep_one, space=pltpu.VMEM) for got in mid_two[1:3]]
            mid_two = (mid_two[0], *got_two, *mid_two[3:])
            away_one = swap(hold(away_one, *got_two, space=pltpu.VMEM), "fsdp", fsdp, 1)
            near_three = finish_line(near_three, seq, away_one)
            near_two = near_step(mid_two, ())
            one_send = add_call(
                add_one_body,
                [shape(*keep_one.shape[1:])] * 4,
                (keep_one, away_one),
                (near_two[0],),
                "add_one",
            )
            got_one = [swap(one_send[e], "fsdp", fsdp, 2 * e) for e in (1, 2, 3)]
            line_one = add_call(
                add_line_body,
                [shape(*keep_one.shape[2:])] * 4,
                (one_send[0], *got_one),
                (),
                "add_line",
            )
            got_line = [swap(line_one[d], "seq", seq, d) for d in (1, 2, 3)]
            grads_three = near_three[0] + hold(near_three[1], line_one[0]).astype(F32)
            near_two = finish_line(near_two, seq, line_one[0])
            grads_two = near_two[0] + near_two[1].astype(F32)
            grads_one = line_one[0].astype(F32)
            for block in got_line:
                grads_one = grads_one + block.astype(F32)
            input_after = (one_send[0],)
        else:
            grads_one = whole_sum(keep_one, away_one, fsdp, seq)
            grads_two = whole_sum(keep_two, away_two, fsdp, seq)
            grads_three = jnp.stack([keep_three, away_three], axis=1).reshape(feat, 2 * wide)
            grads_three = regroup(grads_three, near_one.shape[2], chunk, wide)
            grads_three = scatter_blocks(grads_three[None], fsdp, seq, False)[0]
        near_input = finish_line((input_own, odd_parts, even_parts[0]), seq, *input_after)
        input_grad = near_input[0] + near_input[1].astype(F32)

        def stacked(flat_rows):
            return flat_rows.reshape(row_count, loc_count, feat)

        def cols(grads, place):
            return grads[:, place * feat : (place + 1) * feat]

        vec_out = grads_two[:, 5 * feat : 5 * feat + 6].T
        grad_outer = jnp.concatenate(
            [grads_three[:, wide + r * feat : wide + (r + 1) * feat] for r in range(sub)], axis=0
        )
        return (
            stacked(layer_out),
            stacked(input_grad),
            stacked(encoder_grad),
            cols(grads_one, 0),
            cols(grads_one, 1),
            cols(grads_one, 2),
            cols(grads_two, 0),
            vec_out[0],
            vec_out[1],
            cols(grads_two, 1),
            cols(grads_two, 2),
            cols(grads_two, 3),
            cols(grads_two, 4),
            vec_out[2],
            vec_out[3],
            grads_three[:, :wide],
            grad_outer,
            vec_out[4],
            vec_out[5],
        )

    return on_device


def solution(mesh):
    rows = P("fsdp", "seq", None)
    marks = P("fsdp", "seq")
    weight = P(("fsdp", "seq"), None)
    vector = P(("fsdp", "seq"))
    layer = (weight,) * 4 + (vector,) * 2
    return jax.shard_map(
        make(mesh.shape["fsdp"], mesh.shape["seq"]),
        mesh=mesh,
        in_specs=(rows, rows, marks, marks, marks, rows, rows)
        + layer
        + layer
        + (weight,) * 2
        + (vector,) * 2,
        out_specs=(rows,) * 3 + layer + layer + (weight,) * 2 + (vector,) * 2,
        check_vma=False,
    )
```

```python
import functools

import jax
import jax.numpy as jnp
from jax import lax
from jax.experimental import pallas as pl
from jax.experimental.pallas import tpu as pltpu
from jax.sharding import PartitionSpec as P

HEADS = 8
HEAD = 64
PAIR = 2 * HEAD
SLOT = HEAD + 16


norm_eps = 1e-05
mask_fill = -1e30

BF = jnp.bfloat16
F32 = jnp.float32
VM = pltpu.VMEM
WHOLE = pl.BlockSpec(memory_space=pltpu.VMEM)
SCALARS = pl.BlockSpec(memory_space=pltpu.SMEM)
APART = pl.BlockSpec(memory_space=pl.ANY)


def shape(*dims, dtype=BF):
    return jax.ShapeDtypeStruct(dims, dtype)


def low(values):
    return values.astype(BF)


def dot(left, right):
    return jnp.dot(left, right, preferred_element_type=F32)


def dot_t(left, right):
    return lax.dot_general(left, right, (((1,), (1,)), ((), ())), preferred_element_type=F32)


def head_cols(block, head):
    pair = block[:, head // 2 * PAIR : (head // 2 + 1) * PAIR]
    lane = lax.broadcasted_iota(jnp.int32, pair.shape, 1)
    return jnp.where((lane >= HEAD) == (head % 2 == 1), pair, jnp.zeros_like(pair))


def head_rows(block, head):
    mine = block[head * HEAD : (head + 1) * HEAD, :]
    rest = jnp.zeros_like(mine)
    return jnp.concatenate([mine, rest] if head % 2 == 0 else [rest, mine], axis=0)


def chunk_of(pos, seq, c, e, d):
    return (pos[0] ^ (2 * e + c)) * seq + (pos[1] ^ d)


def in_order(pos, parts, target, col, sub=1):
    width = target.shape[1]
    for c, sides in enumerate(parts):
        if len(sides) == 1:
            sides = [sides[0].at[e] for e in range(sides[0].shape[0])]
        for e, part in enumerate(sides):
            for d in range(part.shape[0]):
                rows = part.shape[1]
                first = chunk_of(pos, part.shape[0], c, e, d) * (rows * sub)
                for r in range(sub):
                    start = pl.multiple_of(first + r * rows, rows)
                    target[pl.ds(start, rows), :] = part[
                        d, :, col + r * width : col + (r + 1) * width
                    ]


def by_distance(pos, source, parts, col, sub=1):
    width = source.shape[1]
    for c, part in enumerate(parts):
        for e in range(part.shape[0]):
            for d in range(part.shape[1]):
                rows = part.shape[2]
                first = chunk_of(pos, part.shape[1], c, e, d) * (rows * sub)
                for r in range(sub):
                    start = pl.multiple_of(first + r * rows, rows)
                    part[e, d, :, col + r * width : col + (r + 1) * width] = source[
                        pl.ds(start, rows), :
                    ]


def normalise(flow):
    centre = jnp.mean(flow, axis=1, keepdims=True)
    centered = flow - centre
    spread = jnp.mean(centered * centered, axis=1, keepdims=True)
    inverse = lax.rsqrt(spread + norm_eps)
    return centered * inverse, inverse


def normalise_back(grad, unit, inverse, gain):
    scaled = grad * gain
    mean_one = jnp.mean(scaled, axis=1, keepdims=True)
    mean_two = jnp.mean(scaled * unit, axis=1, keepdims=True)
    grad_flow = inverse * (scaled - mean_one - unit * mean_two)
    return (
        grad_flow,
        jnp.sum(grad * unit, axis=0, keepdims=True),
        jnp.sum(grad, axis=0, keepdims=True),
    )


def set_bias(key_rows, query_row, bias):
    count = query_row.shape[1]
    for d in range(len(key_rows)):
        column = jnp.broadcast_to(key_rows[d], (128, count)).T
        column = jnp.concatenate([column] * (count // 128), axis=1)
        bias[d * count : (d + 1) * count, :] = jnp.where(column == query_row, 0.0, mask_fill)


def set_values(values, slots, first):
    turned = values.T
    count = values.shape[0]
    cols = slice(first, first + count)
    for head in range(HEADS):
        slots[head * SLOT : head * SLOT + HEAD, cols] = turned[head * HEAD : (head + 1) * HEAD, :]
        slots[head * SLOT + HEAD : (head + 1) * SLOT, cols] = jnp.ones((SLOT - HEAD, count), BF)


def finish_head(head, exp_scores, slots, mixed_out, inverse_out):
    summed = dot(slots[head * SLOT : (head + 1) * SLOT, :], exp_scores)
    inverse = 1.0 / summed[HEAD : HEAD + 1, :]
    mixed_out[head * HEAD : (head + 1) * HEAD, :] = low(summed[:HEAD, :] * inverse)
    inverse_out[head : head + 1, :] = inverse


def attend(query, keys, slots, bias, exps, exps_out, sem, mixed_out, inverse_out):
    count = query.shape[0]

    def scores_of(head):
        pair_keys = keys[:, head // 2 * PAIR : (head // 2 + 1) * PAIR]
        return dot_t(pair_keys, head_cols(query, head)) + bias[...]

    scores, before = scores_of(0), None
    for head in range(HEADS):
        after = scores_of(head + 1) if head + 1 < HEADS else None
        if head > 0:
            finish_head(head - 1, before, slots, mixed_out, inverse_out)
        top = jnp.max(scores, axis=0, keepdims=True)
        before = low(jnp.exp(scores - top))
        exps[head // 2, :, head % 2 * count : (head % 2 + 1) * count] = before
        if head % 2 == 1:
            pltpu.make_async_copy(
                exps.at[head // 2], exps_out.at[head // 2], sem.at[head // 2]
            ).start()
        scores = after
    finish_head(HEADS - 1, before, slots, mixed_out, inverse_out)
    for pair in range(HEADS // 2):
        pltpu.make_async_copy(exps.at[pair], exps_out.at[pair], sem.at[pair]).wait()


def fetch(exps_in, exps, sem, pair):
    return pltpu.make_async_copy(exps_in.at[pair], exps.at[pair], sem.at[pair])


def attend_back(
    query, keys_t, values, mixed_t, grad_t, grad, exps_in, exps, sem, query_t_out, kv_out
):
    count, feat = query.shape

    def head_dot(head):
        rows = slice(head * HEAD, (head + 1) * HEAD)
        both = grad_t[rows, :].astype(F32) * mixed_t[rows, :].astype(F32)
        return jnp.sum(both, axis=0, keepdims=True)

    def grad_probs(pair):
        heads = (2 * pair, 2 * pair + 1)
        both = jnp.concatenate([head_rows(grad_t, head) for head in heads], axis=1)
        return dot(values[:, pair * PAIR : (pair + 1) * PAIR], both)

    def pair_cols(block, pair):
        return jnp.concatenate([head_cols(block, 2 * pair), head_cols(block, 2 * pair + 1)], axis=0)

    row_dots = [head_dot(head) for head in range(HEADS)]
    grad_prob = grad_probs(0)
    for pair in range(HEADS // 2):
        after = grad_probs(pair + 1) if pair + 1 < HEADS // 2 else None
        fetch(exps_in, exps, sem, pair).wait()
        cols = slice(pair * PAIR, (pair + 1) * PAIR)
        exp_scores = exps[pair]
        row_dot = jnp.concatenate([row_dots[2 * pair], row_dots[2 * pair + 1]], axis=1)
        grad_scores = low(exp_scores.astype(F32) * (grad_prob - row_dot))
        kv_out[:, feat + pair * PAIR : feat + (pair + 1) * PAIR] = low(
            dot(exp_scores, pair_cols(grad, pair))
        )
        kv_out[:, cols] = low(dot(grad_scores, pair_cols(query, pair)))
        for head in (2 * pair, 2 * pair + 1):
            rows = slice(head * HEAD, (head + 1) * HEAD)
            mine = grad_scores[:, head % 2 * count : (head % 2 + 1) * count]
            query_t_out[rows, :] = low(dot(keys_t[rows, :], mine) * HEAD ** (-0.5))
        grad_prob = after


def over_sums(grad_t, inverse):
    return low(
        jnp.concatenate(
            [
                grad_t[head * HEAD : (head + 1) * HEAD, :] * inverse[head : head + 1, :]
                for head in range(HEADS)
            ],
            axis=0,
        )
    )


def send_out(pairs, sem):
    copies = [pltpu.make_async_copy(a, b, sem.at[i]) for i, (a, b) in enumerate(pairs)]
    for copy in copies:
        copy.start()
    return copies


def self_attend_body(n_blocks, n_parts, pos, *refs):
    blocks, refs = refs[:n_blocks], refs[n_blocks:]
    near, far, refs = refs[:n_parts], refs[n_parts : 2 * n_parts], refs[2 * n_parts :]
    (ids, q_out, v_out, kt_out, mixed_out, inverse_out, kid_out, exps_out) = refs[:8]
    weight, keys, slots, bias, exps, sem, values, keys_t, out_sem = refs[8:]
    count, feat = q_out.shape
    in_order(pos, (near, far), weight, 0)
    query = low(dot(blocks[0][:count, :], weight[:, :feat]))
    query = query * BF(HEAD ** (-0.5))
    q_out[...] = query
    for d, block in enumerate(blocks):
        rows = slice(d * count, (d + 1) * count)
        key = low(dot(block[:count, :], weight[:, feat : 2 * feat]))
        value = low(dot(block[:count, :], weight[:, 2 * feat :]))
        keys[rows, :] = key
        keys_t[:, rows] = key.T
        values[rows, :] = value
        set_values(value, slots, d * count)
        kid_out[d : d + 1, :] = block[count : count + 1, :count].astype(F32)
    copies = send_out(((keys_t, kt_out), (values, v_out)), out_sem)
    set_bias([kid_out[d : d + 1, :] for d in range(n_blocks)], ids[...].astype(F32), bias)
    attend(query, keys, slots, bias, exps, exps_out, sem, mixed_out, inverse_out)
    for copy in copies:
        copy.wait()


def attend_scratch(keys, feat, count):
    return [
        VM((keys, feat), BF),
        VM((HEADS * SLOT, keys), BF),
        VM((keys, count), F32),
        VM((HEADS // 2, keys, 2 * count), BF),
        pltpu.SemaphoreType.DMA((HEADS // 2,)),
        VM((keys, feat), BF),
        VM((feat, keys), BF),
        pltpu.SemaphoreType.DMA((2,)),
    ]


SMALL = ("stack", "join", "add_far", "add_mid", "add_near", "add_one", "add_line")
ROOM = {"self_attend": 22, "cross_attend": 24, "feed": 28, "cross_back": 28, "self_back": 22}


def kernel_call(
    body, outs, out_specs, in_specs, scratch, name, flops, size, after=(), held_in=(), held_out=()
):
    n_in = len(in_specs)
    small = name in SMALL

    def space(place, held):
        return pltpu.VMEM if small or place in held else pltpu.HBM

    def run(*refs):
        body(*refs[:n_in], *refs[n_in + len(after) :])

    single = not isinstance(outs, (tuple, list))
    outs = tuple(
        space(place, held_out)(out.shape, out.dtype)
        for place, out in enumerate([outs] if single else outs)
    )
    outs = outs[0] if single else outs
    call = pl.pallas_call(
        run if after else body,
        out_shape=outs,
        in_specs=in_specs + [APART] * len(after),
        out_specs=out_specs,
        scratch_shapes=scratch,
        compiler_params=pltpu.CompilerParams(vmem_limit_bytes=(4 if small else ROOM.get(name, 12)) * 2**20),
        cost_estimate=pl.CostEstimate(flops=flops, bytes_accessed=size, transcendentals=0),
        name=name,
    )

    def go(*operands):
        operands = [
            x
            if spec is SCALARS
            else pltpu.with_memory_space_constraint(x, space(place, held_in))
            for place, (x, spec) in enumerate(zip(operands, in_specs, strict=True))
        ]
        return call(*operands, *after)

    return go


def self_attend(pos, blocks, ids, near, far, count, feat, after):
    keys = count * len(blocks)
    return kernel_call(
        functools.partial(self_attend_body, len(blocks), len(near)),
        (
            shape(count, feat),
            shape(keys, feat),
            shape(feat, keys),
            shape(feat, count),
            shape(HEADS, count, dtype=F32),
            shape(len(blocks), count, dtype=F32),
            shape(HEADS // 2, keys, 2 * count),
        ),
        [WHOLE] + [APART] * 2 + [WHOLE] * 3 + [APART],
        [SCALARS] + [WHOLE] * (len(blocks) + 2 * len(near) + 1),
        [VM((feat, 3 * feat), BF)] + attend_scratch(keys, feat, count),
        "self_attend",
        12 * 10**9,
        20 * 10**6,
        after,
    )(pos, *blocks, *near, *far, ids)


def cross_attend_body(n_blocks, n_parts, pos, *refs):
    blocks, refs = refs[:n_blocks], refs[n_blocks:]
    near, far, refs = refs[:n_parts], refs[n_parts : 2 * n_parts], refs[2 * n_parts :]
    (ids, kid, mixed, mixed_one) = refs[:4]
    (vec_out, unit_out, inv_out, q_out, v_out, kt_out, mixed_out, inverse_out) = refs[4:12]
    (unit_two_out, inv_two_out, exps_out) = refs[12:15]
    weight, keys, slots, bias, exps, sem, values, keys_t, out_sem = refs[15:]
    count, feat = q_out.shape
    in_order(pos, (near, far), weight, 0)
    vec_out[...] = weight[:, 5 * feat :].astype(F32).T[:8, :]
    flow = mixed[:count, :].astype(F32) + dot(mixed_one[...].T, weight[:, :feat])
    unit, inverse = normalise(flow)
    unit_out[...] = unit
    inv_out[...] = jnp.broadcast_to(inverse, inv_out.shape)
    normed = unit * vec_out[0:1, :] + vec_out[1:2, :]
    query = low(dot(low(normed), weight[:, feat : 2 * feat])) * BF(HEAD ** (-0.5))
    q_out[...] = query
    for d, block in enumerate(blocks):
        rows = slice(d * count, (d + 1) * count)
        key = low(dot(block[...], weight[:, 2 * feat : 3 * feat]))
        value = low(dot(block[...], weight[:, 3 * feat : 4 * feat]))
        keys[rows, :] = key
        keys_t[:, rows] = key.T
        values[rows, :] = value
        set_values(value, slots, d * count)
    copies = send_out(((keys_t, kt_out), (values, v_out)), out_sem)
    set_bias([kid[d : d + 1, :] for d in range(n_blocks)], ids[...].astype(F32), bias)
    attend(query, keys, slots, bias, exps, exps_out, sem, mixed_out, inverse_out)
    flow = unit_out[...] * vec_out[0:1, :] + vec_out[1:2, :]
    flow = flow + dot(mixed_out[...].T, weight[:, 4 * feat : 5 * feat])
    unit, inverse = normalise(flow)
    unit_two_out[...] = unit
    inv_two_out[...] = jnp.broadcast_to(inverse, inv_two_out.shape)
    for copy in copies:
        copy.wait()


def cross_attend(pos, blocks, ids, kid, mixed, mixed_one, near, far, after):
    count, feat = blocks[0].shape
    keys = count * len(blocks)
    return kernel_call(
        functools.partial(cross_attend_body, len(blocks), len(near)),
        (
            shape(8, feat, dtype=F32),
            shape(count, feat, dtype=F32),
            shape(count, 128, dtype=F32),
            shape(count, feat),
            shape(keys, feat),
            shape(feat, keys),
            shape(feat, count),
            shape(HEADS, count, dtype=F32),
            shape(count, feat, dtype=F32),
            shape(count, 128, dtype=F32),
            shape(HEADS // 2, keys, 2 * count),
        ),
        [WHOLE] * 4 + [APART] * 2 + [WHOLE] * 4 + [APART],
        [SCALARS] + [WHOLE] * (len(blocks) + 2 * len(near) + 4),
        [VM((feat, 5 * feat + 128), BF)] + attend_scratch(keys, feat, count),
        "cross_attend",
        14 * 10**9,
        20 * 10**6,
        after,
        held_out=(8, 9),
    )(pos, *blocks, *near, *far, ids, kid, mixed, mixed_one)


def feed_body(pos, unit_in, inv_in, vec, grad_in, pad, three, *refs):
    (layer_out, flow_out, vec_grad_out, keep_out, away_out) = refs[:5]
    w_out, g_in, g_out = refs[5:]
    feat, wide = g_in.shape
    sub = wide // feat
    w_in = three.at[:, :wide]
    rows = keep_out.shape[2]
    for first in range(0, feat, rows):
        for r in range(sub):
            w_out[first * sub + r * rows : first * sub + (r + 1) * rows, :] = three[
                first : first + rows, wide + r * feat : wide + (r + 1) * feat
            ]
    real = jnp.broadcast_to(pad[...].astype(F32), (128, pad.shape[1])).T[:, :1]
    unit_two = unit_in[...]
    normed_two = unit_two * vec[2:3, :] + vec[3:4, :]
    normed_low = low(normed_two)
    inner = dot(normed_low, w_in[...])
    cube = 0.044715 * inner * inner
    bend = jnp.tanh((2.0 / jnp.pi) ** 0.5 * inner * (1.0 + cube))
    active = low(0.5 * inner * (1.0 + bend))
    slope = 0.5 * (1.0 + bend) + 0.5 * inner * (1.0 - bend * bend) * (2.0 / jnp.pi) ** 0.5 * (
        1.0 + 3.0 * cube
    )
    flow = normed_two + dot(active, w_out[...])
    unit, inverse = normalise(flow)
    layer_out[...] = low((unit * vec[4:5, :] + vec[5:6, :]) * real)
    top = grad_in[...].astype(F32) * real
    grad_flow, grad_gain, grad_shift = normalise_back(top, unit, inverse, vec[4:5, :])
    vec_grad_out[...] = jnp.zeros_like(vec_grad_out)
    vec_grad_out[4:5, :] = grad_gain
    vec_grad_out[5:6, :] = grad_shift
    grad_y = low(grad_flow)
    grad_inner = low(slope * dot_t(grad_y, w_out[...]))
    grad_normed = grad_flow + dot_t(grad_inner, w_in[...])
    grad_flow, grad_gain, grad_shift = normalise_back(
        grad_normed, unit_two, inv_in[:, :1], vec[2:3, :]
    )
    vec_grad_out[2:3, :] = grad_gain
    vec_grad_out[3:4, :] = grad_shift
    flow_out[...] = grad_flow
    g_out[...] = low(dot(active.T, grad_y))
    by_distance(pos, g_out, (keep_out, away_out), wide, sub)
    g_in[...] = low(dot(normed_low.T, grad_inner))
    by_distance(pos, g_in, (keep_out, away_out), 0)


def feed(pos, unit, inverse, vec, out_grad, pad, three, whole):
    count, feat = unit.shape
    wide = three.shape[1] // 2
    return kernel_call(
        feed_body,
        (
            shape(count, feat),
            shape(count, feat, dtype=F32),
            shape(8, feat, dtype=F32),
            shape(*whole),
            shape(*whole),
        ),
        [WHOLE] * 5,
        [SCALARS] + [WHOLE] * 6,
        [VM((wide, feat), BF), VM((feat, wide), BF), VM((wide, feat), BF)],
        "feed",
        6 * 10**9,
        20 * 10**6,
        held_in=(1, 2),
        held_out=(1, 2, 3, 4),
    )(pos, unit, inverse, vec, out_grad, pad, three)


def cross_back_body(n_blocks, n_parts, pos, line, *refs):
    blocks, refs = refs[:n_blocks], refs[n_blocks:]
    near, far, refs = refs[:n_parts], refs[n_parts : 2 * n_parts], refs[2 * n_parts :]
    (flow_in, mixed_two, inverse_two, query, keys_t, values, exps_in) = refs[:7]
    (unit_in, inv_in, vec, vec_grad, mixed_one, inverse_one) = refs[7:13]
    refs = refs[13:]
    flow_out, one_t_out, keep_out, away_out, parts_out = refs[:5]
    weight, grads, kv, query_t, exps, sem = refs[5:]
    count, feat = query.shape
    for pair in range(HEADS // 2):
        fetch(exps_in, exps, sem, pair).start()
    in_order(pos, (near, far), weight, 0)
    grad_y = low(flow_in[...])
    grad_t = over_sums(dot_t(weight[:, 4 * feat : 5 * feat], grad_y), inverse_two)
    grads[:, 4 * feat : 5 * feat] = low(dot(mixed_two[...], grad_y))
    attend_back(
        query, keys_t, values, mixed_two, grad_t, grad_t.T, exps_in, exps, sem, query_t, kv
    )
    grad_query = query_t[...].T
    grad_normed = flow_in[...] + dot_t(grad_query, weight[:, feat : 2 * feat])
    unit = unit_in[...]
    grad_flow, grad_gain, grad_shift = normalise_back(grad_normed, unit, inv_in[:, :1], vec[0:1, :])
    flow_out[...] = grad_flow
    grad_y = low(grad_flow)
    one_t_out[...] = over_sums(dot_t(weight[:, :feat], grad_y), inverse_one)
    grads[:, :feat] = low(dot(mixed_one[...], grad_y))
    normed = low(unit * vec[0:1, :] + vec[1:2, :])
    grads[:, feat : 2 * feat] = low(dot(normed.T, grad_query))
    turned = jnp.concatenate([block[...].T for block in blocks], axis=1)
    grads[:, 2 * feat : 4 * feat] = low(dot(turned, kv[...]))
    rows = jnp.concatenate(
        [grad_gain, grad_shift, vec_grad[2:8, :], jnp.zeros((120, feat), F32)], axis=0
    )
    grads[:, 5 * feat :] = low(rows.T)
    by_distance(pos, grads, (keep_out, away_out), 0)
    for d in range(n_blocks):
        part = dot_t(kv[d * count : (d + 1) * count, :], weight[:, 2 * feat : 4 * feat])
        place = pl.multiple_of((line[0] ^ d) * count, count)
        parts_out[pl.ds(place, count), :] = low(part)


def back_scratch(keys, feat, count):
    return [
        VM((keys, 2 * feat), BF),
        VM((feat, count), BF),
        VM((HEADS // 2, keys, 2 * count), BF),
        pltpu.SemaphoreType.DMA((HEADS // 2,)),
    ]


def cross_back(pos, line, blocks, near, far, after, *args):
    count, feat = blocks[0].shape
    keys = count * len(blocks)
    whole = near[0].shape if len(near) == 1 else (len(near),) + near[0].shape
    return kernel_call(
        functools.partial(cross_back_body, len(blocks), len(near)),
        (
            shape(count, feat, dtype=F32),
            shape(feat, count),
            shape(*whole),
            shape(*whole),
        )
        + (shape(keys, feat),),
        [WHOLE] * 5,
        [SCALARS] * 2 + [WHOLE] * (len(blocks) + 2 * len(near) + 6) + [APART] + [WHOLE] * 6,
        [VM((feat, 5 * feat + 128), BF)] * 2 + back_scratch(keys, feat, count),
        "cross_back",
        15 * 10**9,
        20 * 10**6,
        after,
        held_in=(2 + len(blocks) + 2 * len(near),),
        held_out=range(4),
    )(pos, line, *blocks, *near, *far, *args)


def self_back_body(
    n_blocks, n_parts, pos, line, flow_in, one_t, mixed_one, query, keys_t, values, exps_in, *refs
):
    near, far, refs = refs[:n_parts], refs[n_parts : 2 * n_parts], refs[2 * n_parts :]
    (own_out, query_t_out, kv_out, parts_out) = refs[:4]
    weight, exps, sem = refs[4:]
    count, feat = query.shape
    for pair in range(HEADS // 2):
        fetch(exps_in, exps, sem, pair).start()
    in_order(pos, (near, far), weight, 0)
    grad_t = one_t[...]
    attend_back(
        query,
        keys_t,
        values,
        mixed_one,
        grad_t,
        grad_t.T,
        exps_in,
        exps,
        sem,
        query_t_out,
        kv_out,
    )
    for d in range(n_blocks):
        part = dot_t(kv_out[d * count : (d + 1) * count, :], weight[:, feat:])
        place = pl.multiple_of((line[0] ^ d) * count, count)
        parts_out[pl.ds(place, count), :] = low(part)
    own_out[...] = flow_in[...] + dot_t(query_t_out[...].T, weight[:, :feat])


def self_back(pos, line, n_blocks, near, far, after, *args):
    count, feat = args[3].shape
    keys = count * n_blocks
    return kernel_call(
        functools.partial(self_back_body, n_blocks, len(near)),
        (
            shape(count, feat, dtype=F32),
            shape(feat, count),
            shape(keys, 2 * feat),
            shape(keys, feat),
        ),
        [WHOLE] * 4,
        [SCALARS] * 2 + [WHOLE] * 6 + [APART] + [WHOLE] * (2 * len(near)),
        [VM((feat, 3 * feat), BF)] + back_scratch(keys, feat, count)[2:],
        "self_back",
        12 * 10**9,
        20 * 10**6,
        after,
        held_in=(2, 3),
        held_out=(1, 2),
    )(pos, line, *args, *near, *far)


def self_grads_body(n_blocks, pos, *refs):
    blocks = refs[:n_blocks]
    query_t, kv, keep_out, away_out, grads = refs[n_blocks:]
    feat, count = query_t.shape
    turned = jnp.concatenate([block[:count, :].T for block in blocks], axis=1)
    grads[:, :feat] = low(dot_t(turned[:, :count], query_t[...]))
    grads[:, feat:] = low(dot(turned, kv[...]))
    by_distance(pos, grads, (keep_out, away_out), 0)


def self_grads(pos, blocks, query_t, kv, part_shape, after):
    feat = query_t.shape[0]
    return kernel_call(
        functools.partial(self_grads_body, len(blocks)),
        (shape(*part_shape), shape(*part_shape)),
        [WHOLE] * 2,
        [SCALARS] + [WHOLE] * (len(blocks) + 2),
        [VM((feat, 3 * feat), BF)],
        "self_grads",
        5 * 10**9,
        8 * 10**6,
        after,
        held_in=(1 + len(blocks), 2 + len(blocks)),
        held_out=(0, 1),
    )(pos, *blocks, query_t, kv)


def pack_body(sub, source, target, glance, ids, pad, encoder, *refs):
    refs, encoder_out = refs[:-1], refs[-1]
    encoder_out[...] = encoder[...]
    weights, (vectors, inner, outer, three, early, mixed) = refs[:8], refs[8:]
    rows, feat = weights[0].shape
    count = glance.shape[1]
    wide = inner.shape[1]
    three[:, :wide] = inner[...]
    for r in range(sub):
        three[:, wide + r * feat : wide + (r + 1) * feat] = outer[r * rows : (r + 1) * rows, :]
    for place, weight in enumerate(weights):
        early[:, place * feat : (place + 1) * feat] = weight[...]
    lines = vectors[...].astype(F32)
    lines = jnp.concatenate([lines, jnp.zeros((128 - lines.shape[0], lines.shape[1]), F32)], axis=0)
    early[:, 8 * feat :] = low(lines.T)[:rows, :]
    taken = jnp.broadcast_to(glance[...].astype(F32), (128, count)).T[:, :1]
    mixed[:count, :] = jnp.where(taken > 0.5, target[0], source[0])
    key_ids = jnp.where(pad[...] == 1, ids[...], -1).astype(F32)
    key_ids = jnp.concatenate([key_ids, jnp.zeros((1, feat - count), F32)], axis=1)
    mixed[count:, :] = low(jnp.broadcast_to(key_ids, (16, feat)))


def join_body(n, *refs):
    for i in range(n):
        refs[n][i] = refs[i][...]


def join(parts, *after):
    return kernel_call(
        functools.partial(join_body, len(parts)),
        shape(len(parts), *parts[0].shape),
        WHOLE,
        [WHOLE] * len(parts),
        [],
        "join",
        10**9,
        2 * 10**6,
        after,
    )(*parts)


def stack_body(n, cuts, *refs):
    parts, outs = refs[:n], refs[n:]
    for out, (first, last) in zip(outs, cuts, strict=True):
        for i in range(n):
            out[i] = parts[i][:, first:last]


def stack(parts, cuts, *after):
    rows = parts[0].shape[0]
    return kernel_call(
        functools.partial(stack_body, len(parts), cuts),
        tuple(shape(len(parts), rows, last - first) for first, last in cuts),
        [WHOLE] * len(cuts),
        [WHOLE] * len(parts),
        [],
        "stack",
        2 * 10**10,
        2 * 10**6,
        after,
    )(*parts)


def hold_body(*refs):
    pass


def hold(block, *after, space=None):
    out = shape(*block.shape, dtype=block.dtype)
    if space is not None:
        block = pltpu.with_memory_space_constraint(block, space)
        out = space(block.shape, block.dtype)
    return pl.pallas_call(
        hold_body,
        out_shape=out,
        in_specs=[APART] * (1 + len(after)),
        out_specs=APART,
        input_output_aliases={0: 0},
        name="hold",
    )(block, *after)


def swap(block, axis_name, size, bits):
    return lax.ppermute(block, axis_name, [(i, i ^ bits) for i in range(size)])


def stages(size):
    bits = size.bit_length() - 1
    return [2] * (bits // 2) + [1] * (bits % 2)


def spread(block, axis_name, size, unit, width):
    return [block] + [swap(block, axis_name, size, unit * far) for far in range(1, 1 << width)]


def spread_line(block, axis_name, size, unit, width):
    if width < 2:
        return spread(block, axis_name, size, unit, width)
    far = swap(block, axis_name, size, 2 * unit)
    return [block, swap(block, axis_name, size, unit), far, swap(far, axis_name, size, unit)]


def over_line(block, seq, way):
    blocks = [block]
    unit = 1
    for width in stages(seq):
        got = [way(b, "seq", seq, unit, width) for b in blocks]
        blocks = [g[far] for far in range(1 << width) for g in got]
        unit <<= width
    return blocks


def add_far_body(cut, keep, away, x_send, y_send, x_rest, y_rest):
    for e in range(4):
        both = low(keep[e].astype(F32) + away[e].astype(F32))
        (x_send if e % 2 == 1 else x_rest)[e // 2] = both[:, :, :cut]
        (y_send if e >= 2 else y_rest)[e % 2] = both[:, :, cut:]


def add_one_body(keep, away, *outs):
    for e in range(4):
        outs[e][...] = low(keep[e].astype(F32) + away[e].astype(F32))


def add_line_body(own, first, second, third, *outs):
    for d in range(4):
        total = own[d].astype(F32) + first[d].astype(F32)
        outs[d][...] = low(total + second[d].astype(F32) + third[d].astype(F32))


def add_mid_body(x_rest, x_got, y_rest, y_got, y_send, x_send, x_own, y_own):
    x_own[...] = x_rest[0].astype(F32) + x_got[0].astype(F32)
    y_send[...] = low(x_rest[1].astype(F32) + x_got[1].astype(F32))
    y_own[...] = y_rest[0].astype(F32) + y_got[0].astype(F32)
    x_send[...] = low(y_rest[1].astype(F32) + y_got[1].astype(F32))


def add_near_body(cut, x_own, x_got, y_own, y_got, own, odd, even):
    for d in range(4):
        left = x_own[d] + x_got[d].astype(F32)
        right = y_own[d] + y_got[d].astype(F32)
        if d == 0:
            own[:, :cut] = left
            own[:, cut:] = right
        elif d == 2:
            even[:, :cut] = low(left)
            even[:, cut:] = low(right)
        else:
            odd[d // 2, :, :cut] = low(left)
            odd[d // 2, :, cut:] = low(right)


def add_call(body, outs, operands, after, name):
    return kernel_call(
        body,
        outs,
        [WHOLE] * len(outs),
        [WHOLE] * len(operands),
        [],
        name,
        10**9,
        4 * 10**6,
        after,
    )(*operands)


def far_step(keep, away, after, fsdp):
    cols = keep.shape[3]
    cut = cols // 256 * 128
    dims = keep.shape[1:3]
    outs = [shape(2, *dims, width) for width in (cut, cols - cut) * 2]
    x_send, y_send, x_rest, y_rest = add_call(
        functools.partial(add_far_body, cut), outs, (keep, away), after, "add_far"
    )
    return (x_send, swap(x_send, "fsdp", fsdp, 2), swap(y_send, "fsdp", fsdp, 4), x_rest, y_rest)


def mid_step(far, after, fsdp):
    _, x_got, y_got, x_rest, y_rest = far
    x_dims, y_dims = x_rest.shape[1:], y_rest.shape[1:]
    outs = [shape(*x_dims), shape(*y_dims), shape(*x_dims, dtype=F32), shape(*y_dims, dtype=F32)]
    y_send, x_send, x_own, y_own = add_call(
        add_mid_body, outs, (x_rest, x_got, y_rest, y_got), after, "add_mid"
    )
    return (y_send, swap(y_send, "fsdp", fsdp, 4), swap(x_send, "fsdp", fsdp, 2), x_own, y_own)


def near_step(mid, after):
    _, x_got, y_got, x_own, y_own = mid
    cut = x_own.shape[2]
    rows, cols = x_own.shape[1], cut + y_own.shape[2]
    outs = [shape(rows, cols, dtype=F32), shape(2, rows, cols), shape(rows, cols)]
    return add_call(
        functools.partial(add_near_body, cut), outs, (x_own, x_got, y_own, y_got), after, "add_near"
    )


def finish_line(near, seq, *after):
    own, odd, even = near
    got = swap(odd, "seq", seq, 1)
    if after:
        got = hold(got, *after, space=pltpu.VMEM)
    even = low(even.astype(F32) + got[1].astype(F32))
    return own.astype(F32) + got[0].astype(F32), swap(even, "seq", seq, 2)


def bit_of(axis_name, bit):
    return (lax.axis_index(axis_name) & bit) != 0


def double(block, axis_name, size, bit, place):
    other = swap(block, axis_name, size, bit)
    high = bit_of(axis_name, bit)
    return jnp.where(
        high, jnp.stack([other, block], axis=place), jnp.stack([block, other], axis=place)
    )


def bits_below(size):
    return [1 << k for k in range(size.bit_length() - 1)]


def gather_blocks(shard, fsdp, seq, turned):
    block = shard
    for bit in bits_below(seq):
        block = double(block, "seq", seq, bit, 1)
    upper = bits_below(fsdp)[1:]
    done = []
    for bit in upper[::-1] if turned else upper:
        place = 1 + sum(b > bit for b in done)
        block = double(block, "fsdp", fsdp, bit, place)
        done.append(bit)
    if fsdp > 1:
        block = double(block, "fsdp", fsdp, 1, 1 + len(upper))
    return block.reshape(shard.shape[0], fsdp * seq * shard.shape[1], shard.shape[2])


def halve(block, axis_name, size, bit, place):
    high = bit_of(axis_name, bit).astype(jnp.int32)
    away = lax.dynamic_index_in_dim(block, 1 - high, place, keepdims=False)
    kept = lax.dynamic_index_in_dim(block, high, place, keepdims=False)
    other = swap(away, axis_name, size, bit)
    return (kept.astype(jnp.float32) + other.astype(jnp.float32)).astype(jnp.bfloat16)


def scatter_blocks(whole, fsdp, seq, turned):
    w, depth, cols = whole.shape
    n_up = len(bits_below(fsdp)) - 1
    n_seq = len(bits_below(seq))
    rows = depth // (fsdp * seq)
    block = whole.reshape((w,) + (2,) * (n_up + 1 + n_seq) + (rows, cols))
    block = halve(block, "fsdp", fsdp, 1, 1 + n_up)
    upper = bits_below(fsdp)[1:]
    left = list(upper)
    for bit in upper[::-1] if turned else upper:
        place = 1 + sum(b > bit for b in left)
        block = halve(block, "fsdp", fsdp, bit, place)
        left.remove(bit)
    for bit in bits_below(seq)[::-1]:
        block = halve(block, "seq", seq, bit, 1)
    return block.astype(jnp.float32)


def whole_parts(shard, fsdp, seq):
    whole = gather_blocks(shard[None], fsdp, seq, False)[0]
    parts = whole.reshape(4, 2, 4, -1, whole.shape[1])
    return parts[:, 0], parts[:, 1]


def whole_sum(keep, away, fsdp, seq):
    whole = jnp.stack([keep, away], axis=1).reshape(-1, keep.shape[3])
    return scatter_blocks(whole[None], fsdp, seq, False)[0]


def regroup(three, rows, to, wide):
    feat = three.shape[0]
    sub = wide // feat
    outer = three[:, wide:].reshape(-1, rows, sub, feat).transpose(0, 2, 1, 3)
    outer = outer.reshape(-1, sub, to, feat).transpose(0, 2, 1, 3)
    return jnp.concatenate([three[:, :wide], outer.reshape(feat, sub * feat)], axis=1)


def make(fsdp, seq):
    def on_device(
        source_copy,
        target_embed,
        glance_mask,
        segment_ids,
        pad_mask,
        encoder_out,
        out_grad,
        self_query,
        self_key,
        self_value,
        self_output,
        norm1_gain,
        norm1_shift,
        cross_query,
        cross_key,
        cross_value,
        cross_output,
        norm2_gain,
        norm2_shift,
        inner_weight,
        outer_weight,
        norm3_gain,
        norm3_shift,
    ):
        row_count, loc_count, feat = source_copy.shape
        count = row_count * loc_count
        chunk = self_query.shape[0]
        sub = outer_weight.shape[0] // chunk
        pos = jnp.stack([lax.axis_index("fsdp"), lax.axis_index("seq")]).astype(jnp.int32)
        ids = segment_ids.reshape(1, count)
        pad = pad_mask.reshape(1, count)
        encoder = encoder_out.reshape(count, feat)
        vectors = jnp.stack(
            [norm1_gain, norm1_shift, norm2_gain, norm2_shift, norm3_gain, norm3_shift]
        )
        vectors = jnp.pad(vectors, ((0, 0), (0, 128 - chunk)))
        wide = sub * feat
        three, early, mixed, encoder = kernel_call(
            functools.partial(pack_body, sub),
            (shape(chunk, 2 * wide), shape(chunk, 8 * feat + 128), shape(count + 16, feat), shape(count, feat)),
            [WHOLE] * 4,
            [WHOLE] * 17,
            [],
            "pack",
            10**9,
            2 * 10**6,
        )(
            source_copy,
            target_embed,
            glance_mask.reshape(1, count),
            ids,
            pad,
            encoder,
            self_query,
            self_key,
            self_value,
            self_output,
            cross_query,
            cross_key,
            cross_value,
            cross_output,
            vectors,
            inner_weight,
            outer_weight,
        )
        all_three = lax.all_gather(three, ("fsdp", "seq"), axis=0, tiled=True)
        home = pos
        near_rows = seq == 4 and fsdp == 8 and chunk % 16 == 0
        if near_rows:
            early_blocks = over_line(early, seq, spread)
            mixed_far = swap(mixed, "seq", seq, 2)
            mixed_near = swap(mixed, "seq", seq, 1)
            line_one, line_two = stack(
                early_blocks, ((0, 3 * feat), (3 * feat, 8 * feat + 128)), mixed_near
            )
            plane_one = spread(line_one, "fsdp", fsdp, 2, 2)
            near_one = join(plane_one, mixed_far)
            far_one = swap(near_one, "fsdp", fsdp, 1)
            mixed_far = hold(mixed_far, near_one, space=pltpu.VMEM)
            mixed_blocks = [mixed, mixed_near, mixed_far, swap(mixed_far, "seq", seq, 1)]
            plane_two = spread(line_two, "fsdp", fsdp, 2, 2)
            encoder_late = hold(encoder, far_one)
            encoder_far = swap(encoder_late, "seq", seq, 2)
            encoder_near = swap(encoder_late, "seq", seq, 1)
        else:
            home = jnp.zeros_like(pos)
            near_one, far_one = whole_parts(early[:, : 3 * feat], fsdp, seq)
            near_two, far_two = whole_parts(early[:, 3 * feat :], fsdp, seq)
            all_three = regroup(all_three, chunk, near_one.shape[2], wide)
            mixed_blocks = over_line(mixed, seq, spread)
            encoder_blocks = over_line(encoder, seq, spread)

        q_one, v_one, kt_one, mixed_one, inverse_one, key_rows, exps_one = self_attend(
            home, mixed_blocks, ids, [near_one], [far_one], count, feat, ()
        )
        if near_rows:
            encoder_far = hold(encoder_far, mixed_one, space=pltpu.VMEM)
            got_two = [hold(part, encoder_far, space=pltpu.VMEM) for part in plane_two[1:]]
            encoder_near = hold(encoder_near, mixed_one, space=pltpu.VMEM)
            near_two = join([line_two, *got_two], encoder_near)
            far_two = swap(near_two, "fsdp", fsdp, 1)
            near_two, far_two = [near_two], [far_two]
            encoder_blocks = [encoder, encoder_near, encoder_far]
            encoder_blocks.append(swap(encoder_far, "seq", seq, 1))
        else:
            near_two, far_two = [near_two], [far_two]
        (
            vec,
            unit_one,
            inv_one,
            q_two,
            v_two,
            kt_two,
            mixed_two,
            inverse_two,
            unit_two,
            inv_two,
            exps_two,
        ) = cross_attend(
            home,
            encoder_blocks,
            ids,
            key_rows,
            mixed,
            mixed_one,
            near_two,
            far_two,
            (),
        )
        layer_out, flow_two, vec_grad, keep_three, away_three = feed(
            home,
            unit_two,
            inv_two,
            vec,
            out_grad.reshape(count, feat),
            pad,
            all_three,
            near_one.shape[:3] + (2 * wide,),
        )
        after_feed = ()
        if near_rows:
            away_three = swap(away_three, "fsdp", fsdp, 1)
            far_three = far_step(keep_three, away_three, (), fsdp)
            after_feed = (far_three[0],)
        flow_one, one_t, keep_two, away_two, encoder_parts = cross_back(
            home,
            pos[1:],
            encoder_blocks,
            near_two,
            far_two,
            after_feed,
            flow_two,
            mixed_two,
            inverse_two,
            q_two,
            kt_two,
            v_two,
            exps_two,
            unit_one,
            inv_one,
            vec,
            vec_grad,
            mixed_one,
            inverse_one,
        )
        if near_rows:
            mid_three = mid_step(far_three, (flow_one,), fsdp)
            away_two = swap(hold(away_two, mid_three[0], space=pltpu.VMEM), "fsdp", fsdp, 1)
        encoder_grad = lax.psum_scatter(
            encoder_parts, "seq", scatter_dimension=0, tiled=True
        ).astype(F32)
        after_back, after_grads = (), ()
        if near_rows:
            far_two = far_step(keep_two, away_two, (), fsdp)
            after_back = (far_two[0],)
        input_own, query_t, kv, input_parts = self_back(
            home,
            pos[1:],
            seq,
            [near_one],
            [far_one],
            after_back,
            flow_one,
            one_t,
            mixed_one,
            q_one,
            kt_one,
            v_one,
            exps_one,
        )
        if near_rows:
            near_three = near_step(mid_three, (query_t,))
            mid_two = mid_step(far_two, (query_t,), fsdp)
            after_grads = (near_three[0], mid_two[0])
        keep_one, away_one = self_grads(
            home, mixed_blocks, query_t, kv, near_one.shape, after_grads
        )
        if near_rows:
            got_two = [hold(got, keep_one, space=pltpu.VMEM) for got in mid_two[1:3]]
            mid_two = (mid_two[0], *got_two, *mid_two[3:])
            away_one = swap(hold(away_one, *got_two, space=pltpu.VMEM), "fsdp", fsdp, 1)
            one_send = add_call(
                add_one_body,
                [shape(*keep_one.shape[1:])] * 4,
                (keep_one, away_one),
                (),
                "add_one",
            )
            near_two = near_step(mid_two, (one_send[0],))
            near_three = finish_line(near_three, seq, one_send[0])
            got_one = [swap(one_send[e], "fsdp", fsdp, 2 * e) for e in (1, 2, 3)]
            line_one = add_call(
                add_line_body,
                [shape(*keep_one.shape[2:])] * 4,
                (one_send[0], *got_one),
                (),
                "add_line",
            )
            got_line = [swap(line_one[d], "seq", seq, d) for d in (1, 2, 3)]
            grads_three = near_three[0] + hold(near_three[1], got_line[0]).astype(F32)
            near_two = finish_line(near_two, seq, line_one[0])
            grads_two = near_two[0] + near_two[1].astype(F32)
            grads_one = line_one[0].astype(F32)
            for block in got_line:
                grads_one = grads_one + block.astype(F32)
        else:
            grads_one = whole_sum(keep_one, away_one, fsdp, seq)
            grads_two = whole_sum(keep_two, away_two, fsdp, seq)
            grads_three = jnp.stack([keep_three, away_three], axis=1).reshape(feat, 2 * wide)
            grads_three = regroup(grads_three, near_one.shape[2], chunk, wide)
            grads_three = scatter_blocks(grads_three[None], fsdp, seq, False)[0]
        input_got = lax.psum_scatter(input_parts, "seq", scatter_dimension=0, tiled=True)
        input_grad = input_own + input_got.astype(F32)

        def stacked(flat_rows):
            return flat_rows.reshape(row_count, loc_count, feat)

        def cols(grads, place):
            return grads[:, place * feat : (place + 1) * feat]

        vec_out = grads_two[:, 5 * feat : 5 * feat + 6].T
        grad_outer = jnp.concatenate(
            [grads_three[:, wide + r * feat : wide + (r + 1) * feat] for r in range(sub)], axis=0
        )
        return (
            stacked(layer_out),
            stacked(input_grad),
            stacked(encoder_grad),
            cols(grads_one, 0),
            cols(grads_one, 1),
            cols(grads_one, 2),
            cols(grads_two, 0),
            vec_out[0],
            vec_out[1],
            cols(grads_two, 1),
            cols(grads_two, 2),
            cols(grads_two, 3),
            cols(grads_two, 4),
            vec_out[2],
            vec_out[3],
            grads_three[:, :wide],
            grad_outer,
            vec_out[4],
            vec_out[5],
        )

    return on_device


def solution(mesh):
    rows = P("fsdp", "seq", None)
    marks = P("fsdp", "seq")
    weight = P(("fsdp", "seq"), None)
    vector = P(("fsdp", "seq"))
    layer = (weight,) * 4 + (vector,) * 2
    return jax.shard_map(
        make(mesh.shape["fsdp"], mesh.shape["seq"]),
        mesh=mesh,
        in_specs=(rows, rows, marks, marks, marks, rows, rows)
        + layer
        + layer
        + (weight,) * 2
        + (vector,) * 2,
        out_specs=(rows,) * 3 + layer + layer + (weight,) * 2 + (vector,) * 2,
        check_vma=False,
    )
```

```python
import functools

import jax
import jax.numpy as jnp
from jax import lax
from jax.experimental import pallas as pl
from jax.experimental.pallas import tpu as pltpu
from jax.sharding import PartitionSpec as P

HEADS = 8
HEAD = 64
PAIR = 2 * HEAD
SLOT = HEAD + 16


norm_eps = 1e-05
mask_fill = -1e30

BF = jnp.bfloat16
F32 = jnp.float32
VM = pltpu.VMEM
WHOLE = pl.BlockSpec(memory_space=pltpu.VMEM)
SCALARS = pl.BlockSpec(memory_space=pltpu.SMEM)
APART = pl.BlockSpec(memory_space=pl.ANY)


def shape(*dims, dtype=BF):
    return jax.ShapeDtypeStruct(dims, dtype)


def low(values):
    return values.astype(BF)


def dot(left, right):
    return jnp.dot(left, right, preferred_element_type=F32)


def dot_t(left, right):
    return lax.dot_general(left, right, (((1,), (1,)), ((), ())), preferred_element_type=F32)


def head_cols(block, head):
    pair = block[:, head // 2 * PAIR : (head // 2 + 1) * PAIR]
    lane = lax.broadcasted_iota(jnp.int32, pair.shape, 1)
    return jnp.where((lane >= HEAD) == (head % 2 == 1), pair, jnp.zeros_like(pair))


def head_rows(block, head):
    mine = block[head * HEAD : (head + 1) * HEAD, :]
    rest = jnp.zeros_like(mine)
    return jnp.concatenate([mine, rest] if head % 2 == 0 else [rest, mine], axis=0)


def chunk_of(pos, seq, c, e, d):
    return (pos[0] ^ (2 * e + c)) * seq + (pos[1] ^ d)


def in_order(pos, parts, target, col, sub=1):
    width = target.shape[1]
    for c, sides in enumerate(parts):
        if len(sides) == 1:
            sides = [sides[0].at[e] for e in range(sides[0].shape[0])]
        for e, part in enumerate(sides):
            for d in range(part.shape[0]):
                rows = part.shape[1]
                first = chunk_of(pos, part.shape[0], c, e, d) * (rows * sub)
                for r in range(sub):
                    start = pl.multiple_of(first + r * rows, rows)
                    target[pl.ds(start, rows), :] = part[
                        d, :, col + r * width : col + (r + 1) * width
                    ]


def fetch_parts(near, far, held, sem):
    copies = [
        pltpu.make_async_copy(ref, held.at[side], sem.at[side])
        for side, ref in enumerate((near, far))
    ]
    for copy in copies:
        copy.start()
    return copies


def by_distance(pos, source, parts, col, sub=1):
    width = source.shape[1]
    for c, part in enumerate(parts):
        for e in range(part.shape[0]):
            for d in range(part.shape[1]):
                rows = part.shape[2]
                first = chunk_of(pos, part.shape[1], c, e, d) * (rows * sub)
                for r in range(sub):
                    start = pl.multiple_of(first + r * rows, rows)
                    part[e, d, :, col + r * width : col + (r + 1) * width] = source[
                        pl.ds(start, rows), :
                    ]


def normalise(flow):
    centre = jnp.mean(flow, axis=1, keepdims=True)
    centered = flow - centre
    spread = jnp.mean(centered * centered, axis=1, keepdims=True)
    inverse = lax.rsqrt(spread + norm_eps)
    return centered * inverse, inverse


def normalise_back(grad, unit, inverse, gain):
    scaled = grad * gain
    mean_one = jnp.mean(scaled, axis=1, keepdims=True)
    mean_two = jnp.mean(scaled * unit, axis=1, keepdims=True)
    grad_flow = inverse * (scaled - mean_one - unit * mean_two)
    return (
        grad_flow,
        jnp.sum(grad * unit, axis=0, keepdims=True),
        jnp.sum(grad, axis=0, keepdims=True),
    )


def set_bias(key_rows, query_row, bias):
    count = query_row.shape[1]
    for d in range(len(key_rows)):
        column = jnp.broadcast_to(key_rows[d], (128, count)).T
        column = jnp.concatenate([column] * (count // 128), axis=1)
        bias[d * count : (d + 1) * count, :] = jnp.where(column == query_row, 0.0, mask_fill)


def set_values(values, slots, first):
    turned = values.T
    count = values.shape[0]
    cols = slice(first, first + count)
    for head in range(HEADS):
        slots[head * SLOT : head * SLOT + HEAD, cols] = turned[head * HEAD : (head + 1) * HEAD, :]
        slots[head * SLOT + HEAD : (head + 1) * SLOT, cols] = jnp.ones((SLOT - HEAD, count), BF)


def finish_head(head, exp_scores, slots, mixed_out, inverse_out):
    summed = dot(slots[head * SLOT : (head + 1) * SLOT, :], exp_scores)
    inverse = 1.0 / summed[HEAD : HEAD + 1, :]
    mixed_out[head * HEAD : (head + 1) * HEAD, :] = low(summed[:HEAD, :] * inverse)
    inverse_out[head : head + 1, :] = inverse


def attend(query, keys, slots, bias, exps, exps_out, sem, mixed_out, inverse_out):
    count = query.shape[0]

    def scores_of(head):
        pair_keys = keys[:, head // 2 * PAIR : (head // 2 + 1) * PAIR]
        return dot_t(pair_keys, head_cols(query, head)) + bias[...]

    scores, before = scores_of(0), None
    for head in range(HEADS):
        after = scores_of(head + 1) if head + 1 < HEADS else None
        if head > 0:
            finish_head(head - 1, before, slots, mixed_out, inverse_out)
        top = jnp.max(scores, axis=0, keepdims=True)
        before = low(jnp.exp(scores - top))
        exps[head // 2, :, head % 2 * count : (head % 2 + 1) * count] = before
        if head % 2 == 1:
            pltpu.make_async_copy(
                exps.at[head // 2], exps_out.at[head // 2], sem.at[head // 2]
            ).start()
        scores = after
    finish_head(HEADS - 1, before, slots, mixed_out, inverse_out)
    for pair in range(HEADS // 2):
        pltpu.make_async_copy(exps.at[pair], exps_out.at[pair], sem.at[pair]).wait()


def fetch(exps_in, exps, sem, pair):
    return pltpu.make_async_copy(exps_in.at[pair], exps.at[pair], sem.at[pair])


def attend_back(
    query, keys_t, values, mixed_t, grad_t, grad, exps_in, exps, sem, query_t_out, kv_out
):
    count, feat = query.shape

    def head_dot(head):
        rows = slice(head * HEAD, (head + 1) * HEAD)
        both = grad_t[rows, :].astype(F32) * mixed_t[rows, :].astype(F32)
        return jnp.sum(both, axis=0, keepdims=True)

    def grad_probs(pair):
        heads = (2 * pair, 2 * pair + 1)
        both = jnp.concatenate([head_rows(grad_t, head) for head in heads], axis=1)
        return dot(values[:, pair * PAIR : (pair + 1) * PAIR], both)

    def pair_cols(block, pair):
        return jnp.concatenate([head_cols(block, 2 * pair), head_cols(block, 2 * pair + 1)], axis=0)

    row_dots = [head_dot(head) for head in range(HEADS)]
    grad_prob = grad_probs(0)
    for pair in range(HEADS // 2):
        after = grad_probs(pair + 1) if pair + 1 < HEADS // 2 else None
        fetch(exps_in, exps, sem, pair).wait()
        cols = slice(pair * PAIR, (pair + 1) * PAIR)
        exp_scores = exps[pair]
        row_dot = jnp.concatenate([row_dots[2 * pair], row_dots[2 * pair + 1]], axis=1)
        grad_scores = low(exp_scores.astype(F32) * (grad_prob - row_dot))
        kv_out[:, feat + pair * PAIR : feat + (pair + 1) * PAIR] = low(
            dot(exp_scores, pair_cols(grad, pair))
        )
        kv_out[:, cols] = low(dot(grad_scores, pair_cols(query, pair)))
        for head in (2 * pair, 2 * pair + 1):
            rows = slice(head * HEAD, (head + 1) * HEAD)
            mine = grad_scores[:, head % 2 * count : (head % 2 + 1) * count]
            query_t_out[rows, :] = low(dot(keys_t[rows, :], mine) * HEAD ** (-0.5))
        grad_prob = after


def over_sums(grad_t, inverse):
    return low(
        jnp.concatenate(
            [
                grad_t[head * HEAD : (head + 1) * HEAD, :] * inverse[head : head + 1, :]
                for head in range(HEADS)
            ],
            axis=0,
        )
    )


def send_out(pairs, sem):
    copies = [pltpu.make_async_copy(a, b, sem.at[i]) for i, (a, b) in enumerate(pairs)]
    for copy in copies:
        copy.start()
    return copies


def self_attend_body(n_blocks, n_parts, pos, *refs):
    blocks, refs = refs[:n_blocks], refs[n_blocks:]
    near, far, refs = refs[:n_parts], refs[n_parts : 2 * n_parts], refs[2 * n_parts :]
    (ids, q_out, v_out, kt_out, mixed_out, inverse_out, kid_out, exps_out) = refs[:8]
    weight, keys, slots, bias, exps, sem, values, keys_t, out_sem = refs[8:]
    count, feat = q_out.shape
    in_order(pos, (near, far), weight, 0)
    query = low(dot(blocks[0][:count, :], weight[:, :feat]))
    query = query * BF(HEAD ** (-0.5))
    q_out[...] = query
    for d, block in enumerate(blocks):
        rows = slice(d * count, (d + 1) * count)
        key = low(dot(block[:count, :], weight[:, feat : 2 * feat]))
        value = low(dot(block[:count, :], weight[:, 2 * feat :]))
        keys[rows, :] = key
        keys_t[:, rows] = key.T
        values[rows, :] = value
        set_values(value, slots, d * count)
        kid_out[d : d + 1, :] = block[count : count + 1, :count].astype(F32)
    copies = send_out(((keys_t, kt_out), (values, v_out)), out_sem)
    set_bias([kid_out[d : d + 1, :] for d in range(n_blocks)], ids[...].astype(F32), bias)
    attend(query, keys, slots, bias, exps, exps_out, sem, mixed_out, inverse_out)
    for copy in copies:
        copy.wait()


def attend_scratch(keys, feat, count):
    return [
        VM((keys, feat), BF),
        VM((HEADS * SLOT, keys), BF),
        VM((keys, count), F32),
        VM((HEADS // 2, keys, 2 * count), BF),
        pltpu.SemaphoreType.DMA((HEADS // 2,)),
        VM((keys, feat), BF),
        VM((feat, keys), BF),
        pltpu.SemaphoreType.DMA((2,)),
    ]


SMALL = ("stack", "join", "add_far", "add_mid", "add_near", "add_one", "add_line")
ROOM = {"self_attend": 22, "cross_attend": 24, "feed": 28, "cross_back": 28, "self_back": 22}


def kernel_call(
    body, outs, out_specs, in_specs, scratch, name, flops, size, after=(), held_in=(), held_out=(), far_in=(), far_out=()
):
    n_in = len(in_specs)
    small = name in SMALL

    def space(place, held, far):
        return pltpu.VMEM if small and place not in far or place in held else pltpu.HBM

    def run(*refs):
        body(*refs[:n_in], *refs[n_in + len(after) :])

    single = not isinstance(outs, (tuple, list))
    outs = tuple(
        space(place, held_out, far_out)(out.shape, out.dtype)
        for place, out in enumerate([outs] if single else outs)
    )
    outs = outs[0] if single else outs
    call = pl.pallas_call(
        run if after else body,
        out_shape=outs,
        in_specs=in_specs + [APART] * len(after),
        out_specs=out_specs,
        scratch_shapes=scratch,
        compiler_params=pltpu.CompilerParams(vmem_limit_bytes=(8 if small else ROOM.get(name, 12)) * 2**20),
        cost_estimate=pl.CostEstimate(flops=flops, bytes_accessed=size, transcendentals=0),
        name=name,
    )

    def go(*operands):
        operands = [
            x
            if spec is SCALARS
            else pltpu.with_memory_space_constraint(x, space(place, held_in, far_in))
            for place, (x, spec) in enumerate(zip(operands, in_specs, strict=True))
        ]
        return call(*operands, *after)

    return go


def self_attend(pos, blocks, ids, near, far, count, feat, after):
    keys = count * len(blocks)
    return kernel_call(
        functools.partial(self_attend_body, len(blocks), len(near)),
        (
            shape(count, feat),
            shape(keys, feat),
            shape(feat, keys),
            shape(feat, count),
            shape(HEADS, count, dtype=F32),
            shape(len(blocks), count, dtype=F32),
            shape(HEADS // 2, keys, 2 * count),
        ),
        [WHOLE] + [APART] * 2 + [WHOLE] * 3 + [APART],
        [SCALARS] + [WHOLE] * (len(blocks) + 2 * len(near) + 1),
        [VM((feat, 3 * feat), BF)] + attend_scratch(keys, feat, count),
        "self_attend",
        12 * 10**9,
        20 * 10**6,
        after,
    )(pos, *blocks, *near, *far, ids)


def cross_attend_body(n_blocks, n_parts, pos, *refs):
    blocks, refs = refs[:n_blocks], refs[n_blocks:]
    near, far, refs = refs[:n_parts], refs[n_parts : 2 * n_parts], refs[2 * n_parts :]
    (ids, kid, mixed, mixed_one) = refs[:4]
    (vec_out, unit_out, inv_out, q_out, v_out, kt_out, mixed_out, inverse_out) = refs[4:12]
    (unit_two_out, inv_two_out, exps_out) = refs[12:15]
    weight, keys, slots, bias, exps, sem, values, keys_t, out_sem = refs[15:]
    count, feat = q_out.shape
    in_order(pos, (near, far), weight, 0)
    vec_out[...] = weight[:, 5 * feat :].astype(F32).T[:8, :]
    flow = mixed[:count, :].astype(F32) + dot(mixed_one[...].T, weight[:, :feat])
    unit, inverse = normalise(flow)
    unit_out[...] = unit
    inv_out[...] = jnp.broadcast_to(inverse, inv_out.shape)
    normed = unit * vec_out[0:1, :] + vec_out[1:2, :]
    query = low(dot(low(normed), weight[:, feat : 2 * feat])) * BF(HEAD ** (-0.5))
    q_out[...] = query
    for d, block in enumerate(blocks):
        rows = slice(d * count, (d + 1) * count)
        key = low(dot(block[...], weight[:, 2 * feat : 3 * feat]))
        value = low(dot(block[...], weight[:, 3 * feat : 4 * feat]))
        keys[rows, :] = key
        keys_t[:, rows] = key.T
        values[rows, :] = value
        set_values(value, slots, d * count)
    copies = send_out(((keys_t, kt_out), (values, v_out)), out_sem)
    set_bias([kid[d : d + 1, :] for d in range(n_blocks)], ids[...].astype(F32), bias)
    attend(query, keys, slots, bias, exps, exps_out, sem, mixed_out, inverse_out)
    flow = unit_out[...] * vec_out[0:1, :] + vec_out[1:2, :]
    flow = flow + dot(mixed_out[...].T, weight[:, 4 * feat : 5 * feat])
    unit, inverse = normalise(flow)
    unit_two_out[...] = unit
    inv_two_out[...] = jnp.broadcast_to(inverse, inv_two_out.shape)
    for copy in copies:
        copy.wait()


def cross_attend(pos, blocks, ids, kid, mixed, mixed_one, near, far, after):
    count, feat = blocks[0].shape
    keys = count * len(blocks)
    return kernel_call(
        functools.partial(cross_attend_body, len(blocks), len(near)),
        (
            shape(8, feat, dtype=F32),
            shape(count, feat, dtype=F32),
            shape(count, 128, dtype=F32),
            shape(count, feat),
            shape(keys, feat),
            shape(feat, keys),
            shape(feat, count),
            shape(HEADS, count, dtype=F32),
            shape(count, feat, dtype=F32),
            shape(count, 128, dtype=F32),
            shape(HEADS // 2, keys, 2 * count),
        ),
        [WHOLE] * 4 + [APART] * 2 + [WHOLE] * 4 + [APART],
        [SCALARS] + [WHOLE] * (len(blocks) + 2 * len(near) + 4),
        [VM((feat, 5 * feat + 128), BF)] + attend_scratch(keys, feat, count),
        "cross_attend",
        14 * 10**9,
        20 * 10**6,
        after,
        held_out=(8, 9),
    )(pos, *blocks, *near, *far, ids, kid, mixed, mixed_one)


def feed_body(pos, unit_in, inv_in, vec, grad_in, pad, three, *refs):
    (layer_out, flow_out, vec_grad_out, keep_out, away_out) = refs[:5]
    w_out, g_in, g_out = refs[5:]
    feat, wide = g_in.shape
    sub = wide // feat
    w_in = three.at[:, :wide]
    rows = keep_out.shape[2]
    for first in range(0, feat, rows):
        for r in range(sub):
            w_out[first * sub + r * rows : first * sub + (r + 1) * rows, :] = three[
                first : first + rows, wide + r * feat : wide + (r + 1) * feat
            ]
    real = jnp.broadcast_to(pad[...].astype(F32), (128, pad.shape[1])).T[:, :1]
    unit_two = unit_in[...]
    normed_two = unit_two * vec[2:3, :] + vec[3:4, :]
    normed_low = low(normed_two)
    inner = dot(normed_low, w_in[...])
    cube = 0.044715 * inner * inner
    bend = jnp.tanh((2.0 / jnp.pi) ** 0.5 * inner * (1.0 + cube))
    active = low(0.5 * inner * (1.0 + bend))
    slope = 0.5 * (1.0 + bend) + 0.5 * inner * (1.0 - bend * bend) * (2.0 / jnp.pi) ** 0.5 * (
        1.0 + 3.0 * cube
    )
    flow = normed_two + dot(active, w_out[...])
    unit, inverse = normalise(flow)
    layer_out[...] = low((unit * vec[4:5, :] + vec[5:6, :]) * real)
    top = grad_in[...].astype(F32) * real
    grad_flow, grad_gain, grad_shift = normalise_back(top, unit, inverse, vec[4:5, :])
    vec_grad_out[...] = jnp.zeros_like(vec_grad_out)
    vec_grad_out[4:5, :] = grad_gain
    vec_grad_out[5:6, :] = grad_shift
    grad_y = low(grad_flow)
    grad_inner = low(slope * dot_t(grad_y, w_out[...]))
    grad_normed = grad_flow + dot_t(grad_inner, w_in[...])
    grad_flow, grad_gain, grad_shift = normalise_back(
        grad_normed, unit_two, inv_in[:, :1], vec[2:3, :]
    )
    vec_grad_out[2:3, :] = grad_gain
    vec_grad_out[3:4, :] = grad_shift
    flow_out[...] = grad_flow
    g_out[...] = low(dot(active.T, grad_y))
    by_distance(pos, g_out, (keep_out, away_out), wide, sub)
    g_in[...] = low(dot(normed_low.T, grad_inner))
    by_distance(pos, g_in, (keep_out, away_out), 0)


def feed(pos, unit, inverse, vec, out_grad, pad, three, whole):
    count, feat = unit.shape
    wide = three.shape[1] // 2
    return kernel_call(
        feed_body,
        (
            shape(count, feat),
            shape(count, feat, dtype=F32),
            shape(8, feat, dtype=F32),
            shape(*whole),
            shape(*whole),
        ),
        [WHOLE] * 5,
        [SCALARS] + [WHOLE] * 6,
        [VM((wide, feat), BF), VM((feat, wide), BF), VM((wide, feat), BF)],
        "feed",
        6 * 10**9,
        20 * 10**6,
        held_in=(1, 2),
        held_out=(1, 2, 3, 4),
    )(pos, unit, inverse, vec, out_grad, pad, three)


def cross_back_body(n_blocks, n_parts, pos, line, *refs):
    blocks, refs = refs[:n_blocks], refs[n_blocks:]
    near, far, refs = refs[:n_parts], refs[n_parts : 2 * n_parts], refs[2 * n_parts :]
    (flow_in, mixed_two, inverse_two, query, keys_t, values, exps_in) = refs[:7]
    (unit_in, inv_in, vec, vec_grad, mixed_one, inverse_one) = refs[7:13]
    refs = refs[13:]
    flow_out, one_t_out, keep_out, away_out, parts_out = refs[:5]
    weight, grads, kv, query_t, exps, sem = refs[5:]
    count, feat = query.shape
    for pair in range(HEADS // 2):
        fetch(exps_in, exps, sem, pair).start()
    in_order(pos, (near, far), weight, 0)
    grad_y = low(flow_in[...])
    grad_t = over_sums(dot_t(weight[:, 4 * feat : 5 * feat], grad_y), inverse_two)
    grads[:, 4 * feat : 5 * feat] = low(dot(mixed_two[...], grad_y))
    attend_back(
        query, keys_t, values, mixed_two, grad_t, grad_t.T, exps_in, exps, sem, query_t, kv
    )
    grad_query = query_t[...].T
    grad_normed = flow_in[...] + dot_t(grad_query, weight[:, feat : 2 * feat])
    unit = unit_in[...]
    grad_flow, grad_gain, grad_shift = normalise_back(grad_normed, unit, inv_in[:, :1], vec[0:1, :])
    flow_out[...] = grad_flow
    grad_y = low(grad_flow)
    one_t_out[...] = over_sums(dot_t(weight[:, :feat], grad_y), inverse_one)
    grads[:, :feat] = low(dot(mixed_one[...], grad_y))
    normed = low(unit * vec[0:1, :] + vec[1:2, :])
    grads[:, feat : 2 * feat] = low(dot(normed.T, grad_query))
    turned = jnp.concatenate([block[...].T for block in blocks], axis=1)
    grads[:, 2 * feat : 4 * feat] = low(dot(turned, kv[...]))
    rows = jnp.concatenate(
        [grad_gain, grad_shift, vec_grad[2:8, :], jnp.zeros((120, feat), F32)], axis=0
    )
    grads[:, 5 * feat :] = low(rows.T)
    by_distance(pos, grads, (keep_out, away_out), 0)
    for d in range(n_blocks):
        part = dot_t(kv[d * count : (d + 1) * count, :], weight[:, 2 * feat : 4 * feat])
        place = pl.multiple_of((line[0] ^ d) * count, count)
        parts_out[pl.ds(place, count), :] = low(part)


def back_scratch(keys, feat, count):
    return [
        VM((keys, 2 * feat), BF),
        VM((feat, count), BF),
        VM((HEADS // 2, keys, 2 * count), BF),
        pltpu.SemaphoreType.DMA((HEADS // 2,)),
    ]


def cross_back(pos, line, blocks, near, far, after, *args):
    count, feat = blocks[0].shape
    keys = count * len(blocks)
    whole = near[0].shape if len(near) == 1 else (len(near),) + near[0].shape
    return kernel_call(
        functools.partial(cross_back_body, len(blocks), len(near)),
        (
            shape(count, feat, dtype=F32),
            shape(feat, count),
            shape(*whole),
            shape(*whole),
        )
        + (shape(keys, feat),),
        [WHOLE] * 5,
        [SCALARS] * 2 + [WHOLE] * (len(blocks) + 2 * len(near) + 6) + [APART] + [WHOLE] * 6,
        [VM((feat, 5 * feat + 128), BF)] * 2 + back_scratch(keys, feat, count),
        "cross_back",
        15 * 10**9,
        20 * 10**6,
        after,
        held_in=(2 + len(blocks) + 2 * len(near),),
        held_out=range(4),
    )(pos, line, *blocks, *near, *far, *args)


def self_back_body(
    n_blocks, n_parts, pos, line, flow_in, one_t, mixed_one, query, keys_t, values, exps_in, *refs
):
    near, far, refs = refs[0], refs[1], refs[2:]
    (own_out, query_t_out, kv_out, parts_out) = refs[:4]
    weight, exps, sem, held, part_sem = refs[4:]
    count, feat = query.shape
    for pair in range(HEADS // 2):
        fetch(exps_in, exps, sem, pair).start()
    copies = fetch_parts(near, far, held, part_sem)
    grad_t = one_t[...]
    attend_back(
        query,
        keys_t,
        values,
        mixed_one,
        grad_t,
        grad_t.T,
        exps_in,
        exps,
        sem,
        query_t_out,
        kv_out,
    )
    for copy in copies:
        copy.wait()
    in_order(pos, ([held.at[0]], [held.at[1]]), weight, 0)
    for d in range(n_blocks):
        part = dot_t(kv_out[d * count : (d + 1) * count, :], weight[:, feat:])
        place = pl.multiple_of((line[0] ^ d) * count, count)
        parts_out[pl.ds(place, count), :] = low(part)
    own_out[...] = flow_in[...] + dot_t(query_t_out[...].T, weight[:, :feat])


def self_back(pos, line, n_blocks, near, far, after, *args):
    count, feat = args[3].shape
    keys = count * n_blocks
    return kernel_call(
        functools.partial(self_back_body, n_blocks, len(near)),
        (
            shape(count, feat, dtype=F32),
            shape(feat, count),
            shape(keys, 2 * feat),
            shape(keys, feat),
        ),
        [WHOLE] * 4,
        [SCALARS] * 2 + [WHOLE] * 6 + [APART] * 3,
        [VM((feat, 3 * feat), BF)]
        + back_scratch(keys, feat, count)[2:]
        + [VM((2,) + near[0].shape, BF), pltpu.SemaphoreType.DMA((2,))],
        "self_back",
        12 * 10**9,
        20 * 10**6,
        after,
        held_in=(2, 3),
        held_out=(1, 2),
    )(pos, line, *args, *near, *far)


def self_grads_body(n_blocks, pos, *refs):
    blocks = refs[:n_blocks]
    query_t, kv, keep_out, away_out, grads = refs[n_blocks:]
    feat, count = query_t.shape
    turned = jnp.concatenate([block[:count, :].T for block in blocks], axis=1)
    grads[:, :feat] = low(dot_t(turned[:, :count], query_t[...]))
    grads[:, feat:] = low(dot(turned, kv[...]))
    by_distance(pos, grads, (keep_out, away_out), 0)


def self_grads(pos, blocks, query_t, kv, part_shape, after):
    feat = query_t.shape[0]
    return kernel_call(
        functools.partial(self_grads_body, len(blocks)),
        (shape(*part_shape), shape(*part_shape)),
        [WHOLE] * 2,
        [SCALARS] + [WHOLE] * (len(blocks) + 2),
        [VM((feat, 3 * feat), BF)],
        "self_grads",
        5 * 10**9,
        8 * 10**6,
        after,
        held_in=(1 + len(blocks), 2 + len(blocks)),
        held_out=(0, 1),
    )(pos, *blocks, query_t, kv)


def pack_body(sub, source, target, glance, ids, pad, encoder, *refs):
    refs, encoder_out = (*refs[:-2], refs[-1]), refs[-2]
    encoder_out[...] = encoder[...]
    weights, vectors, refs = refs[:8], refs[8:14], refs[14:]
    inner, outer, three, early, mixed, lines = refs
    rows, feat = weights[0].shape
    count = glance.shape[1]
    wide = inner.shape[1]
    three[:, :wide] = inner[...]
    for r in range(sub):
        three[:, wide + r * feat : wide + (r + 1) * feat] = outer[r * rows : (r + 1) * rows, :]
    for place, weight in enumerate(weights):
        early[:, place * feat : (place + 1) * feat] = weight[...]
    lines[...] = jnp.zeros_like(lines)
    for place, vector in enumerate(vectors):
        lines[place : place + 1, :rows] = vector[...].astype(F32)
    early[:, 8 * feat :] = low(lines[...].T)[:rows, :]
    taken = jnp.broadcast_to(glance[...].astype(F32), (128, count)).T[:, :1]
    mixed[:count, :] = jnp.where(taken > 0.5, target[0], source[0])
    key_ids = jnp.where(pad[...] == 1, ids[...], -1).astype(F32)
    key_ids = jnp.concatenate([key_ids, jnp.zeros((1, feat - count), F32)], axis=1)
    mixed[count:, :] = low(jnp.broadcast_to(key_ids, (16, feat)))


def join_body(n, *refs):
    for i in range(n):
        refs[n][i] = refs[i][...]


def join(parts, *after):
    return kernel_call(
        functools.partial(join_body, len(parts)),
        shape(len(parts), *parts[0].shape),
        WHOLE,
        [WHOLE] * len(parts),
        [],
        "join",
        10**9,
        2 * 10**6,
        after,
    )(*parts)


def stack_body(n, cuts, *refs):
    parts, outs = refs[:n], refs[n:]
    for out, (first, last) in zip(outs, cuts, strict=True):
        for i in range(n):
            out[i] = parts[i][:, first:last]


def stack(parts, cuts, *after):
    rows = parts[0].shape[0]
    return kernel_call(
        functools.partial(stack_body, len(parts), cuts),
        tuple(shape(len(parts), rows, last - first) for first, last in cuts),
        [WHOLE] * len(cuts),
        [WHOLE] * len(parts),
        [],
        "stack",
        2 * 10**10,
        2 * 10**6,
        after,
    )(*parts)


def hold_body(*refs):
    pass


def hold(block, *after, space=None):
    out = shape(*block.shape, dtype=block.dtype)
    if space is not None:
        block = pltpu.with_memory_space_constraint(block, space)
        out = space(block.shape, block.dtype)
    return pl.pallas_call(
        hold_body,
        out_shape=out,
        in_specs=[APART] * (1 + len(after)),
        out_specs=APART,
        input_output_aliases={0: 0},
        name="hold",
    )(block, *after)


def swap(block, axis_name, size, bits):
    return lax.ppermute(block, axis_name, [(i, i ^ bits) for i in range(size)])


def stages(size):
    bits = size.bit_length() - 1
    return [2] * (bits // 2) + [1] * (bits % 2)


def spread(block, axis_name, size, unit, width):
    return [block] + [swap(block, axis_name, size, unit * far) for far in range(1, 1 << width)]


def spread_line(block, axis_name, size, unit, width):
    if width < 2:
        return spread(block, axis_name, size, unit, width)
    far = swap(block, axis_name, size, 2 * unit)
    return [block, swap(block, axis_name, size, unit), far, swap(far, axis_name, size, unit)]


def over_line(block, seq, way):
    blocks = [block]
    unit = 1
    for width in stages(seq):
        got = [way(b, "seq", seq, unit, width) for b in blocks]
        blocks = [g[far] for far in range(1 << width) for g in got]
        unit <<= width
    return blocks


def add_far_body(cut, keep, away, x_send, y_send, x_rest, y_rest):
    for e in range(4):
        both = low(keep[e].astype(F32) + away[e].astype(F32))
        (x_send if e % 2 == 1 else x_rest)[e // 2] = both[:, :, :cut]
        (y_send if e >= 2 else y_rest)[e % 2] = both[:, :, cut:]


def add_one_body(keep, away, *outs):
    for e in range(4):
        outs[e][...] = low(keep[e].astype(F32) + away[e].astype(F32))


def add_line_body(own, first, second, third, *outs):
    for d in range(4):
        total = own[d].astype(F32) + first[d].astype(F32)
        outs[d][...] = low(total + second[d].astype(F32) + third[d].astype(F32))


def add_mid_body(x_rest, x_got, y_rest, y_got, y_send, x_send, x_own, y_own):
    x_own[...] = x_rest[0].astype(F32) + x_got[0].astype(F32)
    y_send[...] = low(x_rest[1].astype(F32) + x_got[1].astype(F32))
    y_own[...] = y_rest[0].astype(F32) + y_got[0].astype(F32)
    x_send[...] = low(y_rest[1].astype(F32) + y_got[1].astype(F32))


def add_near_body(cut, x_own, x_got, y_own, y_got, own, odd, even):
    for d in range(4):
        left = x_own[d] + x_got[d].astype(F32)
        right = y_own[d] + y_got[d].astype(F32)
        if d == 0:
            own[:, :cut] = left
            own[:, cut:] = right
        elif d == 2:
            even[:, :cut] = low(left)
            even[:, cut:] = low(right)
        else:
            odd[d // 2, :, :cut] = low(left)
            odd[d // 2, :, cut:] = low(right)


def add_call(body, outs, operands, after, name, far_in=(), far_out=()):
    return kernel_call(
        body,
        outs,
        [WHOLE] * len(outs),
        [WHOLE] * len(operands),
        [],
        name,
        10**9,
        4 * 10**6,
        after,
        far_in=far_in,
        far_out=far_out,
    )(*operands)


def far_step(keep, away, after, fsdp):
    cols = keep.shape[3]
    cut = cols // 256 * 128
    dims = keep.shape[1:3]
    outs = [shape(2, *dims, width) for width in (cut, cols - cut) * 2]
    x_send, y_send, x_rest, y_rest = add_call(
        functools.partial(add_far_body, cut), outs, (keep, away), after, "add_far"
    )
    return (x_send, swap(x_send, "fsdp", fsdp, 2), swap(y_send, "fsdp", fsdp, 4), x_rest, y_rest)


def mid_step(far, after, fsdp):
    _, x_got, y_got, x_rest, y_rest = far
    x_dims, y_dims = x_rest.shape[1:], y_rest.shape[1:]
    outs = [shape(*x_dims), shape(*y_dims), shape(*x_dims, dtype=F32), shape(*y_dims, dtype=F32)]
    y_send, x_send, x_own, y_own = add_call(
        add_mid_body, outs, (x_rest, x_got, y_rest, y_got), after, "add_mid", (), (2, 3)
    )
    return (y_send, swap(y_send, "fsdp", fsdp, 4), swap(x_send, "fsdp", fsdp, 2), x_own, y_own)


def near_step(mid, after):
    _, x_got, y_got, x_own, y_own = mid
    cut = x_own.shape[2]
    rows, cols = x_own.shape[1], cut + y_own.shape[2]
    outs = [shape(rows, cols, dtype=F32), shape(2, rows, cols), shape(rows, cols)]
    return add_call(
        functools.partial(add_near_body, cut), outs, (x_own, x_got, y_own, y_got), after, "add_near", (0, 2)
    )


def finish_line(near, seq, *after):
    own, odd, even = near
    got = swap(odd, "seq", seq, 1)
    if after:
        got = hold(got, *after, space=pltpu.VMEM)
    even = low(even.astype(F32) + got[1].astype(F32))
    return own.astype(F32) + got[0].astype(F32), swap(even, "seq", seq, 2)


def bit_of(axis_name, bit):
    return (lax.axis_index(axis_name) & bit) != 0


def double(block, axis_name, size, bit, place):
    other = swap(block, axis_name, size, bit)
    high = bit_of(axis_name, bit)
    return jnp.where(
        high, jnp.stack([other, block], axis=place), jnp.stack([block, other], axis=place)
    )


def bits_below(size):
    return [1 << k for k in range(size.bit_length() - 1)]


def gather_blocks(shard, fsdp, seq, turned):
    block = shard
    for bit in bits_below(seq):
        block = double(block, "seq", seq, bit, 1)
    upper = bits_below(fsdp)[1:]
    done = []
    for bit in upper[::-1] if turned else upper:
        place = 1 + sum(b > bit for b in done)
        block = double(block, "fsdp", fsdp, bit, place)
        done.append(bit)
    if fsdp > 1:
        block = double(block, "fsdp", fsdp, 1, 1 + len(upper))
    return block.reshape(shard.shape[0], fsdp * seq * shard.shape[1], shard.shape[2])


def halve(block, axis_name, size, bit, place):
    high = bit_of(axis_name, bit).astype(jnp.int32)
    away = lax.dynamic_index_in_dim(block, 1 - high, place, keepdims=False)
    kept = lax.dynamic_index_in_dim(block, high, place, keepdims=False)
    other = swap(away, axis_name, size, bit)
    return (kept.astype(jnp.float32) + other.astype(jnp.float32)).astype(jnp.bfloat16)


def scatter_blocks(whole, fsdp, seq, turned):
    w, depth, cols = whole.shape
    n_up = len(bits_below(fsdp)) - 1
    n_seq = len(bits_below(seq))
    rows = depth // (fsdp * seq)
    block = whole.reshape((w,) + (2,) * (n_up + 1 + n_seq) + (rows, cols))
    block = halve(block, "fsdp", fsdp, 1, 1 + n_up)
    upper = bits_below(fsdp)[1:]
    left = list(upper)
    for bit in upper[::-1] if turned else upper:
        place = 1 + sum(b > bit for b in left)
        block = halve(block, "fsdp", fsdp, bit, place)
        left.remove(bit)
    for bit in bits_below(seq)[::-1]:
        block = halve(block, "seq", seq, bit, 1)
    return block.astype(jnp.float32)


def whole_parts(shard, fsdp, seq):
    whole = gather_blocks(shard[None], fsdp, seq, False)[0]
    parts = whole.reshape(4, 2, 4, -1, whole.shape[1])
    return parts[:, 0], parts[:, 1]


def whole_sum(keep, away, fsdp, seq):
    whole = jnp.stack([keep, away], axis=1).reshape(-1, keep.shape[3])
    return scatter_blocks(whole[None], fsdp, seq, False)[0]


def regroup(three, rows, to, wide):
    feat = three.shape[0]
    sub = wide // feat
    outer = three[:, wide:].reshape(-1, rows, sub, feat).transpose(0, 2, 1, 3)
    outer = outer.reshape(-1, sub, to, feat).transpose(0, 2, 1, 3)
    return jnp.concatenate([three[:, :wide], outer.reshape(feat, sub * feat)], axis=1)


def make(fsdp, seq):
    def on_device(
        source_copy,
        target_embed,
        glance_mask,
        segment_ids,
        pad_mask,
        encoder_out,
        out_grad,
        self_query,
        self_key,
        self_value,
        self_output,
        norm1_gain,
        norm1_shift,
        cross_query,
        cross_key,
        cross_value,
        cross_output,
        norm2_gain,
        norm2_shift,
        inner_weight,
        outer_weight,
        norm3_gain,
        norm3_shift,
    ):
        row_count, loc_count, feat = source_copy.shape
        count = row_count * loc_count
        chunk = self_query.shape[0]
        sub = outer_weight.shape[0] // chunk
        pos = jnp.stack([lax.axis_index("fsdp"), lax.axis_index("seq")]).astype(jnp.int32)
        ids = segment_ids.reshape(1, count)
        pad = pad_mask.reshape(1, count)
        encoder = encoder_out.reshape(count, feat)
        vectors = (norm1_gain, norm1_shift, norm2_gain, norm2_shift, norm3_gain, norm3_shift)
        vectors = [vector.reshape(1, chunk) for vector in vectors]
        wide = sub * feat
        three, early, mixed, encoder = kernel_call(
            functools.partial(pack_body, sub),
            (shape(chunk, 2 * wide), shape(chunk, 8 * feat + 128), shape(count + 16, feat), shape(count, feat)),
            [WHOLE] * 4,
            [WHOLE] * 22,
            [VM((128, 128), F32)],
            "pack",
            10**9,
            2 * 10**6,
        )(
            source_copy,
            target_embed,
            glance_mask.reshape(1, count),
            ids,
            pad,
            encoder,
            self_query,
            self_key,
            self_value,
            self_output,
            cross_query,
            cross_key,
            cross_value,
            cross_output,
            *vectors,
            inner_weight,
            outer_weight,
        )
        all_three = lax.all_gather(three, ("fsdp", "seq"), axis=0, tiled=True)
        home = pos
        near_rows = seq == 4 and fsdp == 8 and chunk % 16 == 0
        if near_rows:
            early_blocks = over_line(early, seq, spread)
            mixed_far = swap(mixed, "seq", seq, 2)
            mixed_near = swap(mixed, "seq", seq, 1)
            line_one, line_two = stack(
                early_blocks, ((0, 3 * feat), (3 * feat, 8 * feat + 128)), mixed_near
            )
            plane_one = spread(line_one, "fsdp", fsdp, 2, 2)
            near_one = join(plane_one, mixed_far)
            far_one = swap(near_one, "fsdp", fsdp, 1)
            mixed_far = hold(mixed_far, near_one, space=pltpu.VMEM)
            mixed_blocks = [mixed, mixed_near, mixed_far, swap(mixed_far, "seq", seq, 1)]
            plane_two = spread(line_two, "fsdp", fsdp, 2, 2)
            encoder_late = hold(encoder, far_one)
            encoder_far = swap(encoder_late, "seq", seq, 2)
            encoder_near = swap(encoder_late, "seq", seq, 1)
        else:
            home = jnp.zeros_like(pos)
            near_one, far_one = whole_parts(early[:, : 3 * feat], fsdp, seq)
            near_two, far_two = whole_parts(early[:, 3 * feat :], fsdp, seq)
            all_three = regroup(all_three, chunk, near_one.shape[2], wide)
            mixed_blocks = over_line(mixed, seq, spread)
            encoder_blocks = over_line(encoder, seq, spread)

        q_one, v_one, kt_one, mixed_one, inverse_one, key_rows, exps_one = self_attend(
            home, mixed_blocks, ids, [near_one], [far_one], count, feat, ()
        )
        if near_rows:
            encoder_far = hold(encoder_far, mixed_one, space=pltpu.VMEM)
            got_two = [hold(part, encoder_far, space=pltpu.VMEM) for part in plane_two[1:]]
            encoder_near = hold(encoder_near, mixed_one, space=pltpu.VMEM)
            near_two = join([line_two, *got_two], encoder_near)
            far_two = swap(near_two, "fsdp", fsdp, 1)
            near_two, far_two = [near_two], [far_two]
            encoder_blocks = [encoder, encoder_near, encoder_far]
            encoder_blocks.append(swap(encoder_far, "seq", seq, 1))
        else:
            near_two, far_two = [near_two], [far_two]
        (
            vec,
            unit_one,
            inv_one,
            q_two,
            v_two,
            kt_two,
            mixed_two,
            inverse_two,
            unit_two,
            inv_two,
            exps_two,
        ) = cross_attend(
            home,
            encoder_blocks,
            ids,
            key_rows,
            mixed,
            mixed_one,
            near_two,
            far_two,
            (),
        )
        layer_out, flow_two, vec_grad, keep_three, away_three = feed(
            home,
            unit_two,
            inv_two,
            vec,
            out_grad.reshape(count, feat),
            pad,
            all_three,
            near_one.shape[:3] + (2 * wide,),
        )
        after_feed = ()
        if near_rows:
            away_three = swap(away_three, "fsdp", fsdp, 1)
            far_three = far_step(keep_three, away_three, (), fsdp)
            after_feed = (far_three[0],)
        flow_one, one_t, keep_two, away_two, encoder_parts = cross_back(
            home,
            pos[1:],
            encoder_blocks,
            near_two,
            far_two,
            after_feed,
            flow_two,
            mixed_two,
            inverse_two,
            q_two,
            kt_two,
            v_two,
            exps_two,
            unit_one,
            inv_one,
            vec,
            vec_grad,
            mixed_one,
            inverse_one,
        )
        if near_rows:
            mid_three = mid_step(far_three, (flow_one,), fsdp)
            away_two = swap(hold(away_two, mid_three[0], space=pltpu.VMEM), "fsdp", fsdp, 1)
        encoder_grad = lax.psum_scatter(
            encoder_parts, "seq", scatter_dimension=0, tiled=True
        ).astype(F32)
        after_back, after_grads = (), ()
        if near_rows:
            far_two = far_step(keep_two, away_two, (), fsdp)
            after_back = (far_two[0],)
        input_own, query_t, kv, input_parts = self_back(
            home,
            pos[1:],
            seq,
            [near_one],
            [far_one],
            after_back,
            flow_one,
            one_t,
            mixed_one,
            q_one,
            kt_one,
            v_one,
            exps_one,
        )
        if near_rows:
            near_three = near_step(mid_three, (query_t,))
            mid_two = mid_step(far_two, (query_t,), fsdp)
            after_grads = (near_three[0], mid_two[0])
        keep_one, away_one = self_grads(
            home, mixed_blocks, query_t, kv, near_one.shape, after_grads
        )
        if near_rows:
            away_one = swap(away_one, "fsdp", fsdp, 1)
            one_send = add_call(
                add_one_body,
                [shape(*keep_one.shape[1:])] * 4,
                (keep_one, away_one),
                (),
                "add_one",
            )
            got_two = [hold(got, one_send[0], space=pltpu.VMEM) for got in mid_two[1:3]]
            mid_two = (mid_two[0], *got_two, *mid_two[3:])
            near_two = near_step(mid_two, ())
            near_three = finish_line(near_three, seq, one_send[0])
            got_one = [swap(one_send[e], "fsdp", fsdp, 2 * e) for e in (1, 2, 3)]
            line_one = add_call(
                add_line_body,
                [shape(*keep_one.shape[2:])] * 4,
                (one_send[0], *got_one),
                (),
                "add_line",
            )
            got_line = [swap(line_one[d], "seq", seq, d) for d in (1, 2, 3)]
            grads_three = near_three[0] + hold(near_three[1], got_line[0]).astype(F32)
            near_two = finish_line(near_two, seq, line_one[0])
            grads_two = near_two[0] + near_two[1].astype(F32)
            grads_one = line_one[0].astype(F32)
            for block in got_line:
                grads_one = grads_one + block.astype(F32)
        else:
            grads_one = whole_sum(keep_one, away_one, fsdp, seq)
            grads_two = whole_sum(keep_two, away_two, fsdp, seq)
            grads_three = jnp.stack([keep_three, away_three], axis=1).reshape(feat, 2 * wide)
            grads_three = regroup(grads_three, near_one.shape[2], chunk, wide)
            grads_three = scatter_blocks(grads_three[None], fsdp, seq, False)[0]
        input_got = lax.psum_scatter(input_parts, "seq", scatter_dimension=0, tiled=True)
        input_grad = input_own + input_got.astype(F32)

        def stacked(flat_rows):
            return flat_rows.reshape(row_count, loc_count, feat)

        def cols(grads, place):
            return grads[:, place * feat : (place + 1) * feat]

        vec_out = grads_two[:, 5 * feat : 5 * feat + 6].T
        grad_outer = jnp.concatenate(
            [grads_three[:, wide + r * feat : wide + (r + 1) * feat] for r in range(sub)], axis=0
        )
        return (
            stacked(layer_out),
            stacked(input_grad),
            stacked(encoder_grad),
            cols(grads_one, 0),
            cols(grads_one, 1),
            cols(grads_one, 2),
            cols(grads_two, 0),
            vec_out[0],
            vec_out[1],
            cols(grads_two, 1),
            cols(grads_two, 2),
            cols(grads_two, 3),
            cols(grads_two, 4),
            vec_out[2],
            vec_out[3],
            grads_three[:, :wide],
            grad_outer,
            vec_out[4],
            vec_out[5],
        )

    return on_device


def solution(mesh):
    rows = P("fsdp", "seq", None)
    marks = P("fsdp", "seq")
    weight = P(("fsdp", "seq"), None)
    vector = P(("fsdp", "seq"))
    layer = (weight,) * 4 + (vector,) * 2
    return jax.shard_map(
        make(mesh.shape["fsdp"], mesh.shape["seq"]),
        mesh=mesh,
        in_specs=(rows, rows, marks, marks, marks, rows, rows)
        + layer
        + layer
        + (weight,) * 2
        + (vector,) * 2,
        out_specs=(rows,) * 3 + layer + layer + (weight,) * 2 + (vector,) * 2,
        check_vma=False,
    )
```

```python
import functools

import jax
import jax.numpy as jnp
from jax import lax
from jax.experimental import pallas as pl
from jax.experimental.pallas import tpu as pltpu
from jax.sharding import PartitionSpec as P

HEADS = 8
HEAD = 64
PAIR = 2 * HEAD
SLOT = HEAD + 16


norm_eps = 1e-05
mask_fill = -1e30

BF = jnp.bfloat16
F32 = jnp.float32
VM = pltpu.VMEM
WHOLE = pl.BlockSpec(memory_space=pltpu.VMEM)
SCALARS = pl.BlockSpec(memory_space=pltpu.SMEM)
APART = pl.BlockSpec(memory_space=pl.ANY)


def shape(*dims, dtype=BF):
    return jax.ShapeDtypeStruct(dims, dtype)


def low(values):
    return values.astype(BF)


def dot(left, right):
    return jnp.dot(left, right, preferred_element_type=F32)


def dot_t(left, right):
    return lax.dot_general(left, right, (((1,), (1,)), ((), ())), preferred_element_type=F32)


def head_cols(block, head):
    pair = block[:, head // 2 * PAIR : (head // 2 + 1) * PAIR]
    lane = lax.broadcasted_iota(jnp.int32, pair.shape, 1)
    return jnp.where((lane >= HEAD) == (head % 2 == 1), pair, jnp.zeros_like(pair))


def head_rows(block, head):
    mine = block[head * HEAD : (head + 1) * HEAD, :]
    rest = jnp.zeros_like(mine)
    return jnp.concatenate([mine, rest] if head % 2 == 0 else [rest, mine], axis=0)


def chunk_of(pos, seq, c, e, d):
    return (pos[0] ^ (2 * e + c)) * seq + (pos[1] ^ d)


def in_order(pos, parts, target, col, sub=1):
    width = target.shape[1]
    for c, sides in enumerate(parts):
        if len(sides) == 1:
            sides = [sides[0].at[e] for e in range(sides[0].shape[0])]
        for e, part in enumerate(sides):
            for d in range(part.shape[0]):
                rows = part.shape[1]
                first = chunk_of(pos, part.shape[0], c, e, d) * (rows * sub)
                for r in range(sub):
                    start = pl.multiple_of(first + r * rows, rows)
                    target[pl.ds(start, rows), :] = part[
                        d, :, col + r * width : col + (r + 1) * width
                    ]


def fetch_parts(near, far, held, sem):
    copies = [
        pltpu.make_async_copy(ref, held.at[side], sem.at[side])
        for side, ref in enumerate((near, far))
    ]
    for copy in copies:
        copy.start()
    return copies


def by_distance(pos, source, parts, col, sub=1):
    width = source.shape[1]
    for c, part in enumerate(parts):
        for e in range(part.shape[0]):
            for d in range(part.shape[1]):
                rows = part.shape[2]
                first = chunk_of(pos, part.shape[1], c, e, d) * (rows * sub)
                for r in range(sub):
                    start = pl.multiple_of(first + r * rows, rows)
                    part[e, d, :, col + r * width : col + (r + 1) * width] = source[
                        pl.ds(start, rows), :
                    ]


def normalise(flow):
    centre = jnp.mean(flow, axis=1, keepdims=True)
    centered = flow - centre
    spread = jnp.mean(centered * centered, axis=1, keepdims=True)
    inverse = lax.rsqrt(spread + norm_eps)
    return centered * inverse, inverse


def normalise_back(grad, unit, inverse, gain):
    scaled = grad * gain
    mean_one = jnp.mean(scaled, axis=1, keepdims=True)
    mean_two = jnp.mean(scaled * unit, axis=1, keepdims=True)
    grad_flow = inverse * (scaled - mean_one - unit * mean_two)
    return (
        grad_flow,
        jnp.sum(grad * unit, axis=0, keepdims=True),
        jnp.sum(grad, axis=0, keepdims=True),
    )


def set_bias(key_rows, query_row, bias):
    count = query_row.shape[1]
    for d in range(len(key_rows)):
        column = jnp.broadcast_to(key_rows[d], (128, count)).T
        column = jnp.concatenate([column] * (count // 128), axis=1)
        bias[d * count : (d + 1) * count, :] = jnp.where(column == query_row, 0.0, mask_fill)


def set_values(values, slots, first):
    turned = values.T
    count = values.shape[0]
    cols = slice(first, first + count)
    for head in range(HEADS):
        slots[head * SLOT : head * SLOT + HEAD, cols] = turned[head * HEAD : (head + 1) * HEAD, :]
        slots[head * SLOT + HEAD : (head + 1) * SLOT, cols] = jnp.ones((SLOT - HEAD, count), BF)


def finish_head(head, exp_scores, slots, mixed_out, inverse_out):
    summed = dot(slots[head * SLOT : (head + 1) * SLOT, :], exp_scores)
    inverse = 1.0 / summed[HEAD : HEAD + 1, :]
    mixed_out[head * HEAD : (head + 1) * HEAD, :] = low(summed[:HEAD, :] * inverse)
    inverse_out[head : head + 1, :] = inverse


def attend(query, keys, slots, bias, exps, exps_out, sem, mixed_out, inverse_out):
    count = query.shape[0]

    def scores_of(head):
        pair_keys = keys[:, head // 2 * PAIR : (head // 2 + 1) * PAIR]
        return dot_t(pair_keys, head_cols(query, head)) + bias[...]

    scores, before = scores_of(0), None
    for head in range(HEADS):
        after = scores_of(head + 1) if head + 1 < HEADS else None
        if head > 0:
            finish_head(head - 1, before, slots, mixed_out, inverse_out)
        top = jnp.max(scores, axis=0, keepdims=True)
        before = low(jnp.exp(scores - top))
        exps[head // 2, :, head % 2 * count : (head % 2 + 1) * count] = before
        if head % 2 == 1:
            pltpu.make_async_copy(
                exps.at[head // 2], exps_out.at[head // 2], sem.at[head // 2]
            ).start()
        scores = after
    finish_head(HEADS - 1, before, slots, mixed_out, inverse_out)
    for pair in range(HEADS // 2):
        pltpu.make_async_copy(exps.at[pair], exps_out.at[pair], sem.at[pair]).wait()


def fetch(exps_in, exps, sem, pair):
    return pltpu.make_async_copy(exps_in.at[pair], exps.at[pair], sem.at[pair])


def attend_back(
    query, keys_t, values, mixed_t, grad_t, grad, exps_in, exps, sem, query_t_out, kv_out
):
    count, feat = query.shape

    def head_dot(head):
        rows = slice(head * HEAD, (head + 1) * HEAD)
        both = grad_t[rows, :].astype(F32) * mixed_t[rows, :].astype(F32)
        return jnp.sum(both, axis=0, keepdims=True)

    def grad_probs(pair):
        heads = (2 * pair, 2 * pair + 1)
        both = jnp.concatenate([head_rows(grad_t, head) for head in heads], axis=1)
        return dot(values[:, pair * PAIR : (pair + 1) * PAIR], both)

    def pair_cols(block, pair):
        return jnp.concatenate([head_cols(block, 2 * pair), head_cols(block, 2 * pair + 1)], axis=0)

    row_dots = [head_dot(head) for head in range(HEADS)]
    grad_prob = grad_probs(0)
    for pair in range(HEADS // 2):
        after = grad_probs(pair + 1) if pair + 1 < HEADS // 2 else None
        fetch(exps_in, exps, sem, pair).wait()
        cols = slice(pair * PAIR, (pair + 1) * PAIR)
        exp_scores = exps[pair]
        row_dot = jnp.concatenate([row_dots[2 * pair], row_dots[2 * pair + 1]], axis=1)
        grad_scores = low(exp_scores.astype(F32) * (grad_prob - row_dot))
        kv_out[:, feat + pair * PAIR : feat + (pair + 1) * PAIR] = low(
            dot(exp_scores, pair_cols(grad, pair))
        )
        kv_out[:, cols] = low(dot(grad_scores, pair_cols(query, pair)))
        for head in (2 * pair, 2 * pair + 1):
            rows = slice(head * HEAD, (head + 1) * HEAD)
            mine = grad_scores[:, head % 2 * count : (head % 2 + 1) * count]
            query_t_out[rows, :] = low(dot(keys_t[rows, :], mine) * HEAD ** (-0.5))
        grad_prob = after


def over_sums(grad_t, inverse):
    return low(
        jnp.concatenate(
            [
                grad_t[head * HEAD : (head + 1) * HEAD, :] * inverse[head : head + 1, :]
                for head in range(HEADS)
            ],
            axis=0,
        )
    )


def send_out(pairs, sem):
    copies = [pltpu.make_async_copy(a, b, sem.at[i]) for i, (a, b) in enumerate(pairs)]
    for copy in copies:
        copy.start()
    return copies


def self_attend_body(n_blocks, n_parts, pos, *refs):
    blocks, refs = refs[:n_blocks], refs[n_blocks:]
    near, far, refs = refs[:n_parts], refs[n_parts : 2 * n_parts], refs[2 * n_parts :]
    (ids, q_out, v_out, kt_out, mixed_out, inverse_out, kid_out, exps_out) = refs[:8]
    weight, keys, slots, bias, exps, sem, values, keys_t, out_sem = refs[8:]
    count, feat = q_out.shape
    in_order(pos, (near, far), weight, 0)
    query = low(dot(blocks[0][:count, :], weight[:, :feat]))
    query = query * BF(HEAD ** (-0.5))
    q_out[...] = query
    for d, block in enumerate(blocks):
        rows = slice(d * count, (d + 1) * count)
        key = low(dot(block[:count, :], weight[:, feat : 2 * feat]))
        value = low(dot(block[:count, :], weight[:, 2 * feat :]))
        keys[rows, :] = key
        keys_t[:, rows] = key.T
        values[rows, :] = value
        set_values(value, slots, d * count)
        kid_out[d : d + 1, :] = block[count : count + 1, :count].astype(F32)
    copies = send_out(((keys_t, kt_out), (values, v_out)), out_sem)
    set_bias([kid_out[d : d + 1, :] for d in range(n_blocks)], ids[...].astype(F32), bias)
    attend(query, keys, slots, bias, exps, exps_out, sem, mixed_out, inverse_out)
    for copy in copies:
        copy.wait()


def attend_scratch(keys, feat, count):
    return [
        VM((keys, feat), BF),
        VM((HEADS * SLOT, keys), BF),
        VM((keys, count), F32),
        VM((HEADS // 2, keys, 2 * count), BF),
        pltpu.SemaphoreType.DMA((HEADS // 2,)),
        VM((keys, feat), BF),
        VM((feat, keys), BF),
        pltpu.SemaphoreType.DMA((3,)),
    ]


SMALL = ("stack", "join", "add_far", "add_mid", "add_near", "add_one", "add_line")
ROOM = {"self_attend": 22, "cross_attend": 24, "feed": 28, "cross_back": 28, "self_back": 22}


def kernel_call(
    body, outs, out_specs, in_specs, scratch, name, flops, size, after=(), held_in=(), held_out=(), far_in=(), far_out=()
):
    n_in = len(in_specs)
    small = name in SMALL

    def space(place, held, far):
        return pltpu.VMEM if small and place not in far or place in held else pltpu.HBM

    def run(*refs):
        body(*refs[:n_in], *refs[n_in + len(after) :])

    single = not isinstance(outs, (tuple, list))
    outs = tuple(
        space(place, held_out, far_out)(out.shape, out.dtype)
        for place, out in enumerate([outs] if single else outs)
    )
    outs = outs[0] if single else outs
    call = pl.pallas_call(
        run if after else body,
        out_shape=outs,
        in_specs=in_specs + [APART] * len(after),
        out_specs=out_specs,
        scratch_shapes=scratch,
        compiler_params=pltpu.CompilerParams(vmem_limit_bytes=(8 if small else ROOM.get(name, 12)) * 2**20),
        cost_estimate=pl.CostEstimate(flops=flops, bytes_accessed=size, transcendentals=0),
        name=name,
    )

    def go(*operands):
        operands = [
            x
            if spec is SCALARS
            else pltpu.with_memory_space_constraint(x, space(place, held_in, far_in))
            for place, (x, spec) in enumerate(zip(operands, in_specs, strict=True))
        ]
        return call(*operands, *after)

    return go


def self_attend(pos, blocks, ids, near, far, count, feat, after):
    keys = count * len(blocks)
    return kernel_call(
        functools.partial(self_attend_body, len(blocks), len(near)),
        (
            shape(count, feat),
            shape(keys, feat),
            shape(feat, keys),
            shape(feat, count),
            shape(HEADS, count, dtype=F32),
            shape(len(blocks), count, dtype=F32),
            shape(HEADS // 2, keys, 2 * count),
        ),
        [WHOLE] + [APART] * 2 + [WHOLE] * 3 + [APART],
        [SCALARS] + [WHOLE] * (len(blocks) + 2 * len(near) + 1),
        [VM((feat, 3 * feat), BF)] + attend_scratch(keys, feat, count),
        "self_attend",
        12 * 10**9,
        20 * 10**6,
        after,
    )(pos, *blocks, *near, *far, ids)


def cross_attend_body(n_blocks, n_parts, pos, *refs):
    blocks, refs = refs[:n_blocks], refs[n_blocks:]
    near, far, refs = refs[:n_parts], refs[n_parts : 2 * n_parts], refs[2 * n_parts :]
    (ids, kid, mixed, mixed_one, three) = refs[:5]
    (vec_out, unit_out, inv_out, q_out, v_out, kt_out, mixed_out, inverse_out) = refs[5:13]
    (unit_two_out, inv_two_out, exps_out, three_out) = refs[13:17]
    weight, keys, slots, bias, exps, sem, values, keys_t, out_sem = refs[17:]
    ahead = pltpu.make_async_copy(three, three_out, out_sem.at[2])
    ahead.start()
    count, feat = q_out.shape
    in_order(pos, (near, far), weight, 0)
    vec_out[...] = weight[:, 5 * feat :].astype(F32).T[:8, :]
    flow = mixed[:count, :].astype(F32) + dot(mixed_one[...].T, weight[:, :feat])
    unit, inverse = normalise(flow)
    unit_out[...] = unit
    inv_out[...] = jnp.broadcast_to(inverse, inv_out.shape)
    normed = unit * vec_out[0:1, :] + vec_out[1:2, :]
    query = low(dot(low(normed), weight[:, feat : 2 * feat])) * BF(HEAD ** (-0.5))
    q_out[...] = query
    for d, block in enumerate(blocks):
        rows = slice(d * count, (d + 1) * count)
        key = low(dot(block[...], weight[:, 2 * feat : 3 * feat]))
        value = low(dot(block[...], weight[:, 3 * feat : 4 * feat]))
        keys[rows, :] = key
        keys_t[:, rows] = key.T
        values[rows, :] = value
        set_values(value, slots, d * count)
    copies = send_out(((keys_t, kt_out), (values, v_out)), out_sem)
    set_bias([kid[d : d + 1, :] for d in range(n_blocks)], ids[...].astype(F32), bias)
    attend(query, keys, slots, bias, exps, exps_out, sem, mixed_out, inverse_out)
    flow = unit_out[...] * vec_out[0:1, :] + vec_out[1:2, :]
    flow = flow + dot(mixed_out[...].T, weight[:, 4 * feat : 5 * feat])
    unit, inverse = normalise(flow)
    unit_two_out[...] = unit
    inv_two_out[...] = jnp.broadcast_to(inverse, inv_two_out.shape)
    for copy in copies:
        copy.wait()
    ahead.wait()


def cross_attend(pos, blocks, ids, kid, mixed, mixed_one, three, near, far, after):
    count, feat = blocks[0].shape
    keys = count * len(blocks)
    return kernel_call(
        functools.partial(cross_attend_body, len(blocks), len(near)),
        (
            shape(8, feat, dtype=F32),
            shape(count, feat, dtype=F32),
            shape(count, 128, dtype=F32),
            shape(count, feat),
            shape(keys, feat),
            shape(feat, keys),
            shape(feat, count),
            shape(HEADS, count, dtype=F32),
            shape(count, feat, dtype=F32),
            shape(count, 128, dtype=F32),
            shape(HEADS // 2, keys, 2 * count),
            shape(*three.shape),
        ),
        [WHOLE] * 4 + [APART] * 2 + [WHOLE] * 4 + [APART, WHOLE],
        [SCALARS] + [WHOLE] * (len(blocks) + 2 * len(near) + 4) + [APART],
        [VM((feat, 5 * feat + 128), BF)] + attend_scratch(keys, feat, count),
        "cross_attend",
        14 * 10**9,
        20 * 10**6,
        after,
        held_out=(8, 9, 11),
    )(pos, *blocks, *near, *far, ids, kid, mixed, mixed_one, three)


def feed_body(pos, unit_in, inv_in, vec, grad_in, pad, three, *refs):
    (layer_out, flow_out, vec_grad_out, keep_out, away_out) = refs[:5]
    w_out, g_in, g_out = refs[5:]
    feat, wide = g_in.shape
    sub = wide // feat
    w_in = three.at[:, :wide]
    rows = keep_out.shape[2]
    for first in range(0, feat, rows):
        for r in range(sub):
            w_out[first * sub + r * rows : first * sub + (r + 1) * rows, :] = three[
                first : first + rows, wide + r * feat : wide + (r + 1) * feat
            ]
    real = jnp.broadcast_to(pad[...].astype(F32), (128, pad.shape[1])).T[:, :1]
    unit_two = unit_in[...]
    normed_two = unit_two * vec[2:3, :] + vec[3:4, :]
    normed_low = low(normed_two)
    inner = dot(normed_low, w_in[...])
    cube = 0.044715 * inner * inner
    bend = jnp.tanh((2.0 / jnp.pi) ** 0.5 * inner * (1.0 + cube))
    active = low(0.5 * inner * (1.0 + bend))
    slope = 0.5 * (1.0 + bend) + 0.5 * inner * (1.0 - bend * bend) * (2.0 / jnp.pi) ** 0.5 * (
        1.0 + 3.0 * cube
    )
    flow = normed_two + dot(active, w_out[...])
    unit, inverse = normalise(flow)
    layer_out[...] = low((unit * vec[4:5, :] + vec[5:6, :]) * real)
    top = grad_in[...].astype(F32) * real
    grad_flow, grad_gain, grad_shift = normalise_back(top, unit, inverse, vec[4:5, :])
    vec_grad_out[...] = jnp.zeros_like(vec_grad_out)
    vec_grad_out[4:5, :] = grad_gain
    vec_grad_out[5:6, :] = grad_shift
    grad_y = low(grad_flow)
    grad_inner = low(slope * dot_t(grad_y, w_out[...]))
    grad_normed = grad_flow + dot_t(grad_inner, w_in[...])
    grad_flow, grad_gain, grad_shift = normalise_back(
        grad_normed, unit_two, inv_in[:, :1], vec[2:3, :]
    )
    vec_grad_out[2:3, :] = grad_gain
    vec_grad_out[3:4, :] = grad_shift
    flow_out[...] = grad_flow
    g_out[...] = low(dot(active.T, grad_y))
    by_distance(pos, g_out, (keep_out, away_out), wide, sub)
    g_in[...] = low(dot(normed_low.T, grad_inner))
    by_distance(pos, g_in, (keep_out, away_out), 0)


def feed(pos, unit, inverse, vec, out_grad, pad, three, whole):
    count, feat = unit.shape
    wide = three.shape[1] // 2
    return kernel_call(
        feed_body,
        (
            shape(count, feat),
            shape(count, feat, dtype=F32),
            shape(8, feat, dtype=F32),
            shape(*whole),
            shape(*whole),
        ),
        [WHOLE] * 5,
        [SCALARS] + [WHOLE] * 6,
        [VM((wide, feat), BF), VM((feat, wide), BF), VM((wide, feat), BF)],
        "feed",
        6 * 10**9,
        20 * 10**6,
        held_in=(1, 2, 6),
        held_out=(1, 2, 3, 4),
    )(pos, unit, inverse, vec, out_grad, pad, three)


def cross_back_body(n_blocks, n_parts, pos, line, *refs):
    blocks, refs = refs[:n_blocks], refs[n_blocks:]
    near, far, refs = refs[:n_parts], refs[n_parts : 2 * n_parts], refs[2 * n_parts :]
    (flow_in, mixed_two, inverse_two, query, keys_t, values, exps_in) = refs[:7]
    (unit_in, inv_in, vec, vec_grad, mixed_one, inverse_one) = refs[7:13]
    refs = refs[13:]
    flow_out, one_t_out, keep_out, away_out, parts_out = refs[:5]
    weight, grads, kv, query_t, exps, sem, rows_held, unit_held, late_sem = refs[5:]
    count, feat = query.shape
    for pair in range(HEADS // 2):
        fetch(exps_in, exps, sem, pair).start()
    late = [(block, rows_held.at[d]) for d, block in enumerate(blocks)] + [(unit_in, unit_held)]
    late = send_out(late, late_sem)
    in_order(pos, (near, far), weight, 0)
    grad_y = low(flow_in[...])
    grad_t = over_sums(dot_t(weight[:, 4 * feat : 5 * feat], grad_y), inverse_two)
    grads[:, 4 * feat : 5 * feat] = low(dot(mixed_two[...], grad_y))
    attend_back(
        query, keys_t, values, mixed_two, grad_t, grad_t.T, exps_in, exps, sem, query_t, kv
    )
    grad_query = query_t[...].T
    grad_normed = flow_in[...] + dot_t(grad_query, weight[:, feat : 2 * feat])
    for copy in late:
        copy.wait()
    unit = unit_held[...]
    grad_flow, grad_gain, grad_shift = normalise_back(grad_normed, unit, inv_in[:, :1], vec[0:1, :])
    flow_out[...] = grad_flow
    grad_y = low(grad_flow)
    one_t_out[...] = over_sums(dot_t(weight[:, :feat], grad_y), inverse_one)
    grads[:, :feat] = low(dot(mixed_one[...], grad_y))
    normed = low(unit * vec[0:1, :] + vec[1:2, :])
    grads[:, feat : 2 * feat] = low(dot(normed.T, grad_query))
    turned = jnp.concatenate([rows_held[d].T for d in range(n_blocks)], axis=1)
    grads[:, 2 * feat : 4 * feat] = low(dot(turned, kv[...]))
    rows = jnp.concatenate(
        [grad_gain, grad_shift, vec_grad[2:8, :], jnp.zeros((120, feat), F32)], axis=0
    )
    grads[:, 5 * feat :] = low(rows.T)
    by_distance(pos, grads, (keep_out, away_out), 0)
    for d in range(n_blocks):
        part = dot_t(kv[d * count : (d + 1) * count, :], weight[:, 2 * feat : 4 * feat])
        place = pl.multiple_of((line[0] ^ d) * count, count)
        parts_out[pl.ds(place, count), :] = low(part)


def back_scratch(keys, feat, count):
    return [
        VM((keys, 2 * feat), BF),
        VM((feat, count), BF),
        VM((HEADS // 2, keys, 2 * count), BF),
        pltpu.SemaphoreType.DMA((HEADS // 2,)),
    ]


def cross_back(pos, line, blocks, near, far, after, *args):
    count, feat = blocks[0].shape
    keys = count * len(blocks)
    whole = near[0].shape if len(near) == 1 else (len(near),) + near[0].shape
    return kernel_call(
        functools.partial(cross_back_body, len(blocks), len(near)),
        (
            shape(count, feat, dtype=F32),
            shape(feat, count),
            shape(*whole),
            shape(*whole),
        )
        + (shape(keys, feat),),
        [WHOLE] * 5,
        [SCALARS] * 2
        + [APART] * len(blocks)
        + [WHOLE] * (2 * len(near) + 6)
        + [APART] * 2
        + [WHOLE] * 5,
        [VM((feat, 5 * feat + 128), BF)] * 2
        + back_scratch(keys, feat, count)
        + [
            VM((len(blocks), count, feat), BF),
            VM((count, feat), F32),
            pltpu.SemaphoreType.DMA((len(blocks) + 1,)),
        ],
        "cross_back",
        15 * 10**9,
        20 * 10**6,
        after,
        held_in=(2 + len(blocks) + 2 * len(near),),
        held_out=range(4),
    )(pos, line, *blocks, *near, *far, *args)


def self_back_body(
    n_blocks, n_parts, pos, line, flow_in, one_t, mixed_one, query, keys_t, values, exps_in, *refs
):
    near, far, refs = refs[0], refs[1], refs[2:]
    (own_out, query_t_out, kv_out, parts_out) = refs[:4]
    weight, exps, sem, held, part_sem = refs[4:]
    count, feat = query.shape
    for pair in range(HEADS // 2):
        fetch(exps_in, exps, sem, pair).start()
    copies = fetch_parts(near, far, held, part_sem)
    grad_t = one_t[...]
    attend_back(
        query,
        keys_t,
        values,
        mixed_one,
        grad_t,
        grad_t.T,
        exps_in,
        exps,
        sem,
        query_t_out,
        kv_out,
    )
    for copy in copies:
        copy.wait()
    in_order(pos, ([held.at[0]], [held.at[1]]), weight, 0)
    for d in range(n_blocks):
        part = dot_t(kv_out[d * count : (d + 1) * count, :], weight[:, feat:])
        place = pl.multiple_of((line[0] ^ d) * count, count)
        parts_out[pl.ds(place, count), :] = low(part)
    own_out[...] = flow_in[...] + dot_t(query_t_out[...].T, weight[:, :feat])


def self_back(pos, line, n_blocks, near, far, after, *args):
    count, feat = args[3].shape
    keys = count * n_blocks
    return kernel_call(
        functools.partial(self_back_body, n_blocks, len(near)),
        (
            shape(count, feat, dtype=F32),
            shape(feat, count),
            shape(keys, 2 * feat),
            shape(keys, feat),
        ),
        [WHOLE] * 4,
        [SCALARS] * 2 + [WHOLE] * 6 + [APART] * 3,
        [VM((feat, 3 * feat), BF)]
        + back_scratch(keys, feat, count)[2:]
        + [VM((2,) + near[0].shape, BF), pltpu.SemaphoreType.DMA((2,))],
        "self_back",
        12 * 10**9,
        20 * 10**6,
        after,
        held_in=(2, 3),
        held_out=(1, 2),
    )(pos, line, *args, *near, *far)


def self_grads_body(n_blocks, pos, *refs):
    blocks = refs[:n_blocks]
    query_t, kv, keep_out, away_out, grads = refs[n_blocks:]
    feat, count = query_t.shape
    turned = jnp.concatenate([block[:count, :].T for block in blocks], axis=1)
    grads[:, :feat] = low(dot_t(turned[:, :count], query_t[...]))
    grads[:, feat:] = low(dot(turned, kv[...]))
    by_distance(pos, grads, (keep_out, away_out), 0)


def self_grads(pos, blocks, query_t, kv, part_shape, after):
    feat = query_t.shape[0]
    return kernel_call(
        functools.partial(self_grads_body, len(blocks)),
        (shape(*part_shape), shape(*part_shape)),
        [WHOLE] * 2,
        [SCALARS] + [WHOLE] * (len(blocks) + 2),
        [VM((feat, 3 * feat), BF)],
        "self_grads",
        5 * 10**9,
        8 * 10**6,
        after,
        held_in=(1 + len(blocks), 2 + len(blocks)),
        held_out=(0, 1),
    )(pos, *blocks, query_t, kv)


def pack_body(sub, source, target, glance, ids, pad, encoder, *refs):
    refs, encoder_out = (*refs[:-2], refs[-1]), refs[-2]
    encoder_out[...] = encoder[...]
    weights, vectors, refs = refs[:8], refs[8:14], refs[14:]
    inner, outer, three, early, mixed, lines = refs
    rows, feat = weights[0].shape
    count = glance.shape[1]
    wide = inner.shape[1]
    three[:, :wide] = inner[...]
    for r in range(sub):
        three[:, wide + r * feat : wide + (r + 1) * feat] = outer[r * rows : (r + 1) * rows, :]
    for place, weight in enumerate(weights):
        early[:, place * feat : (place + 1) * feat] = weight[...]
    lines[...] = jnp.zeros_like(lines)
    for place, vector in enumerate(vectors):
        lines[place : place + 1, :rows] = vector[...].astype(F32)
    early[:, 8 * feat :] = low(lines[...].T)[:rows, :]
    taken = jnp.broadcast_to(glance[...].astype(F32), (128, count)).T[:, :1]
    mixed[:count, :] = jnp.where(taken > 0.5, target[0], source[0])
    key_ids = jnp.where(pad[...] == 1, ids[...], -1).astype(F32)
    key_ids = jnp.concatenate([key_ids, jnp.zeros((1, feat - count), F32)], axis=1)
    mixed[count:, :] = low(jnp.broadcast_to(key_ids, (16, feat)))


def join_body(n, *refs):
    for i in range(n):
        refs[n][i] = refs[i][...]


def join(parts, *after):
    return kernel_call(
        functools.partial(join_body, len(parts)),
        shape(len(parts), *parts[0].shape),
        WHOLE,
        [WHOLE] * len(parts),
        [],
        "join",
        10**9,
        2 * 10**6,
        after,
    )(*parts)


def stack_body(n, cuts, *refs):
    parts, outs = refs[:n], refs[n:]
    for out, (first, last) in zip(outs, cuts, strict=True):
        for i in range(n):
            out[i] = parts[i][:, first:last]


def stack(parts, cuts, *after):
    rows = parts[0].shape[0]
    return kernel_call(
        functools.partial(stack_body, len(parts), cuts),
        tuple(shape(len(parts), rows, last - first) for first, last in cuts),
        [WHOLE] * len(cuts),
        [WHOLE] * len(parts),
        [],
        "stack",
        2 * 10**10,
        2 * 10**6,
        after,
    )(*parts)


def hold_body(*refs):
    pass


def hold(block, *after, space=None):
    out = shape(*block.shape, dtype=block.dtype)
    if space is not None:
        block = pltpu.with_memory_space_constraint(block, space)
        out = space(block.shape, block.dtype)
    return pl.pallas_call(
        hold_body,
        out_shape=out,
        in_specs=[APART] * (1 + len(after)),
        out_specs=APART,
        input_output_aliases={0: 0},
        name="hold",
    )(block, *after)


def swap(block, axis_name, size, bits):
    return lax.ppermute(block, axis_name, [(i, i ^ bits) for i in range(size)])


def stages(size):
    bits = size.bit_length() - 1
    return [2] * (bits // 2) + [1] * (bits % 2)


def spread(block, axis_name, size, unit, width):
    return [block] + [swap(block, axis_name, size, unit * far) for far in range(1, 1 << width)]


def spread_line(block, axis_name, size, unit, width):
    if width < 2:
        return spread(block, axis_name, size, unit, width)
    far = swap(block, axis_name, size, 2 * unit)
    return [block, swap(block, axis_name, size, unit), far, swap(far, axis_name, size, unit)]


def over_line(block, seq, way):
    blocks = [block]
    unit = 1
    for width in stages(seq):
        got = [way(b, "seq", seq, unit, width) for b in blocks]
        blocks = [g[far] for far in range(1 << width) for g in got]
        unit <<= width
    return blocks


def add_far_body(cut, keep, away, x_send, y_send, x_rest, y_rest):
    for e in range(4):
        both = low(keep[e].astype(F32) + away[e].astype(F32))
        (x_send if e % 2 == 1 else x_rest)[e // 2] = both[:, :, :cut]
        (y_send if e >= 2 else y_rest)[e % 2] = both[:, :, cut:]


def add_one_body(keep, away, *outs):
    for e in range(4):
        outs[e][...] = low(keep[e].astype(F32) + away[e].astype(F32))


def add_line_body(own, first, second, third, *outs):
    for d in range(4):
        total = own[d].astype(F32) + first[d].astype(F32)
        outs[d][...] = low(total + second[d].astype(F32) + third[d].astype(F32))


def add_mid_body(x_rest, x_got, y_rest, y_got, y_send, x_send, x_own, y_own):
    x_own[...] = x_rest[0].astype(F32) + x_got[0].astype(F32)
    y_send[...] = low(x_rest[1].astype(F32) + x_got[1].astype(F32))
    y_own[...] = y_rest[0].astype(F32) + y_got[0].astype(F32)
    x_send[...] = low(y_rest[1].astype(F32) + y_got[1].astype(F32))


def add_near_body(cut, x_own, x_got, y_own, y_got, own, odd, even):
    for d in range(4):
        left = x_own[d] + x_got[d].astype(F32)
        right = y_own[d] + y_got[d].astype(F32)
        if d == 0:
            own[:, :cut] = left
            own[:, cut:] = right
        elif d == 2:
            even[:, :cut] = low(left)
            even[:, cut:] = low(right)
        else:
            odd[d // 2, :, :cut] = low(left)
            odd[d // 2, :, cut:] = low(right)


def add_call(body, outs, operands, after, name, far_in=(), far_out=()):
    return kernel_call(
        body,
        outs,
        [WHOLE] * len(outs),
        [WHOLE] * len(operands),
        [],
        name,
        10**9,
        4 * 10**6,
        after,
        far_in=far_in,
        far_out=far_out,
    )(*operands)


def far_step(keep, away, after, fsdp):
    cols = keep.shape[3]
    cut = cols // 256 * 128
    dims = keep.shape[1:3]
    outs = [shape(2, *dims, width) for width in (cut, cols - cut) * 2]
    x_send, y_send, x_rest, y_rest = add_call(
        functools.partial(add_far_body, cut), outs, (keep, away), after, "add_far"
    )
    return (x_send, swap(x_send, "fsdp", fsdp, 2), swap(y_send, "fsdp", fsdp, 4), x_rest, y_rest)


def mid_step(far, after, fsdp):
    _, x_got, y_got, x_rest, y_rest = far
    x_dims, y_dims = x_rest.shape[1:], y_rest.shape[1:]
    outs = [shape(*x_dims), shape(*y_dims), shape(*x_dims, dtype=F32), shape(*y_dims, dtype=F32)]
    y_send, x_send, x_own, y_own = add_call(
        add_mid_body, outs, (x_rest, x_got, y_rest, y_got), after, "add_mid", (), (2, 3)
    )
    return (y_send, swap(y_send, "fsdp", fsdp, 4), swap(x_send, "fsdp", fsdp, 2), x_own, y_own)


def near_step(mid, after):
    _, x_got, y_got, x_own, y_own = mid
    cut = x_own.shape[2]
    rows, cols = x_own.shape[1], cut + y_own.shape[2]
    outs = [shape(rows, cols, dtype=F32), shape(2, rows, cols), shape(rows, cols)]
    return add_call(
        functools.partial(add_near_body, cut), outs, (x_own, x_got, y_own, y_got), after, "add_near", (0, 2)
    )


def finish_line(near, seq, *after):
    own, odd, even = near
    got = swap(odd, "seq", seq, 1)
    if after:
        got = hold(got, *after, space=pltpu.VMEM)
    even = low(even.astype(F32) + got[1].astype(F32))
    return own.astype(F32) + got[0].astype(F32), swap(even, "seq", seq, 2)


def bit_of(axis_name, bit):
    return (lax.axis_index(axis_name) & bit) != 0


def double(block, axis_name, size, bit, place):
    other = swap(block, axis_name, size, bit)
    high = bit_of(axis_name, bit)
    return jnp.where(
        high, jnp.stack([other, block], axis=place), jnp.stack([block, other], axis=place)
    )


def bits_below(size):
    return [1 << k for k in range(size.bit_length() - 1)]


def gather_blocks(shard, fsdp, seq, turned):
    block = shard
    for bit in bits_below(seq):
        block = double(block, "seq", seq, bit, 1)
    upper = bits_below(fsdp)[1:]
    done = []
    for bit in upper[::-1] if turned else upper:
        place = 1 + sum(b > bit for b in done)
        block = double(block, "fsdp", fsdp, bit, place)
        done.append(bit)
    if fsdp > 1:
        block = double(block, "fsdp", fsdp, 1, 1 + len(upper))
    return block.reshape(shard.shape[0], fsdp * seq * shard.shape[1], shard.shape[2])


def halve(block, axis_name, size, bit, place):
    high = bit_of(axis_name, bit).astype(jnp.int32)
    away = lax.dynamic_index_in_dim(block, 1 - high, place, keepdims=False)
    kept = lax.dynamic_index_in_dim(block, high, place, keepdims=False)
    other = swap(away, axis_name, size, bit)
    return (kept.astype(jnp.float32) + other.astype(jnp.float32)).astype(jnp.bfloat16)


def scatter_blocks(whole, fsdp, seq, turned):
    w, depth, cols = whole.shape
    n_up = len(bits_below(fsdp)) - 1
    n_seq = len(bits_below(seq))
    rows = depth // (fsdp * seq)
    block = whole.reshape((w,) + (2,) * (n_up + 1 + n_seq) + (rows, cols))
    block = halve(block, "fsdp", fsdp, 1, 1 + n_up)
    upper = bits_below(fsdp)[1:]
    left = list(upper)
    for bit in upper[::-1] if turned else upper:
        place = 1 + sum(b > bit for b in left)
        block = halve(block, "fsdp", fsdp, bit, place)
        left.remove(bit)
    for bit in bits_below(seq)[::-1]:
        block = halve(block, "seq", seq, bit, 1)
    return block.astype(jnp.float32)


def whole_parts(shard, fsdp, seq):
    whole = gather_blocks(shard[None], fsdp, seq, False)[0]
    parts = whole.reshape(4, 2, 4, -1, whole.shape[1])
    return parts[:, 0], parts[:, 1]


def whole_sum(keep, away, fsdp, seq):
    whole = jnp.stack([keep, away], axis=1).reshape(-1, keep.shape[3])
    return scatter_blocks(whole[None], fsdp, seq, False)[0]


def regroup(three, rows, to, wide):
    feat = three.shape[0]
    sub = wide // feat
    outer = three[:, wide:].reshape(-1, rows, sub, feat).transpose(0, 2, 1, 3)
    outer = outer.reshape(-1, sub, to, feat).transpose(0, 2, 1, 3)
    return jnp.concatenate([three[:, :wide], outer.reshape(feat, sub * feat)], axis=1)


def make(fsdp, seq):
    def on_device(
        source_copy,
        target_embed,
        glance_mask,
        segment_ids,
        pad_mask,
        encoder_out,
        out_grad,
        self_query,
        self_key,
        self_value,
        self_output,
        norm1_gain,
        norm1_shift,
        cross_query,
        cross_key,
        cross_value,
        cross_output,
        norm2_gain,
        norm2_shift,
        inner_weight,
        outer_weight,
        norm3_gain,
        norm3_shift,
    ):
        row_count, loc_count, feat = source_copy.shape
        count = row_count * loc_count
        chunk = self_query.shape[0]
        sub = outer_weight.shape[0] // chunk
        pos = jnp.stack([lax.axis_index("fsdp"), lax.axis_index("seq")]).astype(jnp.int32)
        ids = segment_ids.reshape(1, count)
        pad = pad_mask.reshape(1, count)
        encoder = encoder_out.reshape(count, feat)
        vectors = (norm1_gain, norm1_shift, norm2_gain, norm2_shift, norm3_gain, norm3_shift)
        vectors = [vector.reshape(1, chunk) for vector in vectors]
        wide = sub * feat
        three, early, mixed, encoder = kernel_call(
            functools.partial(pack_body, sub),
            (shape(chunk, 2 * wide), shape(chunk, 8 * feat + 128), shape(count + 16, feat), shape(count, feat)),
            [WHOLE] * 4,
            [WHOLE] * 22,
            [VM((128, 128), F32)],
            "pack",
            10**9,
            2 * 10**6,
        )(
            source_copy,
            target_embed,
            glance_mask.reshape(1, count),
            ids,
            pad,
            encoder,
            self_query,
            self_key,
            self_value,
            self_output,
            cross_query,
            cross_key,
            cross_value,
            cross_output,
            *vectors,
            inner_weight,
            outer_weight,
        )
        all_three = lax.all_gather(three, ("fsdp", "seq"), axis=0, tiled=True)
        home = pos
        near_rows = seq == 4 and fsdp == 8 and chunk % 16 == 0
        if near_rows:
            early_blocks = over_line(early, seq, spread)
            mixed_far = swap(mixed, "seq", seq, 2)
            mixed_near = swap(mixed, "seq", seq, 1)
            line_one, line_two = stack(
                early_blocks, ((0, 3 * feat), (3 * feat, 8 * feat + 128)), mixed_near
            )
            plane_one = spread(line_one, "fsdp", fsdp, 2, 2)
            near_one = join(plane_one, mixed_far)
            far_one = swap(near_one, "fsdp", fsdp, 1)
            mixed_far = hold(mixed_far, near_one, space=pltpu.VMEM)
            mixed_blocks = [mixed, mixed_near, mixed_far, swap(mixed_far, "seq", seq, 1)]
            plane_two = spread(line_two, "fsdp", fsdp, 2, 2)
            encoder_late = hold(encoder, far_one)
            encoder_far = swap(encoder_late, "seq", seq, 2)
            encoder_near = swap(encoder_late, "seq", seq, 1)
        else:
            home = jnp.zeros_like(pos)
            near_one, far_one = whole_parts(early[:, : 3 * feat], fsdp, seq)
            near_two, far_two = whole_parts(early[:, 3 * feat :], fsdp, seq)
            all_three = regroup(all_three, chunk, near_one.shape[2], wide)
            mixed_blocks = over_line(mixed, seq, spread)
            encoder_blocks = over_line(encoder, seq, spread)

        q_one, v_one, kt_one, mixed_one, inverse_one, key_rows, exps_one = self_attend(
            home, mixed_blocks, ids, [near_one], [far_one], count, feat, ()
        )
        if near_rows:
            encoder_far = hold(encoder_far, mixed_one, space=pltpu.VMEM)
            got_two = [hold(part, encoder_far, space=pltpu.VMEM) for part in plane_two[1:]]
            encoder_near = hold(encoder_near, mixed_one, space=pltpu.VMEM)
            near_two = join([line_two, *got_two], encoder_near)
            far_two = swap(near_two, "fsdp", fsdp, 1)
            near_two, far_two = [near_two], [far_two]
            encoder_blocks = [encoder, encoder_near, encoder_far]
            encoder_blocks.append(swap(encoder_far, "seq", seq, 1))
        else:
            near_two, far_two = [near_two], [far_two]
        (
            vec,
            unit_one,
            inv_one,
            q_two,
            v_two,
            kt_two,
            mixed_two,
            inverse_two,
            unit_two,
            inv_two,
            exps_two,
            three_near,
        ) = cross_attend(
            home,
            encoder_blocks,
            ids,
            key_rows,
            mixed,
            mixed_one,
            all_three,
            near_two,
            far_two,
            (),
        )
        layer_out, flow_two, vec_grad, keep_three, away_three = feed(
            home,
            unit_two,
            inv_two,
            vec,
            out_grad.reshape(count, feat),
            pad,
            three_near,
            near_one.shape[:3] + (2 * wide,),
        )
        after_feed = ()
        if near_rows:
            away_three = swap(away_three, "fsdp", fsdp, 1)
            far_three = far_step(keep_three, away_three, (), fsdp)
            after_feed = (far_three[0],)
        flow_one, one_t, keep_two, away_two, encoder_parts = cross_back(
            home,
            pos[1:],
            encoder_blocks,
            near_two,
            far_two,
            after_feed,
            flow_two,
            mixed_two,
            inverse_two,
            q_two,
            kt_two,
            v_two,
            exps_two,
            unit_one,
            inv_one,
            vec,
            vec_grad,
            mixed_one,
            inverse_one,
        )
        if near_rows:
            mid_three = mid_step(far_three, (flow_one,), fsdp)
            away_two = swap(hold(away_two, mid_three[0], space=pltpu.VMEM), "fsdp", fsdp, 1)
        encoder_grad = lax.psum_scatter(
            encoder_parts, "seq", scatter_dimension=0, tiled=True
        ).astype(F32)
        after_back, after_grads = (), ()
        if near_rows:
            far_two = far_step(keep_two, away_two, (), fsdp)
            after_back = (far_two[0],)
        input_own, query_t, kv, input_parts = self_back(
            home,
            pos[1:],
            seq,
            [near_one],
            [far_one],
            after_back,
            flow_one,
            one_t,
            mixed_one,
            q_one,
            kt_one,
            v_one,
            exps_one,
        )
        if near_rows:
            near_three = near_step(mid_three, (query_t,))
            mid_two = mid_step(far_two, (query_t,), fsdp)
            after_grads = (near_three[0], mid_two[0])
        keep_one, away_one = self_grads(
            home, mixed_blocks, query_t, kv, near_one.shape, after_grads
        )
        if near_rows:
            away_one = swap(away_one, "fsdp", fsdp, 1)
            one_send = add_call(
                add_one_body,
                [shape(*keep_one.shape[1:])] * 4,
                (keep_one, away_one),
                (),
                "add_one",
            )
            got_two = [hold(got, one_send[0], space=pltpu.VMEM) for got in mid_two[1:3]]
            mid_two = (mid_two[0], *got_two, *mid_two[3:])
            near_two = near_step(mid_two, ())
            near_three = finish_line(near_three, seq, one_send[0])
            got_one = [swap(one_send[e], "fsdp", fsdp, 2 * e) for e in (1, 2, 3)]
            line_one = add_call(
                add_line_body,
                [shape(*keep_one.shape[2:])] * 4,
                (one_send[0], *got_one),
                (),
                "add_line",
            )
            got_line = [swap(line_one[d], "seq", seq, d) for d in (1, 2, 3)]
            grads_three = near_three[0] + hold(near_three[1], got_line[0]).astype(F32)
            near_two = finish_line(near_two, seq, line_one[0])
            grads_two = near_two[0] + near_two[1].astype(F32)
            grads_one = line_one[0].astype(F32)
            for block in got_line:
                grads_one = grads_one + block.astype(F32)
        else:
            grads_one = whole_sum(keep_one, away_one, fsdp, seq)
            grads_two = whole_sum(keep_two, away_two, fsdp, seq)
            grads_three = jnp.stack([keep_three, away_three], axis=1).reshape(feat, 2 * wide)
            grads_three = regroup(grads_three, near_one.shape[2], chunk, wide)
            grads_three = scatter_blocks(grads_three[None], fsdp, seq, False)[0]
        input_got = lax.psum_scatter(input_parts, "seq", scatter_dimension=0, tiled=True)
        input_grad = input_own + input_got.astype(F32)

        def stacked(flat_rows):
            return flat_rows.reshape(row_count, loc_count, feat)

        def cols(grads, place):
            return grads[:, place * feat : (place + 1) * feat]

        vec_out = grads_two[:, 5 * feat : 5 * feat + 6].T
        grad_outer = jnp.concatenate(
            [grads_three[:, wide + r * feat : wide + (r + 1) * feat] for r in range(sub)], axis=0
        )
        return (
            stacked(layer_out),
            stacked(input_grad),
            stacked(encoder_grad),
            cols(grads_one, 0),
            cols(grads_one, 1),
            cols(grads_one, 2),
            cols(grads_two, 0),
            vec_out[0],
            vec_out[1],
            cols(grads_two, 1),
            cols(grads_two, 2),
            cols(grads_two, 3),
            cols(grads_two, 4),
            vec_out[2],
            vec_out[3],
            grads_three[:, :wide],
            grad_outer,
            vec_out[4],
            vec_out[5],
        )

    return on_device


def solution(mesh):
    rows = P("fsdp", "seq", None)
    marks = P("fsdp", "seq")
    weight = P(("fsdp", "seq"), None)
    vector = P(("fsdp", "seq"))
    layer = (weight,) * 4 + (vector,) * 2
    return jax.shard_map(
        make(mesh.shape["fsdp"], mesh.shape["seq"]),
        mesh=mesh,
        in_specs=(rows, rows, marks, marks, marks, rows, rows)
        + layer
        + layer
        + (weight,) * 2
        + (vector,) * 2,
        out_specs=(rows,) * 3 + layer + layer + (weight,) * 2 + (vector,) * 2,
        check_vma=False,
    )
```

```python
import functools

import jax
import jax.numpy as jnp
from jax import lax
from jax.experimental import pallas as pl
from jax.experimental.pallas import tpu as pltpu
from jax.sharding import PartitionSpec as P

HEADS = 8
HEAD = 64
PAIR = 2 * HEAD
SLOT = HEAD + 16


norm_eps = 1e-05
mask_fill = -1e30

BF = jnp.bfloat16
F32 = jnp.float32
VM = pltpu.VMEM
WHOLE = pl.BlockSpec(memory_space=pltpu.VMEM)
SCALARS = pl.BlockSpec(memory_space=pltpu.SMEM)
APART = pl.BlockSpec(memory_space=pl.ANY)


def shape(*dims, dtype=BF):
    return jax.ShapeDtypeStruct(dims, dtype)


def low(values):
    return values.astype(BF)


def dot(left, right):
    return jnp.dot(left, right, preferred_element_type=F32)


def dot_t(left, right):
    return lax.dot_general(left, right, (((1,), (1,)), ((), ())), preferred_element_type=F32)


def head_cols(block, head):
    pair = block[:, head // 2 * PAIR : (head // 2 + 1) * PAIR]
    lane = lax.broadcasted_iota(jnp.int32, pair.shape, 1)
    return jnp.where((lane >= HEAD) == (head % 2 == 1), pair, jnp.zeros_like(pair))


def head_rows(block, head):
    mine = block[head * HEAD : (head + 1) * HEAD, :]
    rest = jnp.zeros_like(mine)
    return jnp.concatenate([mine, rest] if head % 2 == 0 else [rest, mine], axis=0)


def chunk_of(pos, seq, c, e, d):
    return (pos[0] ^ (2 * e + c)) * seq + (pos[1] ^ d)


def in_order(pos, parts, target, col, sub=1):
    width = target.shape[1]
    for c, sides in enumerate(parts):
        if len(sides) == 1:
            sides = [sides[0].at[e] for e in range(sides[0].shape[0])]
        for e, part in enumerate(sides):
            for d in range(part.shape[0]):
                rows = part.shape[1]
                first = chunk_of(pos, part.shape[0], c, e, d) * (rows * sub)
                for r in range(sub):
                    start = pl.multiple_of(first + r * rows, rows)
                    target[pl.ds(start, rows), :] = part[
                        d, :, col + r * width : col + (r + 1) * width
                    ]


def fetch_parts(near, far, held, sem):
    copies = [
        pltpu.make_async_copy(ref, held.at[side], sem.at[side])
        for side, ref in enumerate((near, far))
    ]
    for copy in copies:
        copy.start()
    return copies


def by_distance(pos, source, parts, col, sub=1):
    width = source.shape[1]
    for c, part in enumerate(parts):
        for e in range(part.shape[0]):
            for d in range(part.shape[1]):
                rows = part.shape[2]
                first = chunk_of(pos, part.shape[1], c, e, d) * (rows * sub)
                for r in range(sub):
                    start = pl.multiple_of(first + r * rows, rows)
                    part[e, d, :, col + r * width : col + (r + 1) * width] = source[
                        pl.ds(start, rows), :
                    ]


def normalise(flow):
    centre = jnp.mean(flow, axis=1, keepdims=True)
    centered = flow - centre
    spread = jnp.mean(centered * centered, axis=1, keepdims=True)
    inverse = lax.rsqrt(spread + norm_eps)
    return centered * inverse, inverse


def normalise_back(grad, unit, inverse, gain):
    scaled = grad * gain
    mean_one = jnp.mean(scaled, axis=1, keepdims=True)
    mean_two = jnp.mean(scaled * unit, axis=1, keepdims=True)
    grad_flow = inverse * (scaled - mean_one - unit * mean_two)
    return (
        grad_flow,
        jnp.sum(grad * unit, axis=0, keepdims=True),
        jnp.sum(grad, axis=0, keepdims=True),
    )


def set_bias(key_rows, query_row, bias):
    count = query_row.shape[1]
    for d in range(len(key_rows)):
        column = jnp.broadcast_to(key_rows[d], (128, count)).T
        column = jnp.concatenate([column] * (count // 128), axis=1)
        bias[d * count : (d + 1) * count, :] = jnp.where(column == query_row, 0.0, mask_fill)


def set_values(values, slots, first):
    turned = values.T
    count = values.shape[0]
    cols = slice(first, first + count)
    for head in range(HEADS):
        slots[head * SLOT : head * SLOT + HEAD, cols] = turned[head * HEAD : (head + 1) * HEAD, :]
        slots[head * SLOT + HEAD : (head + 1) * SLOT, cols] = jnp.ones((SLOT - HEAD, count), BF)


def finish_head(head, exp_scores, slots, mixed_out, inverse_out):
    summed = dot(slots[head * SLOT : (head + 1) * SLOT, :], exp_scores)
    inverse = 1.0 / summed[HEAD : HEAD + 1, :]
    mixed_out[head * HEAD : (head + 1) * HEAD, :] = low(summed[:HEAD, :] * inverse)
    inverse_out[head : head + 1, :] = inverse


def attend(query, keys, slots, bias, exps, exps_out, sem, mixed_out, inverse_out):
    count = query.shape[0]

    def scores_of(head):
        pair_keys = keys[:, head // 2 * PAIR : (head // 2 + 1) * PAIR]
        return dot_t(pair_keys, head_cols(query, head)) + bias[...]

    scores, before = scores_of(0), None
    for head in range(HEADS):
        after = scores_of(head + 1) if head + 1 < HEADS else None
        if head > 0:
            finish_head(head - 1, before, slots, mixed_out, inverse_out)
        top = jnp.max(scores, axis=0, keepdims=True)
        before = low(jnp.exp(scores - top))
        exps[head // 2, :, head % 2 * count : (head % 2 + 1) * count] = before
        if head % 2 == 1:
            pltpu.make_async_copy(
                exps.at[head // 2], exps_out.at[head // 2], sem.at[head // 2]
            ).start()
        scores = after
    finish_head(HEADS - 1, before, slots, mixed_out, inverse_out)
    for pair in range(HEADS // 2):
        pltpu.make_async_copy(exps.at[pair], exps_out.at[pair], sem.at[pair]).wait()


def fetch(exps_in, exps, sem, pair):
    return pltpu.make_async_copy(exps_in.at[pair], exps.at[pair], sem.at[pair])


def attend_back(
    query, keys_t, values, mixed_t, grad_t, grad, exps_in, exps, sem, query_t_out, kv_out
):
    count, feat = query.shape

    def head_dot(head):
        rows = slice(head * HEAD, (head + 1) * HEAD)
        both = grad_t[rows, :].astype(F32) * mixed_t[rows, :].astype(F32)
        return jnp.sum(both, axis=0, keepdims=True)

    def grad_probs(pair):
        heads = (2 * pair, 2 * pair + 1)
        both = jnp.concatenate([head_rows(grad_t, head) for head in heads], axis=1)
        return dot(values[:, pair * PAIR : (pair + 1) * PAIR], both)

    def pair_cols(block, pair):
        return jnp.concatenate([head_cols(block, 2 * pair), head_cols(block, 2 * pair + 1)], axis=0)

    row_dots = [head_dot(head) for head in range(HEADS)]
    grad_prob = grad_probs(0)
    for pair in range(HEADS // 2):
        after = grad_probs(pair + 1) if pair + 1 < HEADS // 2 else None
        fetch(exps_in, exps, sem, pair).wait()
        cols = slice(pair * PAIR, (pair + 1) * PAIR)
        exp_scores = exps[pair]
        row_dot = jnp.concatenate([row_dots[2 * pair], row_dots[2 * pair + 1]], axis=1)
        grad_scores = low(exp_scores.astype(F32) * (grad_prob - row_dot))
        kv_out[:, feat + pair * PAIR : feat + (pair + 1) * PAIR] = low(
            dot(exp_scores, pair_cols(grad, pair))
        )
        kv_out[:, cols] = low(dot(grad_scores, pair_cols(query, pair)))
        for head in (2 * pair, 2 * pair + 1):
            rows = slice(head * HEAD, (head + 1) * HEAD)
            mine = grad_scores[:, head % 2 * count : (head % 2 + 1) * count]
            query_t_out[rows, :] = low(dot(keys_t[rows, :], mine) * HEAD ** (-0.5))
        grad_prob = after


def over_sums(grad_t, inverse):
    return low(
        jnp.concatenate(
            [
                grad_t[head * HEAD : (head + 1) * HEAD, :] * inverse[head : head + 1, :]
                for head in range(HEADS)
            ],
            axis=0,
        )
    )


def send_out(pairs, sem):
    copies = [pltpu.make_async_copy(a, b, sem.at[i]) for i, (a, b) in enumerate(pairs)]
    for copy in copies:
        copy.start()
    return copies


def self_attend_body(n_blocks, n_parts, pos, *refs):
    blocks, refs = refs[:n_blocks], refs[n_blocks:]
    near, far, refs = refs[:n_parts], refs[n_parts : 2 * n_parts], refs[2 * n_parts :]
    (ids, q_out, v_out, kt_out, mixed_out, inverse_out, kid_out, exps_out) = refs[:8]
    weight, keys, slots, bias, exps, sem, values, keys_t, out_sem = refs[8:]
    count, feat = q_out.shape
    in_order(pos, (near, far), weight, 0)
    query = low(dot(blocks[0][:count, :], weight[:, :feat]))
    query = query * BF(HEAD ** (-0.5))
    q_out[...] = query
    for d, block in enumerate(blocks):
        rows = slice(d * count, (d + 1) * count)
        key = low(dot(block[:count, :], weight[:, feat : 2 * feat]))
        value = low(dot(block[:count, :], weight[:, 2 * feat :]))
        keys[rows, :] = key
        keys_t[:, rows] = key.T
        values[rows, :] = value
        set_values(value, slots, d * count)
        kid_out[d : d + 1, :] = block[count : count + 1, :count].astype(F32)
    copies = send_out(((keys_t, kt_out), (values, v_out)), out_sem)
    set_bias([kid_out[d : d + 1, :] for d in range(n_blocks)], ids[...].astype(F32), bias)
    attend(query, keys, slots, bias, exps, exps_out, sem, mixed_out, inverse_out)
    for copy in copies:
        copy.wait()


def attend_scratch(keys, feat, count):
    return [
        VM((keys, feat), BF),
        VM((HEADS * SLOT, keys), BF),
        VM((keys, count), F32),
        VM((HEADS // 2, keys, 2 * count), BF),
        pltpu.SemaphoreType.DMA((HEADS // 2,)),
        VM((keys, feat), BF),
        VM((feat, keys), BF),
        pltpu.SemaphoreType.DMA((3,)),
    ]


SMALL = ("stack", "join", "add_far", "add_mid", "add_near", "add_one", "add_line")
ROOM = {"self_attend": 22, "cross_attend": 24, "feed": 28, "cross_back": 28, "self_back": 22}


def kernel_call(
    body, outs, out_specs, in_specs, scratch, name, flops, size, after=(), held_in=(), held_out=(), far_in=(), far_out=()
):
    n_in = len(in_specs)
    small = name in SMALL

    def space(place, held, far):
        return pltpu.VMEM if small and place not in far or place in held else pltpu.HBM

    def run(*refs):
        body(*refs[:n_in], *refs[n_in + len(after) :])

    single = not isinstance(outs, (tuple, list))
    outs = tuple(
        space(place, held_out, far_out)(out.shape, out.dtype)
        for place, out in enumerate([outs] if single else outs)
    )
    outs = outs[0] if single else outs
    call = pl.pallas_call(
        run if after else body,
        out_shape=outs,
        in_specs=in_specs + [APART] * len(after),
        out_specs=out_specs,
        scratch_shapes=scratch,
        compiler_params=pltpu.CompilerParams(vmem_limit_bytes=(8 if small else ROOM.get(name, 12)) * 2**20),
        cost_estimate=pl.CostEstimate(flops=flops, bytes_accessed=size, transcendentals=0),
        name=name,
    )

    def go(*operands):
        operands = [
            x
            if spec is SCALARS
            else pltpu.with_memory_space_constraint(x, space(place, held_in, far_in))
            for place, (x, spec) in enumerate(zip(operands, in_specs, strict=True))
        ]
        return call(*operands, *after)

    return go


def self_attend(pos, blocks, ids, near, far, count, feat, after):
    keys = count * len(blocks)
    return kernel_call(
        functools.partial(self_attend_body, len(blocks), len(near)),
        (
            shape(count, feat),
            shape(keys, feat),
            shape(feat, keys),
            shape(feat, count),
            shape(HEADS, count, dtype=F32),
            shape(len(blocks), count, dtype=F32),
            shape(HEADS // 2, keys, 2 * count),
        ),
        [WHOLE] + [APART] * 2 + [WHOLE] * 3 + [APART],
        [SCALARS] + [WHOLE] * (len(blocks) + 2 * len(near) + 1),
        [VM((feat, 3 * feat), BF)] + attend_scratch(keys, feat, count),
        "self_attend",
        12 * 10**9,
        20 * 10**6,
        after,
    )(pos, *blocks, *near, *far, ids)


def cross_attend_body(n_blocks, n_parts, pos, *refs):
    blocks, refs = refs[:n_blocks], refs[n_blocks:]
    near, far, refs = refs[:n_parts], refs[n_parts : 2 * n_parts], refs[2 * n_parts :]
    (ids, kid, mixed, mixed_one, three) = refs[:5]
    (vec_out, unit_out, inv_out, q_out, v_out, kt_out, mixed_out, inverse_out) = refs[5:13]
    (unit_two_out, inv_two_out, exps_out, three_out) = refs[13:17]
    weight, keys, slots, bias, exps, sem, values, keys_t, out_sem = refs[17:]
    ahead = pltpu.make_async_copy(three, three_out, out_sem.at[2])
    ahead.start()
    count, feat = q_out.shape
    in_order(pos, (near, far), weight, 0)
    vec_out[...] = weight[:, 5 * feat :].astype(F32).T[:8, :]
    flow = mixed[:count, :].astype(F32) + dot(mixed_one[...].T, weight[:, :feat])
    unit, inverse = normalise(flow)
    unit_out[...] = unit
    inv_out[...] = jnp.broadcast_to(inverse, inv_out.shape)
    normed = unit * vec_out[0:1, :] + vec_out[1:2, :]
    query = low(dot(low(normed), weight[:, feat : 2 * feat])) * BF(HEAD ** (-0.5))
    q_out[...] = query
    for d, block in enumerate(blocks):
        rows = slice(d * count, (d + 1) * count)
        key = low(dot(block[...], weight[:, 2 * feat : 3 * feat]))
        value = low(dot(block[...], weight[:, 3 * feat : 4 * feat]))
        keys[rows, :] = key
        keys_t[:, rows] = key.T
        values[rows, :] = value
        set_values(value, slots, d * count)
    copies = send_out(((keys_t, kt_out), (values, v_out)), out_sem)
    set_bias([kid[d : d + 1, :] for d in range(n_blocks)], ids[...].astype(F32), bias)
    attend(query, keys, slots, bias, exps, exps_out, sem, mixed_out, inverse_out)
    flow = unit_out[...] * vec_out[0:1, :] + vec_out[1:2, :]
    flow = flow + dot(mixed_out[...].T, weight[:, 4 * feat : 5 * feat])
    unit, inverse = normalise(flow)
    unit_two_out[...] = unit
    inv_two_out[...] = jnp.broadcast_to(inverse, inv_two_out.shape)
    for copy in copies:
        copy.wait()
    ahead.wait()


def cross_attend(pos, blocks, ids, kid, mixed, mixed_one, three, near, far, after):
    count, feat = blocks[0].shape
    keys = count * len(blocks)
    return kernel_call(
        functools.partial(cross_attend_body, len(blocks), len(near)),
        (
            shape(8, feat, dtype=F32),
            shape(count, feat, dtype=F32),
            shape(count, 128, dtype=F32),
            shape(count, feat),
            shape(keys, feat),
            shape(feat, keys),
            shape(feat, count),
            shape(HEADS, count, dtype=F32),
            shape(count, feat, dtype=F32),
            shape(count, 128, dtype=F32),
            shape(HEADS // 2, keys, 2 * count),
            shape(*three.shape),
        ),
        [WHOLE] * 4 + [APART] * 2 + [WHOLE] * 4 + [APART, WHOLE],
        [SCALARS] + [WHOLE] * (len(blocks) + 2 * len(near) + 4) + [APART],
        [VM((feat, 5 * feat + 128), BF)] + attend_scratch(keys, feat, count),
        "cross_attend",
        14 * 10**9,
        20 * 10**6,
        after,
        held_out=(8, 9, 11),
    )(pos, *blocks, *near, *far, ids, kid, mixed, mixed_one, three)


def feed_body(pos, unit_in, inv_in, vec, grad_in, pad, three, *refs):
    (layer_out, flow_out, vec_grad_out, keep_out, away_out) = refs[:5]
    w_out, g_in, g_out = refs[5:]
    feat, wide = g_in.shape
    sub = wide // feat
    w_in = three.at[:, :wide]
    rows = keep_out.shape[2]
    for first in range(0, feat, rows):
        for r in range(sub):
            w_out[first * sub + r * rows : first * sub + (r + 1) * rows, :] = three[
                first : first + rows, wide + r * feat : wide + (r + 1) * feat
            ]
    real = jnp.broadcast_to(pad[...].astype(F32), (128, pad.shape[1])).T[:, :1]
    unit_two = unit_in[...]
    normed_two = unit_two * vec[2:3, :] + vec[3:4, :]
    normed_low = low(normed_two)
    inner = dot(normed_low, w_in[...])
    cube = 0.044715 * inner * inner
    bend = jnp.tanh((2.0 / jnp.pi) ** 0.5 * inner * (1.0 + cube))
    active = low(0.5 * inner * (1.0 + bend))
    slope = 0.5 * (1.0 + bend) + 0.5 * inner * (1.0 - bend * bend) * (2.0 / jnp.pi) ** 0.5 * (
        1.0 + 3.0 * cube
    )
    flow = normed_two + dot(active, w_out[...])
    unit, inverse = normalise(flow)
    layer_out[...] = low((unit * vec[4:5, :] + vec[5:6, :]) * real)
    top = grad_in[...].astype(F32) * real
    grad_flow, grad_gain, grad_shift = normalise_back(top, unit, inverse, vec[4:5, :])
    vec_grad_out[...] = jnp.zeros_like(vec_grad_out)
    vec_grad_out[4:5, :] = grad_gain
    vec_grad_out[5:6, :] = grad_shift
    grad_y = low(grad_flow)
    grad_inner = low(slope * dot_t(grad_y, w_out[...]))
    grad_normed = grad_flow + dot_t(grad_inner, w_in[...])
    grad_flow, grad_gain, grad_shift = normalise_back(
        grad_normed, unit_two, inv_in[:, :1], vec[2:3, :]
    )
    vec_grad_out[2:3, :] = grad_gain
    vec_grad_out[3:4, :] = grad_shift
    flow_out[...] = grad_flow
    g_out[...] = low(dot(active.T, grad_y))
    by_distance(pos, g_out, (keep_out, away_out), wide, sub)
    g_in[...] = low(dot(normed_low.T, grad_inner))
    by_distance(pos, g_in, (keep_out, away_out), 0)


def feed(pos, unit, inverse, vec, out_grad, pad, three, whole):
    count, feat = unit.shape
    wide = three.shape[1] // 2
    return kernel_call(
        feed_body,
        (
            shape(count, feat),
            shape(count, feat, dtype=F32),
            shape(8, feat, dtype=F32),
            shape(*whole),
            shape(*whole),
        ),
        [WHOLE] * 5,
        [SCALARS] + [WHOLE] * 6,
        [VM((wide, feat), BF), VM((feat, wide), BF), VM((wide, feat), BF)],
        "feed",
        6 * 10**9,
        20 * 10**6,
        held_in=(1, 2, 6),
        held_out=(1, 2, 3, 4),
    )(pos, unit, inverse, vec, out_grad, pad, three)


def cross_back_body(n_blocks, n_parts, pos, line, *refs):
    blocks, refs = refs[:n_blocks], refs[n_blocks:]
    near, far, refs = refs[:n_parts], refs[n_parts : 2 * n_parts], refs[2 * n_parts :]
    (flow_in, mixed_two, inverse_two, query, keys_t, values, exps_in) = refs[:7]
    (unit_in, inv_in, vec, vec_grad, mixed_one, inverse_one) = refs[7:13]
    refs = refs[13:]
    flow_out, one_t_out, keep_out, away_out, parts_out = refs[:5]
    weight, grads, kv, query_t, exps, sem, rows_held, unit_held, late_sem, one_held, turned_held = refs[5:]
    soon = pltpu.make_async_copy(keys_t, turned_held, late_sem.at[n_blocks + 2])
    soon.start()
    count, feat = query.shape
    for pair in range(HEADS // 2):
        fetch(exps_in, exps, sem, pair).start()
    late = [(block, rows_held.at[d]) for d, block in enumerate(blocks)] + [(unit_in, unit_held)]
    late.append((mixed_one, one_held))
    late = send_out(late, late_sem)
    in_order(pos, (near, far), weight, 0)
    grad_y = low(flow_in[...])
    grad_t = over_sums(dot_t(weight[:, 4 * feat : 5 * feat], grad_y), inverse_two)
    grads[:, 4 * feat : 5 * feat] = low(dot(mixed_two[...], grad_y))
    soon.wait()
    attend_back(
        query, turned_held, values, mixed_two, grad_t, grad_t.T, exps_in, exps, sem, query_t, kv
    )
    grad_query = query_t[...].T
    grad_normed = flow_in[...] + dot_t(grad_query, weight[:, feat : 2 * feat])
    for copy in late:
        copy.wait()
    unit = unit_held[...]
    grad_flow, grad_gain, grad_shift = normalise_back(grad_normed, unit, inv_in[:, :1], vec[0:1, :])
    flow_out[...] = grad_flow
    grad_y = low(grad_flow)
    one_t_out[...] = over_sums(dot_t(weight[:, :feat], grad_y), inverse_one)
    grads[:, :feat] = low(dot(one_held[...], grad_y))
    normed = low(unit * vec[0:1, :] + vec[1:2, :])
    grads[:, feat : 2 * feat] = low(dot(normed.T, grad_query))
    turned = jnp.concatenate([rows_held[d].T for d in range(n_blocks)], axis=1)
    grads[:, 2 * feat : 4 * feat] = low(dot(turned, kv[...]))
    rows = jnp.concatenate(
        [grad_gain, grad_shift, vec_grad[2:8, :], jnp.zeros((120, feat), F32)], axis=0
    )
    grads[:, 5 * feat :] = low(rows.T)
    by_distance(pos, grads, (keep_out, away_out), 0)
    for d in range(n_blocks):
        part = dot_t(kv[d * count : (d + 1) * count, :], weight[:, 2 * feat : 4 * feat])
        place = pl.multiple_of((line[0] ^ d) * count, count)
        parts_out[pl.ds(place, count), :] = low(part)


def back_scratch(keys, feat, count):
    return [
        VM((keys, 2 * feat), BF),
        VM((feat, count), BF),
        VM((HEADS // 2, keys, 2 * count), BF),
        pltpu.SemaphoreType.DMA((HEADS // 2,)),
    ]


def cross_back(pos, line, blocks, near, far, after, *args):
    count, feat = blocks[0].shape
    keys = count * len(blocks)
    whole = near[0].shape if len(near) == 1 else (len(near),) + near[0].shape
    return kernel_call(
        functools.partial(cross_back_body, len(blocks), len(near)),
        (
            shape(count, feat, dtype=F32),
            shape(feat, count),
            shape(*whole),
            shape(*whole),
        )
        + (shape(keys, feat),),
        [WHOLE] * 5,
        [SCALARS] * 2
        + [APART] * len(blocks)
        + [WHOLE] * (2 * len(near) + 4)
        + [APART, WHOLE]
        + [APART] * 2
        + [WHOLE] * 3
        + [APART, WHOLE],
        [VM((feat, 5 * feat + 128), BF)] * 2
        + back_scratch(keys, feat, count)
        + [
            VM((len(blocks), count, feat), BF),
            VM((count, feat), F32),
            pltpu.SemaphoreType.DMA((len(blocks) + 3,)),
            VM((feat, count), BF),
            VM((feat, keys), BF),
        ],
        "cross_back",
        15 * 10**9,
        20 * 10**6,
        after,
        held_in=(2 + len(blocks) + 2 * len(near),),
        held_out=range(4),
    )(pos, line, *blocks, *near, *far, *args)


def self_back_body(
    n_blocks, n_parts, pos, line, flow_in, one_t, mixed_one, query, keys_t, values, exps_in, *refs
):
    near, far, refs = refs[0], refs[1], refs[2:]
    (own_out, query_t_out, kv_out, parts_out) = refs[:4]
    weight, exps, sem, held, part_sem = refs[4:]
    count, feat = query.shape
    for pair in range(HEADS // 2):
        fetch(exps_in, exps, sem, pair).start()
    copies = fetch_parts(near, far, held, part_sem)
    grad_t = one_t[...]
    attend_back(
        query,
        keys_t,
        values,
        mixed_one,
        grad_t,
        grad_t.T,
        exps_in,
        exps,
        sem,
        query_t_out,
        kv_out,
    )
    for copy in copies:
        copy.wait()
    in_order(pos, ([held.at[0]], [held.at[1]]), weight, 0)
    for d in range(n_blocks):
        part = dot_t(kv_out[d * count : (d + 1) * count, :], weight[:, feat:])
        place = pl.multiple_of((line[0] ^ d) * count, count)
        parts_out[pl.ds(place, count), :] = low(part)
    own_out[...] = flow_in[...] + dot_t(query_t_out[...].T, weight[:, :feat])


def self_back(pos, line, n_blocks, near, far, after, *args):
    count, feat = args[3].shape
    keys = count * n_blocks
    return kernel_call(
        functools.partial(self_back_body, n_blocks, len(near)),
        (
            shape(count, feat, dtype=F32),
            shape(feat, count),
            shape(keys, 2 * feat),
            shape(keys, feat),
        ),
        [WHOLE] * 4,
        [SCALARS] * 2 + [WHOLE] * 6 + [APART] * 3,
        [VM((feat, 3 * feat), BF)]
        + back_scratch(keys, feat, count)[2:]
        + [VM((2,) + near[0].shape, BF), pltpu.SemaphoreType.DMA((2,))],
        "self_back",
        12 * 10**9,
        20 * 10**6,
        after,
        held_in=(2, 3),
        held_out=(1, 2),
    )(pos, line, *args, *near, *far)


def self_grads_body(n_blocks, pos, *refs):
    blocks = refs[:n_blocks]
    query_t, kv, keep_out, away_out, grads = refs[n_blocks:]
    feat, count = query_t.shape
    turned = jnp.concatenate([block[:count, :].T for block in blocks], axis=1)
    grads[:, :feat] = low(dot_t(turned[:, :count], query_t[...]))
    grads[:, feat:] = low(dot(turned, kv[...]))
    by_distance(pos, grads, (keep_out, away_out), 0)


def self_grads(pos, blocks, query_t, kv, part_shape, after):
    feat = query_t.shape[0]
    return kernel_call(
        functools.partial(self_grads_body, len(blocks)),
        (shape(*part_shape), shape(*part_shape)),
        [WHOLE] * 2,
        [SCALARS] + [WHOLE] * (len(blocks) + 2),
        [VM((feat, 3 * feat), BF)],
        "self_grads",
        5 * 10**9,
        8 * 10**6,
        after,
        held_in=(1 + len(blocks), 2 + len(blocks)),
        held_out=(0, 1),
    )(pos, *blocks, query_t, kv)


def pack_body(sub, source, target, glance, ids, pad, encoder, *refs):
    refs, encoder_out = (*refs[:-2], refs[-1]), refs[-2]
    encoder_out[...] = encoder[...]
    weights, vectors, refs = refs[:8], refs[8:14], refs[14:]
    inner, outer, three, early, mixed, lines = refs
    rows, feat = weights[0].shape
    count = glance.shape[1]
    wide = inner.shape[1]
    three[:, :wide] = inner[...]
    for r in range(sub):
        three[:, wide + r * feat : wide + (r + 1) * feat] = outer[r * rows : (r + 1) * rows, :]
    for place, weight in enumerate(weights):
        early[:, place * feat : (place + 1) * feat] = weight[...]
    lines[...] = jnp.zeros_like(lines)
    for place, vector in enumerate(vectors):
        lines[place : place + 1, :rows] = vector[...].astype(F32)
    early[:, 8 * feat :] = low(lines[...].T)[:rows, :]
    taken = jnp.broadcast_to(glance[...].astype(F32), (128, count)).T[:, :1]
    mixed[:count, :] = jnp.where(taken > 0.5, target[0], source[0])
    key_ids = jnp.where(pad[...] == 1, ids[...], -1).astype(F32)
    key_ids = jnp.concatenate([key_ids, jnp.zeros((1, feat - count), F32)], axis=1)
    mixed[count:, :] = low(jnp.broadcast_to(key_ids, (16, feat)))


def join_body(n, *refs):
    for i in range(n):
        refs[n][i] = refs[i][...]


def join(parts, *after):
    return kernel_call(
        functools.partial(join_body, len(parts)),
        shape(len(parts), *parts[0].shape),
        WHOLE,
        [WHOLE] * len(parts),
        [],
        "join",
        10**9,
        2 * 10**6,
        after,
    )(*parts)


def stack_body(n, cuts, *refs):
    parts, outs = refs[:n], refs[n:]
    for out, (first, last) in zip(outs, cuts, strict=True):
        for i in range(n):
            out[i] = parts[i][:, first:last]


def stack(parts, cuts, *after):
    rows = parts[0].shape[0]
    return kernel_call(
        functools.partial(stack_body, len(parts), cuts),
        tuple(shape(len(parts), rows, last - first) for first, last in cuts),
        [WHOLE] * len(cuts),
        [WHOLE] * len(parts),
        [],
        "stack",
        2 * 10**10,
        2 * 10**6,
        after,
    )(*parts)


def hold_body(*refs):
    pass


def hold(block, *after, space=None):
    out = shape(*block.shape, dtype=block.dtype)
    if space is not None:
        block = pltpu.with_memory_space_constraint(block, space)
        out = space(block.shape, block.dtype)
    return pl.pallas_call(
        hold_body,
        out_shape=out,
        in_specs=[APART] * (1 + len(after)),
        out_specs=APART,
        input_output_aliases={0: 0},
        name="hold",
    )(block, *after)


def swap(block, axis_name, size, bits):
    return lax.ppermute(block, axis_name, [(i, i ^ bits) for i in range(size)])


def stages(size):
    bits = size.bit_length() - 1
    return [2] * (bits // 2) + [1] * (bits % 2)


def spread(block, axis_name, size, unit, width):
    return [block] + [swap(block, axis_name, size, unit * far) for far in range(1, 1 << width)]


def spread_line(block, axis_name, size, unit, width):
    if width < 2:
        return spread(block, axis_name, size, unit, width)
    far = swap(block, axis_name, size, 2 * unit)
    return [block, swap(block, axis_name, size, unit), far, swap(far, axis_name, size, unit)]


def over_line(block, seq, way):
    blocks = [block]
    unit = 1
    for width in stages(seq):
        got = [way(b, "seq", seq, unit, width) for b in blocks]
        blocks = [g[far] for far in range(1 << width) for g in got]
        unit <<= width
    return blocks


def add_far_body(cut, keep, away, x_send, y_send, x_rest, y_rest):
    for e in range(4):
        both = low(keep[e].astype(F32) + away[e].astype(F32))
        (x_send if e % 2 == 1 else x_rest)[e // 2] = both[:, :, :cut]
        (y_send if e >= 2 else y_rest)[e % 2] = both[:, :, cut:]


def add_one_body(keep, away, *outs):
    for e in range(4):
        outs[e][...] = low(keep[e].astype(F32) + away[e].astype(F32))


def add_line_body(own, first, second, third, *outs):
    for d in range(4):
        total = own[d].astype(F32) + first[d].astype(F32)
        outs[d][...] = low(total + second[d].astype(F32) + third[d].astype(F32))


def add_mid_body(x_rest, x_got, y_rest, y_got, y_send, x_send, x_own, y_own):
    x_own[...] = x_rest[0].astype(F32) + x_got[0].astype(F32)
    y_send[...] = low(x_rest[1].astype(F32) + x_got[1].astype(F32))
    y_own[...] = y_rest[0].astype(F32) + y_got[0].astype(F32)
    x_send[...] = low(y_rest[1].astype(F32) + y_got[1].astype(F32))


def add_near_body(cut, x_own, x_got, y_own, y_got, own, odd, even):
    for d in range(4):
        left = x_own[d] + x_got[d].astype(F32)
        right = y_own[d] + y_got[d].astype(F32)
        if d == 0:
            own[:, :cut] = left
            own[:, cut:] = right
        elif d == 2:
            even[:, :cut] = low(left)
            even[:, cut:] = low(right)
        else:
            odd[d // 2, :, :cut] = low(left)
            odd[d // 2, :, cut:] = low(right)


def add_call(body, outs, operands, after, name, far_in=(), far_out=()):
    return kernel_call(
        body,
        outs,
        [WHOLE] * len(outs),
        [WHOLE] * len(operands),
        [],
        name,
        10**9,
        4 * 10**6,
        after,
        far_in=far_in,
        far_out=far_out,
    )(*operands)


def far_step(keep, away, after, fsdp):
    cols = keep.shape[3]
    cut = cols // 256 * 128
    dims = keep.shape[1:3]
    outs = [shape(2, *dims, width) for width in (cut, cols - cut) * 2]
    x_send, y_send, x_rest, y_rest = add_call(
        functools.partial(add_far_body, cut), outs, (keep, away), after, "add_far"
    )
    return (x_send, swap(x_send, "fsdp", fsdp, 2), swap(y_send, "fsdp", fsdp, 4), x_rest, y_rest)


def mid_step(far, after, fsdp):
    _, x_got, y_got, x_rest, y_rest = far
    x_dims, y_dims = x_rest.shape[1:], y_rest.shape[1:]
    outs = [shape(*x_dims), shape(*y_dims), shape(*x_dims, dtype=F32), shape(*y_dims, dtype=F32)]
    y_send, x_send, x_own, y_own = add_call(
        add_mid_body, outs, (x_rest, x_got, y_rest, y_got), after, "add_mid", (), (2, 3)
    )
    return (y_send, swap(y_send, "fsdp", fsdp, 4), swap(x_send, "fsdp", fsdp, 2), x_own, y_own)


def near_step(mid, after):
    _, x_got, y_got, x_own, y_own = mid
    cut = x_own.shape[2]
    rows, cols = x_own.shape[1], cut + y_own.shape[2]
    outs = [shape(rows, cols, dtype=F32), shape(2, rows, cols), shape(rows, cols)]
    return add_call(
        functools.partial(add_near_body, cut), outs, (x_own, x_got, y_own, y_got), after, "add_near", (0, 2)
    )


def finish_line(near, seq, *after):
    own, odd, even = near
    got = swap(odd, "seq", seq, 1)
    if after:
        got = hold(got, *after, space=pltpu.VMEM)
    even = low(even.astype(F32) + got[1].astype(F32))
    return own.astype(F32) + got[0].astype(F32), swap(even, "seq", seq, 2)


def bit_of(axis_name, bit):
    return (lax.axis_index(axis_name) & bit) != 0


def double(block, axis_name, size, bit, place):
    other = swap(block, axis_name, size, bit)
    high = bit_of(axis_name, bit)
    return jnp.where(
        high, jnp.stack([other, block], axis=place), jnp.stack([block, other], axis=place)
    )


def bits_below(size):
    return [1 << k for k in range(size.bit_length() - 1)]


def gather_blocks(shard, fsdp, seq, turned):
    block = shard
    for bit in bits_below(seq):
        block = double(block, "seq", seq, bit, 1)
    upper = bits_below(fsdp)[1:]
    done = []
    for bit in upper[::-1] if turned else upper:
        place = 1 + sum(b > bit for b in done)
        block = double(block, "fsdp", fsdp, bit, place)
        done.append(bit)
    if fsdp > 1:
        block = double(block, "fsdp", fsdp, 1, 1 + len(upper))
    return block.reshape(shard.shape[0], fsdp * seq * shard.shape[1], shard.shape[2])


def halve(block, axis_name, size, bit, place):
    high = bit_of(axis_name, bit).astype(jnp.int32)
    away = lax.dynamic_index_in_dim(block, 1 - high, place, keepdims=False)
    kept = lax.dynamic_index_in_dim(block, high, place, keepdims=False)
    other = swap(away, axis_name, size, bit)
    return (kept.astype(jnp.float32) + other.astype(jnp.float32)).astype(jnp.bfloat16)


def scatter_blocks(whole, fsdp, seq, turned):
    w, depth, cols = whole.shape
    n_up = len(bits_below(fsdp)) - 1
    n_seq = len(bits_below(seq))
    rows = depth // (fsdp * seq)
    block = whole.reshape((w,) + (2,) * (n_up + 1 + n_seq) + (rows, cols))
    block = halve(block, "fsdp", fsdp, 1, 1 + n_up)
    upper = bits_below(fsdp)[1:]
    left = list(upper)
    for bit in upper[::-1] if turned else upper:
        place = 1 + sum(b > bit for b in left)
        block = halve(block, "fsdp", fsdp, bit, place)
        left.remove(bit)
    for bit in bits_below(seq)[::-1]:
        block = halve(block, "seq", seq, bit, 1)
    return block.astype(jnp.float32)


def whole_parts(shard, fsdp, seq):
    whole = gather_blocks(shard[None], fsdp, seq, False)[0]
    parts = whole.reshape(4, 2, 4, -1, whole.shape[1])
    return parts[:, 0], parts[:, 1]


def whole_sum(keep, away, fsdp, seq):
    whole = jnp.stack([keep, away], axis=1).reshape(-1, keep.shape[3])
    return scatter_blocks(whole[None], fsdp, seq, False)[0]


def regroup(three, rows, to, wide):
    feat = three.shape[0]
    sub = wide // feat
    outer = three[:, wide:].reshape(-1, rows, sub, feat).transpose(0, 2, 1, 3)
    outer = outer.reshape(-1, sub, to, feat).transpose(0, 2, 1, 3)
    return jnp.concatenate([three[:, :wide], outer.reshape(feat, sub * feat)], axis=1)


def make(fsdp, seq):
    def on_device(
        source_copy,
        target_embed,
        glance_mask,
        segment_ids,
        pad_mask,
        encoder_out,
        out_grad,
        self_query,
        self_key,
        self_value,
        self_output,
        norm1_gain,
        norm1_shift,
        cross_query,
        cross_key,
        cross_value,
        cross_output,
        norm2_gain,
        norm2_shift,
        inner_weight,
        outer_weight,
        norm3_gain,
        norm3_shift,
    ):
        row_count, loc_count, feat = source_copy.shape
        count = row_count * loc_count
        chunk = self_query.shape[0]
        sub = outer_weight.shape[0] // chunk
        pos = jnp.stack([lax.axis_index("fsdp"), lax.axis_index("seq")]).astype(jnp.int32)
        ids = segment_ids.reshape(1, count)
        pad = pad_mask.reshape(1, count)
        encoder = encoder_out.reshape(count, feat)
        vectors = (norm1_gain, norm1_shift, norm2_gain, norm2_shift, norm3_gain, norm3_shift)
        vectors = [vector.reshape(1, chunk) for vector in vectors]
        wide = sub * feat
        three, early, mixed, encoder = kernel_call(
            functools.partial(pack_body, sub),
            (shape(chunk, 2 * wide), shape(chunk, 8 * feat + 128), shape(count + 16, feat), shape(count, feat)),
            [WHOLE] * 4,
            [WHOLE] * 22,
            [VM((128, 128), F32)],
            "pack",
            10**9,
            2 * 10**6,
        )(
            source_copy,
            target_embed,
            glance_mask.reshape(1, count),
            ids,
            pad,
            encoder,
            self_query,
            self_key,
            self_value,
            self_output,
            cross_query,
            cross_key,
            cross_value,
            cross_output,
            *vectors,
            inner_weight,
            outer_weight,
        )
        all_three = lax.all_gather(three, ("fsdp", "seq"), axis=0, tiled=True)
        home = pos
        near_rows = seq == 4 and fsdp == 8 and chunk % 16 == 0
        if near_rows:
            early_blocks = over_line(early, seq, spread)
            mixed_far = swap(mixed, "seq", seq, 2)
            mixed_near = swap(mixed, "seq", seq, 1)
            line_one, line_two = stack(
                early_blocks, ((0, 3 * feat), (3 * feat, 8 * feat + 128)), mixed_near
            )
            plane_one = spread(line_one, "fsdp", fsdp, 2, 2)
            near_one = join(plane_one, mixed_far)
            far_one = swap(near_one, "fsdp", fsdp, 1)
            mixed_far = hold(mixed_far, near_one, space=pltpu.VMEM)
            mixed_blocks = [mixed, mixed_near, mixed_far, swap(mixed_far, "seq", seq, 1)]
            plane_two = spread(line_two, "fsdp", fsdp, 2, 2)
            encoder_late = hold(encoder, far_one)
            encoder_far = swap(encoder_late, "seq", seq, 2)
            encoder_near = swap(encoder_late, "seq", seq, 1)
        else:
            home = jnp.zeros_like(pos)
            near_one, far_one = whole_parts(early[:, : 3 * feat], fsdp, seq)
            near_two, far_two = whole_parts(early[:, 3 * feat :], fsdp, seq)
            all_three = regroup(all_three, chunk, near_one.shape[2], wide)
            mixed_blocks = over_line(mixed, seq, spread)
            encoder_blocks = over_line(encoder, seq, spread)

        q_one, v_one, kt_one, mixed_one, inverse_one, key_rows, exps_one = self_attend(
            home, mixed_blocks, ids, [near_one], [far_one], count, feat, ()
        )
        if near_rows:
            encoder_far = hold(encoder_far, mixed_one, space=pltpu.VMEM)
            got_two = [hold(part, encoder_far, space=pltpu.VMEM) for part in plane_two[1:]]
            encoder_near = hold(encoder_near, mixed_one, space=pltpu.VMEM)
            near_two = join([line_two, *got_two], encoder_near)
            far_two = swap(near_two, "fsdp", fsdp, 1)
            near_two, far_two = [near_two], [far_two]
            encoder_blocks = [encoder, encoder_near, encoder_far]
            encoder_blocks.append(swap(encoder_far, "seq", seq, 1))
        else:
            near_two, far_two = [near_two], [far_two]
        (
            vec,
            unit_one,
            inv_one,
            q_two,
            v_two,
            kt_two,
            mixed_two,
            inverse_two,
            unit_two,
            inv_two,
            exps_two,
            three_near,
        ) = cross_attend(
            home,
            encoder_blocks,
            ids,
            key_rows,
            mixed,
            mixed_one,
            all_three,
            near_two,
            far_two,
            (),
        )
        layer_out, flow_two, vec_grad, keep_three, away_three = feed(
            home,
            unit_two,
            inv_two,
            vec,
            out_grad.reshape(count, feat),
            pad,
            three_near,
            near_one.shape[:3] + (2 * wide,),
        )
        after_feed = ()
        if near_rows:
            away_three = swap(away_three, "fsdp", fsdp, 1)
            far_three = far_step(keep_three, away_three, (), fsdp)
            after_feed = (far_three[0],)
        flow_one, one_t, keep_two, away_two, encoder_parts = cross_back(
            home,
            pos[1:],
            encoder_blocks,
            near_two,
            far_two,
            after_feed,
            flow_two,
            mixed_two,
            inverse_two,
            q_two,
            kt_two,
            v_two,
            exps_two,
            unit_one,
            inv_one,
            vec,
            vec_grad,
            mixed_one,
            inverse_one,
        )
        if near_rows:
            mid_three = mid_step(far_three, (flow_one,), fsdp)
            away_two = swap(hold(away_two, mid_three[0], space=pltpu.VMEM), "fsdp", fsdp, 1)
        encoder_grad = lax.psum_scatter(
            encoder_parts, "seq", scatter_dimension=0, tiled=True
        ).astype(F32)
        after_back, after_grads = (), ()
        if near_rows:
            far_two = far_step(keep_two, away_two, (), fsdp)
            after_back = (far_two[0],)
        input_own, query_t, kv, input_parts = self_back(
            home,
            pos[1:],
            seq,
            [near_one],
            [far_one],
            after_back,
            flow_one,
            one_t,
            mixed_one,
            q_one,
            kt_one,
            v_one,
            exps_one,
        )
        if near_rows:
            near_three = near_step(mid_three, (query_t,))
            mid_two = mid_step(far_two, (query_t,), fsdp)
            after_grads = (near_three[0], mid_two[0])
        keep_one, away_one = self_grads(
            home, mixed_blocks, query_t, kv, near_one.shape, after_grads
        )
        if near_rows:
            away_one = swap(away_one, "fsdp", fsdp, 1)
            one_send = add_call(
                add_one_body,
                [shape(*keep_one.shape[1:])] * 4,
                (keep_one, away_one),
                (),
                "add_one",
            )
            got_two = [hold(got, one_send[0], space=pltpu.VMEM) for got in mid_two[1:3]]
            mid_two = (mid_two[0], *got_two, *mid_two[3:])
            near_two = near_step(mid_two, ())
            near_three = finish_line(near_three, seq, one_send[0])
            got_one = [swap(one_send[e], "fsdp", fsdp, 2 * e) for e in (1, 2, 3)]
            line_one = add_call(
                add_line_body,
                [shape(*keep_one.shape[2:])] * 4,
                (one_send[0], *got_one),
                (),
                "add_line",
            )
            got_line = [swap(line_one[d], "seq", seq, d) for d in (1, 2, 3)]
            grads_three = near_three[0] + hold(near_three[1], got_line[0]).astype(F32)
            near_two = finish_line(near_two, seq, line_one[0])
            grads_two = near_two[0] + near_two[1].astype(F32)
            grads_one = line_one[0].astype(F32)
            for block in got_line:
                grads_one = grads_one + block.astype(F32)
        else:
            grads_one = whole_sum(keep_one, away_one, fsdp, seq)
            grads_two = whole_sum(keep_two, away_two, fsdp, seq)
            grads_three = jnp.stack([keep_three, away_three], axis=1).reshape(feat, 2 * wide)
            grads_three = regroup(grads_three, near_one.shape[2], chunk, wide)
            grads_three = scatter_blocks(grads_three[None], fsdp, seq, False)[0]
        input_got = lax.psum_scatter(input_parts, "seq", scatter_dimension=0, tiled=True)
        input_grad = input_own + input_got.astype(F32)

        def stacked(flat_rows):
            return flat_rows.reshape(row_count, loc_count, feat)

        def cols(grads, place):
            return grads[:, place * feat : (place + 1) * feat]

        vec_out = grads_two[:, 5 * feat : 5 * feat + 6].T
        grad_outer = jnp.concatenate(
            [grads_three[:, wide + r * feat : wide + (r + 1) * feat] for r in range(sub)], axis=0
        )
        return (
            stacked(layer_out),
            stacked(input_grad),
            stacked(encoder_grad),
            cols(grads_one, 0),
            cols(grads_one, 1),
            cols(grads_one, 2),
            cols(grads_two, 0),
            vec_out[0],
            vec_out[1],
            cols(grads_two, 1),
            cols(grads_two, 2),
            cols(grads_two, 3),
            cols(grads_two, 4),
            vec_out[2],
            vec_out[3],
            grads_three[:, :wide],
            grad_outer,
            vec_out[4],
            vec_out[5],
        )

    return on_device


def solution(mesh):
    rows = P("fsdp", "seq", None)
    marks = P("fsdp", "seq")
    weight = P(("fsdp", "seq"), None)
    vector = P(("fsdp", "seq"))
    layer = (weight,) * 4 + (vector,) * 2
    return jax.shard_map(
        make(mesh.shape["fsdp"], mesh.shape["seq"]),
        mesh=mesh,
        in_specs=(rows, rows, marks, marks, marks, rows, rows)
        + layer
        + layer
        + (weight,) * 2
        + (vector,) * 2,
        out_specs=(rows,) * 3 + layer + layer + (weight,) * 2 + (vector,) * 2,
        check_vma=False,
    )
```
